32 devices in a mesh: graph: 8 (over y, x, core), row: 4 (over z).
Axes of the slice: x: 2, y: 2, z: 4, core: 2. Of those that a mesh axis runs over, the one named last changes fastest.
Arguments:
- features: bfloat16 [24, 1024, 1024], P('graph', 'row'), may hold values from -6 to 6
- adjacency: int32 [24, 1024, 1024], P('graph', 'row'), may hold values 0 or 1
- counts: int32 [24], P('graph'), may hold values from 341 to 1024, as said below
- proj_weight: bfloat16 [1024, 1024], replicated, may hold values from -0.75 to 0.75
- skip_weight: bfloat16 [1024, 1024], replicated, may hold values from -0.1875 to 0.1875
- attn_dst: bfloat16 [4, 256], replicated, may hold values from -0.09375 to 0.09375
- attn_src: bfloat16 [4, 256], replicated, may hold values from -0.09375 to 0.09375
- attn_bias: float32 [1024], replicated, may hold values from -3 to 3
- norm_gain: float32 [1024], replicated, may hold values from 0.1 to 1.9
- norm_shift: float32 [1024], replicated, may hold values from -3 to 3
- cotangent: bfloat16 [24, 1024, 1024], P('graph', 'row'), may hold values from -6 to 6
Outputs:
- output: bfloat16 [24, 1024, 1024], P('graph', 'row')
- input_grad: bfloat16 [24, 1024, 1024], P('graph', 'row')
- proj_grad: float32 [1024, 1024], replicated
- skip_grad: float32 [1024, 1024], replicated
- attn_dst_grad: float32 [4, 256], replicated
- attn_src_grad: float32 [4, 256], replicated
- bias_grad: float32 [1024], replicated
- gain_grad: float32 [1024], replicated
- shift_grad: float32 [1024], replicated
The draws below stay inside these ranges and needn't reach their ends.
Inputs may be any that keep to these rules, and one draw needn't show every extreme that they name: Real nodes come first in each graph; the counts rise over the graphs with some jitter, and among graphs 3k to 3k+2, for each k, at least one has all 1024 nodes real.
All inputs are finite; a program needn't handle non-finite values. No bound on the sum of `adjacency` on one device may be relied on, other than what follows from the above.
Results may differ from the reference program's by a relative error of at most 0.0087.
Values may be sent and summed in bfloat16 or wider, within the bound.
A program may use at most 192 MiB of HBM per device.

```python
import jax
import jax.numpy as jnp
from jax import lax

F_IN = 1024
HEADS = 4
HEAD = 256
G_DEV = 3
WIDTH = 1024
NODES = 1024
GRAPHS = 24


def draw_counts(key, part):
    key = jax.random.fold_in(key, 7)
    key_jitter, key_slot = jax.random.split(key)
    graph_ids = jnp.arange(GRAPHS)
    least = NODES // 3
    base_count = least + graph_ids * (NODES - least) // GRAPHS
    jitter = jax.random.randint(key_jitter, (GRAPHS,), 0, NODES // 8 + 1)
    drawn_counts = jnp.minimum(base_count + jitter, NODES)
    full_slot = jax.random.randint(key_slot, (GRAPHS // G_DEV,), 0, G_DEV)
    is_full = graph_ids % G_DEV == jnp.repeat(full_slot, G_DEV)
    return jnp.where(is_full, NODES, drawn_counts).astype(jnp.int32)


def plant(drawn, key, smallest, top_value):
    spot = [jax.random.randint(jax.random.fold_in(key, axis), (), 0, length) for axis, length in enumerate(drawn.shape)]
    longest = drawn.shape.index(max(drawn.shape))
    beside = spot[:longest] + [(spot[longest] + 1) % drawn.shape[longest]] + spot[longest + 1:]
    return drawn.at[tuple(spot)].set(smallest).at[tuple(beside)].set(top_value)


def steps_of(stream_key, dims, cuts, low, top_value):
    level, own = 1.0, jax.random.fold_in(stream_key, 6)
    for axis_at, shards_of in cuts:
        draws = jnp.exp(jax.random.uniform(jax.random.fold_in(own, axis_at), (shards_of,), jnp.float32, low / len(cuts), top_value / len(cuts)))
        level = level * jnp.repeat(draws, dims[axis_at] // shards_of).reshape([-1 if axis == axis_at else 1 for axis in range(len(dims))])
    return level


def normal_values(key, extent, spread, limit, pieces=(), held_as=jnp.bfloat16):
    drawn = jax.random.normal(key, extent, jnp.float32) * spread
    if len(pieces) > 0:
        drawn = steps_of(key, extent, pieces, -0.22, 0.18) * drawn
    return jnp.clip(drawn, min=-limit, max=limit).astype(held_as)


def setup_inputs(seed: int = 0) -> dict:
    splits = jax.random.split(jax.random.key(seed), 12)
    return {
        "features": normal_values(splits[0], (GRAPHS, NODES, F_IN), 1.0, 6.0, ((0, 8), (1, 4))),
        "adjacency": plant((jax.random.randint(splits[1], (GRAPHS, NODES, NODES), 0, 32) < 1).astype(jnp.int32), jax.random.fold_in(splits[1], 1), 0, 1),
        "counts": draw_counts(jax.random.fold_in(splits[11], 71), 0),
        "proj_weight": normal_values(splits[3], (F_IN, WIDTH), (F_IN // 16) ** -0.5, 0.75),
        "skip_weight": normal_values(splits[4], (F_IN, WIDTH), F_IN ** -0.5, 0.1875),
        "attn_dst": normal_values(splits[5], (HEADS, HEAD), (16 * HEAD) ** -0.5, 0.09375),
        "attn_src": normal_values(splits[6], (HEADS, HEAD), (16 * HEAD) ** -0.5, 0.09375),
        "attn_bias": normal_values(splits[7], (WIDTH,), 0.5, 3.0, (), jnp.float32),
        "norm_gain": jnp.clip(1.0 + 0.18 * jax.random.normal(splits[8], (WIDTH,), jnp.float32), 0.1, 1.9),
        "norm_shift": normal_values(splits[9], (WIDTH,), 0.5, 3.0, (), jnp.float32),
        "cotangent": normal_values(splits[10], (GRAPHS, NODES, WIDTH), 1.0, 6.0, ((0, 8), (1, 4))),
    }


@jax.custom_vjp
def low(v):
    return lax.optimization_barrier(v.astype(jnp.bfloat16)).astype(jnp.float32)

@jax.custom_vjp
def low_back(v):
    return v

def low_keep(v):
    return (low(v), None)

def low_pass(kept, grad):
    return (grad,)

def back_keep(v):
    return (v, None)

def back_low(kept, grad):
    return (low(grad),)
low.defvjp(low_keep, low_pass)
low_back.defvjp(back_keep, back_low)
EPSILON = 1e-05

def smooth_leaky(value):
    return 0.2 * value + 0.8 * jax.nn.softplus(value)

def graph_attention(inputs):
    hidden, dst_score, src_score, adjacent, live_node = inputs
    node_total = hidden.shape[0]
    node_ids = jnp.arange(node_total)
    allowed = ((adjacent > 0) | (node_ids[:, None] == node_ids[None, :])) & (live_node[:, None] > 0) & (live_node[None, :] > 0)
    logit = smooth_leaky(dst_score.T[:, :, None] + src_score.T[:, None, :])
    peak_logit = lax.optimization_barrier(jnp.max(jnp.where(allowed[None], logit, -1e+30), axis=2))
    peak_logit = jnp.where(live_node[None, :] > 0, peak_logit, 0.0)
    weight = jnp.where(allowed[None], jnp.exp(logit - peak_logit[:, :, None]), 0.0)
    totals = lax.optimization_barrier(jnp.sum(weight, axis=2)) + (1.0 - live_node)[None, :]
    shares = low(weight / totals[:, :, None])
    head_split = hidden.reshape(node_total, HEADS, HEAD)
    mixture = jnp.einsum('hij,jhc->ihc', shares, head_split, precision=lax.Precision.HIGHEST)
    return mixture.reshape(node_total, HEADS * HEAD)

def forward(feats, proj, skip_w, attn_d, attn_s, bias, gain, shift, adjacency, live):
    hidden = low(low_back(jnp.einsum('gnf,fd->gnd', feats, proj, precision=lax.Precision.HIGHEST)))
    head_split = hidden.reshape(GRAPHS, NODES, HEADS, HEAD)
    dst_score = jnp.einsum('gnhc,hc->gnh', head_split, attn_d, precision=lax.Precision.HIGHEST)
    src_score = jnp.einsum('gnhc,hc->gnh', head_split, attn_s, precision=lax.Precision.HIGHEST)
    mixture = lax.map(jax.checkpoint(graph_attention), (hidden, dst_score, src_score, adjacency, live))
    mixture = low_back(mixture)
    skip_out = low_back(jnp.einsum('gnf,fd->gnd', feats, skip_w, precision=lax.Precision.HIGHEST))
    pre_act = mixture + bias + skip_out
    activation = jax.nn.elu(pre_act)
    live_col = live[:, :, None]
    real_count = jnp.sum(live)
    mean_act = lax.optimization_barrier(jnp.sum(activation * live_col, axis=(0, 1))) / real_count
    variance = lax.optimization_barrier(jnp.sum((activation - mean_act) ** 2 * live_col, axis=(0, 1))) / real_count
    normed = (activation - mean_act) * lax.rsqrt(variance + EPSILON)
    return (gain * normed + shift) * live_col

def reference(features, adjacency, counts, proj_weight, skip_weight, attn_dst, attn_src, attn_bias, norm_gain, norm_shift, cotangent):
    live = (jnp.arange(NODES)[None, :] < counts[:, None]).astype(jnp.float32)

    def apply(feats, proj, skip_w, attn_d, attn_s, bias, gain, shift):
        return forward(feats, proj, skip_w, attn_d, attn_s, bias, gain, shift, adjacency, live)
    output, pullback = jax.vjp(apply, features.astype(jnp.float32), proj_weight.astype(jnp.float32), skip_weight.astype(jnp.float32), attn_dst.astype(jnp.float32), attn_src.astype(jnp.float32), attn_bias, norm_gain, norm_shift)
    grads = pullback(cotangent.astype(jnp.float32))
    return (output.astype(jnp.bfloat16), grads[0].astype(jnp.bfloat16), grads[1], grads[2], grads[3], grads[4], grads[5], grads[6], grads[7])
```

```python
import functools

import jax
import jax.numpy as jnp
from jax import lax
from jax.experimental import pallas as pl
from jax.experimental.pallas import tpu as pltpu
from jax.sharding import PartitionSpec as P

EPSILON = 1e-05
MESH = pl.DeviceIdType.MESH
LOG2E = 1.4426950408889634
LN2 = 0.6931471805599453
MASKED = -1e30
TILE = 16
F32 = jnp.float32
BF16 = jnp.bfloat16
ANY = pl.BlockSpec(memory_space=pl.ANY)
VMEM = pl.BlockSpec(memory_space=pltpu.VMEM)
SMEM = pl.BlockSpec(memory_space=pltpu.SMEM)


def dot(left, right, dims=(1, 0)):
    contract = (((dims[0],), (dims[1],)), ((), ()))
    return lax.dot_general(left, right, contract, preferred_element_type=F32)


class Place:
    def __init__(self, planes, slots, group):
        self.planes, self.slots, self.group = planes, slots, group
        self.g = lax.axis_index("graph")
        self.z = lax.axis_index("row")
        self.core = lax.rem(self.g, 2)
        turn = jnp.where(self.core == 1, self.z, planes - 1 - self.z)
        self.mine = [turn == self.turn(s) for s in range(slots)]
        self.slot = sum(jnp.where(own, s, 0) for s, own in enumerate(self.mine))
        self.works = functools.reduce(jnp.logical_or, self.mine)

    def turn(self, slot):
        return slot * self.planes // (self.slots + 1)

    def owner(self, slot):
        turn = self.turn(slot)
        return jnp.where(self.core == 1, turn, self.planes - 1 - turn)


def elu_pair(value):
    grown = jnp.exp(jnp.minimum(value, 0.0))
    return jnp.where(value > 0, value, grown - 1.0), grown


def sub_rows(index, size):
    return pl.ds(pl.multiple_of(index * size, size), size)


def forward_kernel(
    dims,
    feat,
    adj,
    cot,
    counts,
    wp_in,
    ws_in,
    att_rows,
    att_cols,
    bias,
    gain,
    shift,
    feat_out,
    hid_out,
    grad_out,
    norm_out,
    p_out,
    q_out,
    cols_out,
    parts_out,
    sums_out,
    cot_all,
    feat_all,
    hid,
    mask_all,
    mask_own,
    adj_in,
    wp,
    ws,
    pre,
    mix,
    diff,
    low,
    dcol,
    srow,
    p_slot,
    q_slot,
    centered,
    stat,
    stats_a,
    stats_b,
    f_send,
    f_recv,
    a_send,
    a_recv,
    c_send,
    c_recv,
    sa_send,
    sa_recv,
    sb_send,
    sb_recv,
    own_sem,
    adj_sem,
    w_sem,
    p_sem,
    out_sem,
    cot_sem,
):
    planes, group, slots, rows, nodes, heads, head = dims
    width = heads * head
    at = Place(planes, slots, group)
    g, z = at.g, at.z
    block = sub_rows(z, rows)

    barrier = pltpu.get_barrier_semaphore()
    for k in range(1, planes):
        pl.semaphore_signal(barrier, 1, device_id=(g, lax.rem(z + k, planes)), device_id_type=MESH)
    for k in range(1, group):
        pl.semaphore_signal(barrier, 1, device_id=(lax.rem(g + k, group), z), device_id_type=MESH)
    load_wp = pltpu.make_async_copy(wp_in, wp, w_sem.at[0])
    load_ws = pltpu.make_async_copy(ws_in, ws, w_sem.at[1])
    load_wp.start()
    load_ws.start()
    half = rows // 2
    loads = [
        pltpu.make_async_copy(
            adj.at[i // 2, pl.ds(i % 2 * half, half)], adj_in.at[i % 2], adj_sem.at[i % 2]
        )
        for i in range(2 * slots)
    ]
    loads[0].start()
    loads[1].start()
    pl.semaphore_wait(barrier, planes - 1 + group - 1)

    def moves(source, target, send, recv, own):
        out = []
        for s in range(slots):
            to = at.owner(s)
            remote = pltpu.make_async_remote_copy(
                src_ref=source.at[s],
                dst_ref=target.at[block],
                send_sem=send.at[s],
                recv_sem=recv.at[z],
                device_id=(g, to),
                device_id_type=MESH,
            )
            local = pltpu.make_async_copy(source.at[s], target.at[block], own)
            out.append((to, remote, local))
        return out

    def start(copies):
        for to, remote, local in copies:
            pl.when(to != z)(remote.start)
            pl.when(to == z)(local.start)

    def sent(copies):
        for to, remote, local in copies:
            pl.when(to != z)(remote.wait_send)

    def arrived(k, source, target, send, recv, own):
        src = lax.rem(z + k, planes)
        there = target.at[sub_rows(src, rows)]

        @pl.when(k == 0)
        def _():
            pltpu.make_async_copy(source.at[0], there, own).wait()

        @pl.when(k != 0)
        def _():
            pltpu.make_async_remote_copy(
                src_ref=source.at[0],
                dst_ref=there,
                send_sem=send.at[0],
                recv_sem=recv.at[src],
                device_id=(g, src),
                device_id_type=MESH,
            ).wait_recv()

        return src

    f_args = (feat, feat_all, f_send, f_recv, own_sem.at[0])
    a_args = (mask_own, mask_all, a_send, a_recv, own_sem.at[1])
    c_args = (cot, cot_all, c_send, c_recv, own_sem.at[2])
    f_moves, a_moves, c_moves = moves(*f_args), moves(*a_args), moves(*c_args)
    start(f_moves)

    for i, load in enumerate(loads):
        load.wait()
        live_count = counts[i // 2]

        @pl.loop(0, half // TILE)
        def _(t):
            first = i % 2 * half + t * TILE
            shape = (TILE, nodes)
            row = lax.broadcasted_iota(jnp.int32, shape, 0) + (z * rows + first)
            col = lax.broadcasted_iota(jnp.int32, shape, 1)
            allowed = (adj_in[i % 2, sub_rows(t, TILE), :] > 0) | (row == col)
            allowed = allowed & (row < live_count) & (col < live_count)
            mask_own[i // 2, pl.ds(pl.multiple_of(first, TILE), TILE), :] = jnp.where(
                allowed, 0.0, MASKED
            ).astype(BF16)

        if i + 2 < len(loads):
            loads[i + 2].start()

    load_wp.wait()
    load_ws.wait()
    sent(f_moves)
    start(a_moves)
    start(c_moves)

    @pl.when(at.works)
    def _():
        live_count = counts[at.slot]

        @pl.loop(0, planes)
        def _(k):
            src = arrived(k, *f_args)
            here = sub_rows(src, rows)
            value = feat_all[here, :]
            for h in range(heads):
                part = slice(h * head, (h + 1) * head)
                hid[here, part] = dot(value, wp[:, part]).astype(BF16)
                pre[here, part] = dot(value, ws[:, part])
            made = hid[here, :]
            dcol[here, :] = dot(made, att_cols[...]) * LOG2E
            srow[:, here] = dot(att_rows[...], made, (1, 1)) * LOG2E

        pltpu.make_async_copy(feat_all, feat_out, out_sem.at[0]).start()
        pltpu.make_async_copy(hid, hid_out, out_sem.at[1]).start()

        @pl.loop(0, planes)
        def _(k):
            src = arrived(k, *a_args)
            here = sub_rows(src, rows)
            for h in range(heads):
                part = slice(h * head, (h + 1) * head)
                slot = h % 2

                def stores(of):
                    return [
                        pltpu.make_async_copy(kept.at[slot], out.at[h, here], p_sem.at[i, slot])
                        for i, (kept, out) in enumerate(((p_slot, p_out), (q_slot, q_out)))
                    ]

                @pl.when((k > 0) | (h >= 2))
                def _():
                    for store in stores(h):
                        store.wait()

                @pl.loop(0, rows // TILE)
                def _(t):
                    first = src * rows + t * TILE
                    there = pl.ds(pl.multiple_of(first, TILE), TILE)
                    inside = sub_rows(t, TILE)
                    masked = mask_all[there, :].astype(F32) + srow[h : h + 1, :]
                    dst = dcol[there, heads + h : heads + h + 1]
                    node = lax.broadcasted_iota(jnp.int32, (TILE, 1), 0) + first
                    live = (node < live_count).astype(F32)

                    def leaky(raw):
                        small = jnp.exp2(-jnp.abs(raw))
                        soft = jnp.log(1.0 + small)
                        return soft + jnp.maximum(raw * (1.25 * LN2), raw * (0.25 * LN2)), soft

                    peak, _ = leaky(jnp.max(masked, axis=1, keepdims=True) + dst)
                    raw = masked + dst
                    logit, soft = leaky(raw)
                    weight = jnp.exp2((logit - peak) * (0.8 * LOG2E))
                    total = jnp.sum(weight, axis=1, keepdims=True)
                    share = weight * (live / total)
                    slope = jnp.exp2(jnp.minimum(raw, 0.0) - soft * LOG2E) * 0.8 + 0.2
                    sloped = share * slope
                    p_slot[slot, inside, :] = share.astype(BF16)
                    q_slot[slot, inside, :] = sloped.astype(BF16)
                    middle = jnp.sum(sloped, axis=1, keepdims=True)
                    centered[inside, :] = (sloped - middle * share).astype(BF16)

                for store in stores(h):
                    store.start()
                mixed = dot(p_slot[slot], hid[:, part])
                mix[here, part] = mixed
                pre[here, part] += mixed + bias[:, part]
                diff[here, part] = dot(centered[...], hid[:, part]).astype(BF16)

    zero = jnp.zeros((8, width), F32)

    @pl.when(at.works)
    def _():
        live_count = counts[at.slot]

        def live_of(t):
            node = lax.broadcasted_iota(jnp.int32, (TILE, 1), 0) + t * TILE
            return (node < live_count).astype(F32)

        def fold(value):
            return sum(value[8 * i : 8 * i + 8] for i in range(TILE // 8))

        def add_act(t, total):
            act, _ = elu_pair(pre[sub_rows(t, TILE), :])
            return total + fold(act * live_of(t))

        total = lax.fori_loop(0, nodes // TILE, add_act, zero)
        number = jnp.maximum(live_count, 1).astype(F32)
        mean = jnp.sum(total, axis=0, keepdims=True) / number

        def add_square(t, total):
            act, _ = elu_pair(pre[sub_rows(t, TILE), :])
            off = act - mean
            return total + fold(off * off * live_of(t))

        square = lax.fori_loop(0, nodes // TILE, add_square, zero)

        for k in range(planes):
            src = arrived(jnp.int32(k), *c_args)
        pltpu.make_async_copy(feat_all, feat_out, out_sem.at[0]).wait()
        load = pltpu.make_async_copy(cot_all, feat_all, cot_sem)
        load.start()
        load.wait()

        def add_grad(t, totals):
            here = sub_rows(t, TILE)
            act, _ = elu_pair(pre[here, :])
            grad = feat_all[here, :].astype(F32) * live_of(t)
            return totals[0] + fold(grad), totals[1] + fold(grad * (act - mean))

        plain, along = lax.fori_loop(0, nodes // TILE, add_grad, (zero, zero))
        stat[0:1, :] = jnp.full((1, width), live_count.astype(F32))
        stat[1:2, :] = mean
        stat[2:3, :] = jnp.sum(square, axis=0, keepdims=True)
        stat[3:4, :] = jnp.sum(plain, axis=0, keepdims=True)
        stat[4:5, :] = jnp.sum(along, axis=0, keepdims=True)
        stat[5:8, :] = jnp.zeros((3, width), F32)

    @pl.when(jnp.logical_not(at.works))
    def _():
        stat[...] = zero

    def combine(count, one):
        number = sum(one(i, 0) for i in range(count))
        safe = jnp.maximum(number, 1.0)
        mean = sum(one(i, 0) * one(i, 1) for i in range(count)) / safe
        square = sum(
            one(i, 2) + one(i, 0) * (one(i, 1) - mean) * (one(i, 1) - mean) for i in range(count)
        )
        plain = sum(one(i, 3) for i in range(count))
        along = sum(one(i, 4) + one(i, 3) * (one(i, 1) - mean) for i in range(count))
        return number, mean, square, plain, along

    def exchange(size, me, slots_ref, send, recv, device):
        copies = []
        for k in range(1, size):
            peer = lax.rem(me + k, size)
            copy = pltpu.make_async_remote_copy(
                src_ref=stat,
                dst_ref=slots_ref.at[me],
                send_sem=send.at[k],
                recv_sem=recv.at[me],
                device_id=device(peer),
                device_id_type=MESH,
            )
            copy.start()
            copies.append(copy)
        slots_ref[me] = stat[...]
        for k in range(1, size):
            peer = lax.rem(me + k, size)
            pltpu.make_async_remote_copy(
                src_ref=stat,
                dst_ref=slots_ref.at[peer],
                send_sem=send.at[k],
                recv_sem=recv.at[peer],
                device_id=device(peer),
                device_id_type=MESH,
            ).wait_recv()
        for copy in copies:
            copy.wait_send()
        return combine(size, lambda i, j: slots_ref[i, j : j + 1, :])

    sums = exchange(group, g, stats_a, sa_send, sa_recv, lambda peer: (peer, z))
    for j, value in enumerate(sums):
        stat[j : j + 1, :] = value
    number, mean, square, shift_grad, along = exchange(
        planes, z, stats_b, sb_send, sb_recv, lambda peer: (g, peer)
    )
    inv_std = lax.rsqrt(square / number + EPSILON)
    gain_grad = along * inv_std
    sums_out[0:1, :] = gain_grad
    sums_out[1:2, :] = shift_grad
    scale = gain[...] * inv_std
    shift_mean = shift_grad / number
    gain_mean = gain_grad / number

    @pl.when(at.works)
    def _():
        live_count = counts[at.slot]

        def finish(t, total):
            here = sub_rows(t, TILE)
            node = lax.broadcasted_iota(jnp.int32, (TILE, 1), 0) + t * TILE
            live = (node < live_count).astype(F32)
            act, grown = elu_pair(pre[here, :])
            normed = (act - mean) * inv_std
            norm_low = ((gain[...] * normed + shift[...]) * live).astype(BF16)
            cot_value = feat_all[here, :].astype(F32) * live
            feat_all[here, :] = norm_low
            grad = scale * (cot_value - shift_mean - normed * gain_mean) * live
            grad = grad * grown
            grad_low = grad.astype(BF16)
            low[here, :] = grad_low
            grad_low = grad_low.astype(F32)
            lane = lax.broadcasted_iota(jnp.int32, (TILE, 128), 1)
            along_mix = grad_low * mix[here, :]
            along_diff = grad_low * diff[here, :]
            spread = jnp.zeros((TILE, 128), F32)
            for h in range(heads):
                part = slice(h * head, (h + 1) * head)
                one = jnp.sum(along_mix[:, part], axis=1, keepdims=True)
                two = jnp.sum(along_diff[:, part], axis=1, keepdims=True)
                spread = jnp.where(lane % heads == h, one, spread)
                dcol[here, h : h + 1] = two
            top = spread.astype(BF16)
            rest = spread - top.astype(F32)
            middle = rest.astype(BF16)
            bottom = (rest - middle.astype(F32)).astype(BF16)
            third = lane // heads
            mask_all[here, 0:128] = jnp.where(
                third == 0, top, jnp.where(third == 1, middle, jnp.where(third == 2, bottom, 0.0))
            ).astype(BF16)
            return total + sum(grad[8 * i : 8 * i + 8] for i in range(TILE // 8))

        total = lax.fori_loop(0, nodes // TILE, finish, zero)
        sums_out[2:3, :] = jnp.sum(total, axis=0, keepdims=True)
        sums_out[3:8, :] = jnp.zeros((5, width), F32)
        last = [
            pltpu.make_async_copy(low, grad_out, out_sem.at[2]),
            pltpu.make_async_copy(feat_all, norm_out, out_sem.at[3]),
            pltpu.make_async_copy(dcol, cols_out, out_sem.at[4]),
            pltpu.make_async_copy(mask_all.at[:, 0:128], parts_out, out_sem.at[5]),
        ]
        for copy in last:
            copy.start()
        for slot in range(2):
            for i, kept in enumerate((p_slot, q_slot)):
                pltpu.make_async_copy(
                    kept.at[slot], (p_out, q_out)[i].at[0, block], p_sem.at[i, slot]
                ).wait()
        pltpu.make_async_copy(hid, hid_out, out_sem.at[1]).wait()
        for copy in last:
            copy.wait()

    @pl.when(jnp.logical_not(at.works))
    def _():
        sums_out[2:8, :] = jnp.zeros((6, width), F32)

    sent(a_moves)
    sent(c_moves)


def backward_kernel(
    dims,
    feat_in,
    hid_in,
    low_in,
    norm_in,
    p_in,
    q_in,
    cols,
    parts,
    wp_in,
    ws_in,
    att,
    out,
    ig_out,
    proj_out,
    skip_out,
    att_out,
    feat,
    hid,
    low,
    back,
    wp,
    ws,
    ig,
    p_slot,
    q_slot,
    n_send,
    n_recv,
    i_send,
    i_recv,
    own_sem,
    in_sem,
    p_sem,
):
    planes, group, slots, rows, nodes, heads, head = dims
    width = heads * head
    at = Place(planes, slots, group)
    g, z = at.g, at.z
    block = sub_rows(z, rows)

    barrier = pltpu.get_barrier_semaphore()
    for k in range(1, planes):
        pl.semaphore_signal(barrier, 1, device_id=(g, lax.rem(z + k, planes)), device_id_type=MESH)
    loads = [
        pltpu.make_async_copy(source, target, in_sem.at[i])
        for i, (source, target) in enumerate(
            ((feat_in, feat), (hid_in, hid), (low_in, low), (wp_in, wp), (ws_in, ws))
        )
    ]

    def fetch(j, h, slot):
        place = pl.ds(pl.multiple_of(j * rows, rows), rows)
        return [
            pltpu.make_async_copy(kept.at[h, :, place], held.at[slot], p_sem.at[i, slot])
            for i, (kept, held) in enumerate(((p_in, p_slot), (q_in, q_slot)))
        ]

    @pl.when(at.works)
    def _():
        for load in loads:
            load.start()
        for copy in fetch(lax.rem(z + 1, planes), 0, 0):
            copy.start()

    pl.semaphore_wait(barrier, planes - 1)

    def send(source, target, send_sems, recv, to):
        return pltpu.make_async_remote_copy(
            src_ref=source.at[sub_rows(to, rows)],
            dst_ref=target.at[at.slot],
            send_sem=send_sems.at[to],
            recv_sem=recv.at[at.slot],
            device_id=(g, to),
            device_id_type=MESH,
        )

    norm_own = pltpu.make_async_copy(norm_in.at[block], out.at[at.slot], own_sem.at[0])
    ig_own = pltpu.make_async_copy(ig.at[block], ig_out.at[at.slot], own_sem.at[1])

    @pl.when(at.works)
    def _():
        for k in range(1, planes):
            send(norm_in, out, n_send, n_recv, lax.rem(z + k, planes)).start()
        norm_own.start()
        for load in loads:
            load.wait()

        @pl.loop(0, width // head)
        def _(f):
            place = sub_rows(f, head)
            skip_out[place, :] = dot(feat[:, place], low[...], (0, 0)).astype(skip_out.dtype)

        att_out[...] = jnp.zeros_like(att_out)

        @pl.loop(0, planes)
        def _(k):
            j = lax.rem(z + 1 + k, planes)
            here = sub_rows(j, rows)
            for h in range(heads):
                part = slice(h * head, (h + 1) * head)
                slot = h % 2
                if h + 1 < heads:
                    for copy in fetch(j, h + 1, (h + 1) % 2):
                        copy.start()
                else:

                    @pl.when(k + 1 < planes)
                    def _():
                        for copy in fetch(lax.rem(j + 1, planes), 0, heads % 2):
                            copy.start()

                for copy in fetch(j, h, slot):
                    copy.wait()
                grad = dot(p_slot[slot], low[:, part], (0, 0))
                along = dot(q_slot[slot], low[:, part], (0, 0))
                spread = dot(q_slot[slot], parts[...], (0, 0))
                lane = lax.broadcasted_iota(jnp.int32, spread.shape, 1)
                mine = (lane % heads == h) & (lane < 3 * heads)
                own = hid[here, part].astype(F32)
                by_src = jnp.sum(own * along, axis=1, keepdims=True) - jnp.sum(
                    jnp.where(mine, spread, 0.0), axis=1, keepdims=True
                )
                by_dst = cols[here, h : h + 1]
                grad = grad + by_dst * att[h : h + 1, :] + by_src * att[heads + h : heads + h + 1, :]
                back[here, part] = grad.astype(BF16)
                att_out[h : h + 1, :] += jnp.sum(by_dst * own, axis=0, keepdims=True)
                att_out[heads + h : heads + h + 1, :] += jnp.sum(by_src * own, axis=0, keepdims=True)
            for f in range(width // head):
                part = slice(f * head, (f + 1) * head)
                ig[here, part] = (
                    dot(back[here, :], wp[part, :], (1, 1)) + dot(low[here, :], ws[part, :], (1, 1))
                ).astype(BF16)

            @pl.when(j != z)
            def _():
                send(ig, ig_out, i_send, i_recv, j).start()

            pl.when(j == z)(ig_own.start)

        @pl.loop(0, width // head)
        def _(f):
            place = sub_rows(f, head)
            proj_out[place, :] = dot(feat[:, place], back[...], (0, 0)).astype(proj_out.dtype)

    @pl.when(jnp.logical_not(at.works))
    def _():
        proj_out[...] = jnp.zeros_like(proj_out)
        skip_out[...] = jnp.zeros_like(skip_out)
        att_out[...] = jnp.zeros_like(att_out)

    for s in range(slots):
        for source, target, send_sems, recv in (
            (norm_in, out, n_send, n_recv),
            (ig, ig_out, i_send, i_recv),
        ):

            @pl.when(jnp.logical_not(at.mine[s]))
            def _():
                pltpu.make_async_remote_copy(
                    src_ref=source.at[sub_rows(0, rows)],
                    dst_ref=target.at[s],
                    send_sem=send_sems.at[0],
                    recv_sem=recv.at[s],
                    device_id=(g, at.owner(s)),
                    device_id_type=MESH,
                ).wait_recv()

    @pl.when(at.works)
    def _():
        norm_own.wait()
        ig_own.wait()
        for k in range(1, planes):
            to = lax.rem(z + k, planes)
            send(norm_in, out, n_send, n_recv, to).wait_send()
            send(ig, ig_out, i_send, i_recv, to).wait_send()


def params(collective_id):
    return pltpu.CompilerParams(
        collective_id=collective_id, has_side_effects=True, vmem_limit_bytes=60 * 2**20
    )


def shards(
    planes,
    group,
    features,
    adjacency,
    counts,
    proj_weight,
    skip_weight,
    attn_dst,
    attn_src,
    attn_bias,
    norm_gain,
    norm_shift,
    cotangent,
):
    slots, rows, width_in = features.shape
    nodes = adjacency.shape[2]
    heads, head = attn_dst.shape
    width = heads * head
    dims = (planes, group, slots, rows, nodes, heads, head)
    dma = pltpu.SemaphoreType.DMA

    own = jnp.repeat(jnp.eye(heads, dtype=BF16), head, axis=1)
    dst_row, src_row = own * attn_dst.reshape(1, width), own * attn_src.reshape(1, width)
    att_rows = jnp.concatenate([src_row, dst_row, jnp.zeros((16 - 2 * heads, width), BF16)])
    att_cols = jnp.pad(att_rows.T, ((0, 0), (0, 112)))
    att_both = jnp.concatenate([attn_dst, attn_src]).astype(F32)

    shape = jax.ShapeDtypeStruct
    whole = shape((nodes, width), BF16)
    square = shape((heads, nodes, nodes), BF16)
    feat_all, hid, low, norm, p_all, q_all, cols, parts, sums, _ = pl.pallas_call(
        functools.partial(forward_kernel, dims),
        out_shape=[
            shape((nodes, width_in), BF16),
            whole,
            whole,
            whole,
            square,
            square,
            shape((nodes, 128), F32),
            shape((nodes, 128), BF16),
            shape((8, width), F32),
            whole,
        ],
        in_specs=[ANY, ANY, ANY, SMEM, ANY, ANY, VMEM, VMEM, VMEM, VMEM, VMEM],
        out_specs=[ANY] * 8 + [VMEM, ANY],
        scratch_shapes=[
            pltpu.VMEM((nodes, width_in), BF16),
            pltpu.VMEM((nodes, width), BF16),
            pltpu.VMEM((nodes, nodes), BF16),
            pltpu.VMEM((slots, rows, nodes), BF16),
            pltpu.VMEM((2, rows // 2, nodes), jnp.int32),
            pltpu.VMEM((width_in, width), BF16),
            pltpu.VMEM((width_in, width), BF16),
            pltpu.VMEM((nodes, width), F32),
            pltpu.VMEM((nodes, width), F32),
            pltpu.VMEM((nodes, width), BF16),
            pltpu.VMEM((nodes, width), BF16),
            pltpu.VMEM((nodes, 128), F32),
            pltpu.VMEM((16, nodes), F32),
            pltpu.VMEM((2, rows, nodes), BF16),
            pltpu.VMEM((2, rows, nodes), BF16),
            pltpu.VMEM((rows, nodes), BF16),
            pltpu.VMEM((8, width), F32),
            pltpu.VMEM((group, 8, width), F32),
            pltpu.VMEM((planes, 8, width), F32),
            dma((slots,)),
            dma((planes,)),
            dma((slots,)),
            dma((planes,)),
            dma((slots,)),
            dma((planes,)),
            dma((group,)),
            dma((group,)),
            dma((planes,)),
            dma((planes,)),
            dma((3,)),
            dma((2,)),
            dma((2,)),
            dma((2, 2)),
            dma((6,)),
            dma,
        ],
        compiler_params=params(0),
    )(
        features,
        adjacency,
        cotangent,
        counts,
        proj_weight,
        skip_weight,
        att_rows,
        att_cols,
        attn_bias.reshape(1, width),
        norm_gain.reshape(1, width),
        norm_shift.reshape(1, width),
    )
    output, input_grad, proj_local, skip_local, att_local = pl.pallas_call(
        functools.partial(backward_kernel, dims),
        out_shape=[
            shape((slots, rows, width), BF16),
            shape((slots, rows, width_in), BF16),
            shape((width_in, width), BF16),
            shape((width_in, width), BF16),
            shape((2 * heads, head), F32),
        ],
        in_specs=[ANY] * 6 + [VMEM, VMEM, ANY, ANY, VMEM],
        out_specs=[ANY, ANY, VMEM, VMEM, VMEM],
        scratch_shapes=[
            pltpu.VMEM((nodes, width_in), BF16),
            pltpu.VMEM((nodes, width), BF16),
            pltpu.VMEM((nodes, width), BF16),
            pltpu.VMEM((nodes, width), BF16),
            pltpu.VMEM((width_in, width), BF16),
            pltpu.VMEM((width_in, width), BF16),
            pltpu.VMEM((nodes, width_in), BF16),
            pltpu.VMEM((2, nodes, rows), BF16),
            pltpu.VMEM((2, nodes, rows), BF16),
            dma((planes,)),
            dma((slots,)),
            dma((planes,)),
            dma((slots,)),
            dma((2,)),
            dma((5,)),
            dma((2, 2)),
        ],
        compiler_params=params(1),
    )(feat_all, hid, low, norm, p_all, q_all, cols, parts, proj_weight, skip_weight, att_both)
    proj_grad, skip_grad = lax.psum((proj_local, skip_local), ("graph", "row"))
    att_grad, bias_grad = lax.psum((att_local, sums[2]), ("graph", "row"))
    return (
        output,
        input_grad,
        proj_grad.astype(F32),
        skip_grad.astype(F32),
        att_grad[:heads],
        att_grad[heads:],
        bias_grad,
        sums[0],
        sums[1],
    )


def solution(mesh):
    placed = (
        P("graph", "row", None),
        P("graph", "row", None),
        P("graph"),
        P(),
        P(),
        P(),
        P(),
        P(),
        P(),
        P(),
        P("graph", "row", None),
    )
    return jax.shard_map(
        functools.partial(shards, mesh.shape["row"], mesh.shape["graph"]),
        mesh=mesh,
        in_specs=placed,
        out_specs=(
            P("graph", "row", None),
            P("graph", "row", None),
            P(),
            P(),
            P(),
            P(),
            P(),
            P(),
            P(),
        ),
        check_vma=False,
    )
```

```python
import functools

import jax
import jax.numpy as jnp
from jax import lax
from jax.experimental import pallas as pl
from jax.experimental.pallas import tpu as pltpu
from jax.sharding import PartitionSpec as P

EPSILON = 1e-05
MESH = pl.DeviceIdType.MESH
LOG2E = 1.4426950408889634
LN2 = 0.6931471805599453
MASKED = -1e30
TILE = 64
WIDE_TILE = 256
F32 = jnp.float32
BF16 = jnp.bfloat16
ANY = pl.BlockSpec(memory_space=pl.ANY)
VMEM = pl.BlockSpec(memory_space=pltpu.VMEM)
SMEM = pl.BlockSpec(memory_space=pltpu.SMEM)


def dot(left, right, dims=(1, 0)):
    contract = (((dims[0],), (dims[1],)), ((), ()))
    return lax.dot_general(left, right, contract, preferred_element_type=F32)


class Place:
    def __init__(self, planes, slots, group):
        self.planes, self.slots, self.group = planes, slots, group
        self.g = lax.axis_index("graph")
        self.z = lax.axis_index("row")
        self.core = lax.rem(self.g, 2)
        turn = jnp.where(self.core == 1, self.z, planes - 1 - self.z)
        self.mine = [turn == self.turn(s) for s in range(slots)]
        self.slot = sum(jnp.where(own, s, 0) for s, own in enumerate(self.mine))
        self.works = functools.reduce(jnp.logical_or, self.mine)

    def turn(self, slot):
        return slot * self.planes // (self.slots + 1)

    def owner(self, slot):
        turn = self.turn(slot)
        return jnp.where(self.core == 1, turn, self.planes - 1 - turn)


def elu_pair(value):
    grown = jnp.exp(jnp.minimum(value, 0.0))
    return jnp.where(value > 0, value, grown - 1.0), grown


def sub_rows(index, size):
    return pl.ds(pl.multiple_of(index * size, size), size)


def layer_kernel(
    dims,
    feat,
    adj,
    cot,
    counts,
    wp_in,
    ws_in,
    att_rows,
    att_cols,
    bias,
    gain,
    shift,
    out,
    ig_out,
    proj_out,
    skip_out,
    sums_out,
    p_all,
    q_all,
    feat_all,
    hid,
    wide,
    mask_own,
    adj_in,
    wp,
    ws,
    pre,
    mix,
    diff,
    low,
    dcol,
    parts,
    srow,
    p_slot,
    q_slot,
    centered,
    p_back,
    q_back,
    stat,
    stats_a,
    stats_b,
    swap,
    plane_in,
    line_in,
    line_out,
    f_send,
    f_recv,
    a_send,
    a_recv,
    c_send,
    c_recv,
    n_send,
    n_recv,
    i_send,
    i_recv,
    sa_send,
    sa_recv,
    sb_send,
    sb_recv,
    r_send,
    r_recv,
    own_sem,
    adj_sem,
    w_sem,
    p_sem,
    out_sem,
):
    planes, group, slots, rows, nodes, heads, head, width_in = dims
    width = heads * head
    tile = min(TILE, TILE * 1024 // nodes)
    tall = min(WIDE_TILE * 1024 // nodes * 1024 // nodes, rows)
    at = Place(planes, slots, group)
    g, z = at.g, at.z
    block = sub_rows(z, rows)
    mask_all = wide.at[:, 0:nodes]
    back = wide.at[:, 0:width]
    stage = wide.at[:, width : 2 * width]

    barrier = pltpu.get_barrier_semaphore()
    for k in range(1, planes):
        pl.semaphore_signal(barrier, 1, device_id=(g, lax.rem(z + k, planes)), device_id_type=MESH)
    for k in range(1, group):
        pl.semaphore_signal(barrier, 1, device_id=(lax.rem(g + k, group), z), device_id_type=MESH)
    load_wp = pltpu.make_async_copy(wp_in, wp, w_sem.at[0])
    load_ws = pltpu.make_async_copy(ws_in, ws, w_sem.at[1])
    some = adj_in.shape[1]
    cuts = rows // some
    loads = [
        pltpu.make_async_copy(
            adj.at[i // cuts, pl.ds(i % cuts * some, some)], adj_in.at[i % 2], adj_sem.at[i % 2]
        )
        for i in range(cuts * slots)
    ]
    loads[0].start()
    loads[1].start()
    load_wp.start()
    load_ws.start()
    pl.semaphore_wait(barrier, planes - 1 + group - 1)

    def remote(source, target, send, recv, device):
        return pltpu.make_async_remote_copy(
            src_ref=source,
            dst_ref=target,
            send_sem=send,
            recv_sem=recv,
            device_id=device,
            device_id_type=MESH,
        )

    def moves(source, target, send, recv, own):
        found = []
        for s in range(slots):
            to = at.owner(s)
            away = remote(source.at[s], target.at[block], send.at[s], recv.at[z], (g, to))
            local = pltpu.make_async_copy(source.at[s], target.at[block], own)
            found.append((to, away, local))
        return found

    def start(copies):
        for far in range(1, planes):
            for to, away, _ in copies:
                pl.when(jnp.abs(to - z) == far)(away.start)
        for to, _, local in copies:
            pl.when(to == z)(local.start)

    def sent(copies):
        for to, away, _ in copies:
            pl.when(to != z)(away.wait_send)

    def arrived(k, source, target, send, recv, own):
        src = lax.rem(z + k, planes)
        there = target.at[sub_rows(src, rows)]
        pl.when(k == 0)(pltpu.make_async_copy(source.at[0], there, own).wait)
        pl.when(k != 0)(remote(source.at[0], there, send.at[0], recv.at[src], (g, src)).wait_recv)
        return src

    f_args = (feat, feat_all, f_send, f_recv, own_sem.at[0])
    a_args = (mask_own, mask_all, a_send, a_recv, own_sem.at[1])
    c_args = (cot, low, c_send, c_recv, own_sem.at[2])
    f_moves, a_moves, c_moves = moves(*f_args), moves(*a_args), moves(*c_args)
    start(f_moves)

    for i, load in enumerate(loads):
        load.wait()
        live_own = counts[i // cuts]

        @pl.loop(0, some // tile)
        def _(t):
            first = i % cuts * some + t * tile
            shape = (tile, nodes)
            row = lax.broadcasted_iota(jnp.int32, shape, 0) + (z * rows + first)
            col = lax.broadcasted_iota(jnp.int32, shape, 1)
            allowed = (adj_in[i % 2, sub_rows(t, tile), :] > 0) | (row == col)
            allowed = allowed & (row < live_own) & (col < live_own)
            mask_own[i // cuts, pl.ds(pl.multiple_of(first, tile), tile), :] = jnp.where(
                allowed, 0.0, MASKED
            ).astype(BF16)

        if i + 2 < len(loads):
            loads[i + 2].start()

    load_wp.wait()
    load_ws.wait()
    start(a_moves)
    start(c_moves)
    live_count = counts[at.slot]

    def live_of(first, size):
        node = lax.broadcasted_iota(jnp.int32, (size, 1), 0) + first
        return (node < live_count).astype(F32)

    depth = p_slot.shape[0]

    def keep(h, here):
        slot = h % depth
        return [
            pltpu.make_async_copy(p_slot.at[slot], p_all.at[h, here], p_sem.at[0, slot]),
            pltpu.make_async_copy(q_slot.at[slot], q_all.at[h, here], p_sem.at[1, slot]),
        ]

    @pl.when(at.works)
    def _():
        @pl.loop(0, planes)
        def _(k):
            src = arrived(k, *f_args)
            here = sub_rows(src, rows)
            value = feat_all[here, :]
            for h in range(heads):
                part = slice(h * head, (h + 1) * head)
                hid[here, part] = dot(value, wp[:, part]).astype(BF16)
                pre[here, part] = dot(value, ws[:, part])
            made = hid[here, :]
            dcol[here, :] = dot(made, att_cols[...]) * LOG2E
            srow[:, here] = dot(att_rows[...], made, (1, 1)) * LOG2E

        @pl.loop(0, planes)
        def _(k):
            src = arrived(k, *a_args)
            here = sub_rows(src, rows)
            for h in range(heads):
                part = slice(h * head, (h + 1) * head)
                slot = h % depth

                @pl.when((k > 0) | (h >= depth))
                def _():
                    for copy in keep(h, here):
                        copy.wait()

                @pl.loop(0, rows // tall)
                def _(t):
                    first = src * rows + t * tall
                    there = pl.ds(pl.multiple_of(first, tall), tall)
                    inside = sub_rows(t, tall)
                    masked = mask_all[there, :].astype(F32) + srow[h : h + 1, :]
                    dst = dcol[there, heads + h : heads + h + 1]

                    def leaky(raw):
                        small = jnp.exp2(-jnp.abs(raw))
                        soft = jnp.log(1.0 + small)
                        return soft + jnp.maximum(raw * (1.25 * LN2), raw * (0.25 * LN2)), soft

                    peak, _ = leaky(jnp.max(masked, axis=1, keepdims=True) + dst)
                    raw = masked + dst
                    logit, soft = leaky(raw)
                    weight = jnp.exp2((logit - peak) * (0.8 * LOG2E))
                    total = jnp.sum(weight, axis=1, keepdims=True)
                    share = weight * (live_of(first, tall) / total)
                    slope = jnp.exp2(jnp.minimum(raw, 0.0) - soft * LOG2E) * 0.8 + 0.2
                    sloped = share * slope
                    p_slot[slot, inside, :] = share.astype(BF16)
                    q_slot[slot, inside, :] = sloped.astype(BF16)
                    middle = jnp.sum(sloped, axis=1, keepdims=True)
                    centered[inside, :] = (sloped - middle * share).astype(BF16)

                for copy in keep(h, here):
                    copy.start()
                mixed = dot(p_slot[slot], hid[:, part])
                mix[here, part] = mixed.astype(BF16)
                pre[here, part] += mixed + bias[:, part]
                diff[here, part] = dot(centered[...], hid[:, part]).astype(BF16)

    zero = jnp.zeros((8, width), F32)
    tiles = nodes // tile

    def fold(value):
        return sum(value[8 * i : 8 * i + 8] for i in range(tile // 8))

    def total_of(value):
        return jnp.sum(value, axis=0, keepdims=True)

    @pl.when(at.works)
    def _():
        def add_act(t, total):
            act, _ = elu_pair(pre[sub_rows(t, tile), :])
            return total + fold(act * live_of(t * tile, tile))

        number = jnp.maximum(live_count, 1).astype(F32)
        mean = total_of(lax.fori_loop(0, tiles, add_act, zero)) / number

        def add_square(t, total):
            act, _ = elu_pair(pre[sub_rows(t, tile), :])
            off = act - mean
            return total + fold(off * off * live_of(t * tile, tile))

        stat[2:3, :] = total_of(lax.fori_loop(0, tiles, add_square, zero))
        stat[0:1, :] = jnp.full((1, width), live_count.astype(F32))
        stat[1:2, :] = mean
        stat[3:8, :] = jnp.zeros((5, width), F32)

    @pl.when(jnp.logical_not(at.works))
    def _():
        stat[...] = zero

    def exchange(which, size, me, held, send, recv, device):
        copies = []
        for k in range(1, size):
            peer = lax.rem(me + k, size)
            copy = remote(
                stat, held.at[which, me], send.at[which, k], recv.at[which, me], device(peer)
            )
            copy.start()
            copies.append(copy)
        held[which, me] = stat[...]
        for k in range(1, size):
            peer = lax.rem(me + k, size)
            remote(
                stat, held.at[which, peer], send.at[which, k], recv.at[which, peer], device(peer)
            ).wait_recv()
        for copy in copies:
            copy.wait_send()

    def everywhere(which, combine):
        exchange(which, group, g, stats_a, sa_send, sa_recv, lambda peer: (peer, z))
        combine(stats_a.at[which], group)
        exchange(which, planes, z, stats_b, sb_send, sb_recv, lambda peer: (g, peer))
        combine(stats_b.at[which], planes)

    def spread_out(held, size):
        number = sum(held[i, 0:1, :] for i in range(size))
        mean = sum(held[i, 0:1, :] * held[i, 1:2, :] for i in range(size))
        mean = mean / jnp.maximum(number, 1.0)
        square = zero[0:1]
        for i in range(size):
            off = held[i, 1:2, :] - mean
            square = square + held[i, 2:3, :] + held[i, 0:1, :] * off * off
        stat[0:1, :] = number
        stat[1:2, :] = mean
        stat[2:3, :] = square

    def plain_sum(held, size):
        stat[...] = sum(held[i] for i in range(size))

    everywhere(0, spread_out)
    number, mean = stat[0:1, :], stat[1:2, :]
    inv_std = lax.rsqrt(stat[2:3, :] / number + EPSILON)

    def give(target, send, recv, to):
        return remote(
            stage.at[sub_rows(to, rows)],
            target.at[at.slot],
            send.at[to],
            recv.at[at.slot],
            (g, to),
        )

    norm_own = pltpu.make_async_copy(stage.at[block], out.at[at.slot], own_sem.at[3])
    ig_own = pltpu.make_async_copy(stage.at[block], ig_out.at[at.slot], own_sem.at[4])

    @pl.when(at.works)
    def _():
        @pl.loop(0, planes)
        def _(k):
            j = lax.rem(z + 1 + k, planes)

            @pl.loop(0, rows // tile)
            def _(t):
                first = j * rows + t * tile
                here = pl.ds(pl.multiple_of(first, tile), tile)
                act, _ = elu_pair(pre[here, :])
                normed = (act - mean) * inv_std
                value = (gain[...] * normed + shift[...]) * live_of(first, tile)
                stage[here, :] = value.astype(BF16)

            pl.when(j != z)(give(out, n_send, n_recv, j).start)
            pl.when(j == z)(norm_own.start)

        for k in range(planes):
            arrived(jnp.int32(k), *c_args)

        def add_grad(t, totals):
            here = sub_rows(t, tile)
            act, _ = elu_pair(pre[here, :])
            grad = low[here, :].astype(F32) * live_of(t * tile, tile)
            return totals[0] + fold(grad), totals[1] + fold(grad * (act - mean))

        plain, along = lax.fori_loop(0, tiles, add_grad, (zero, zero))
        stat[0:1, :] = total_of(plain)
        stat[1:2, :] = total_of(along)
        stat[2:8, :] = jnp.zeros((6, width), F32)

    @pl.when(jnp.logical_not(at.works))
    def _():
        stat[...] = zero

    everywhere(1, plain_sum)
    shift_grad = stat[0:1, :]
    gain_grad = stat[1:2, :] * inv_std
    sums_out[0:1, :] = gain_grad
    sums_out[1:2, :] = shift_grad
    scale = gain[...] * inv_std
    shift_mean = shift_grad / number
    gain_mean = gain_grad / number
    stat[...] = zero

    @pl.when(at.works)
    def _():
        def finish(t, total):
            here = sub_rows(t, tile)
            live = live_of(t * tile, tile)
            act, grown = elu_pair(pre[here, :])
            normed = (act - mean) * inv_std
            grad = low[here, :].astype(F32) * live
            grad = scale * (grad - shift_mean - normed * gain_mean) * live * grown
            grad_low = grad.astype(BF16)
            low[here, :] = grad_low
            grad_low = grad_low.astype(F32)
            lane = lax.broadcasted_iota(jnp.int32, (tile, 128), 1)
            along_mix = grad_low * mix[here, :].astype(F32)
            along_diff = grad_low * diff[here, :].astype(F32)
            spread = jnp.zeros((tile, 128), F32)
            for h in range(heads):
                part = slice(h * head, (h + 1) * head)
                one = jnp.sum(along_mix[:, part], axis=1, keepdims=True)
                spread = jnp.where(lane % heads == h, one, spread)
                dcol[here, h : h + 1] = jnp.sum(along_diff[:, part], axis=1, keepdims=True)
            top = spread.astype(BF16)
            rest = spread - top.astype(F32)
            middle = rest.astype(BF16)
            bottom = (rest - middle.astype(F32)).astype(BF16)
            third = lane // heads
            parts[here, :] = jnp.where(
                third == 0, top, jnp.where(third == 1, middle, jnp.where(third == 2, bottom, 0.0))
            ).astype(BF16)
            return total + fold(grad)

        stat[0:1, :] = total_of(lax.fori_loop(0, tiles, finish, zero))
        for h in range(depth):
            for copy in keep(h, block):
                copy.wait()

    chips = group // 2
    chip, core = g // 2, lax.rem(g, 2)
    partner = g + 1 - 2 * core
    half_width = width // 2
    quarter = half_width // 2
    strip = width_in // chips
    down = min(planes, strip // 16)
    across = planes // down
    mine = pl.ds(pl.multiple_of(core * quarter, quarter), quarter)
    other = pl.ds(pl.multiple_of((1 - core) * quarter, quarter), quarter)

    def unit_of(u):
        kept = diff if u < 2 else mix
        return kept.at[0:width_in, u % 2 * half_width : (u % 2 + 1) * half_width]

    def strip_of(index):
        return pl.ds(pl.multiple_of(index * strip, strip), strip)

    def piece_of(index):
        high, wide_piece = strip // down, quarter // across
        return (
            pl.ds(pl.multiple_of(lax.rem(index, down) * high, high), high),
            pl.ds(pl.multiple_of(index // down * wide_piece, wide_piece), wide_piece),
        )

    def to_core(u):
        return remote(
            unit_of(u).at[:, other], swap.at[u], r_send.at[u, 0, 0], r_recv.at[u, 0, 0], (partner, z)
        )

    def to_chip(u, peer, landed):
        return remote(
            unit_of(u).at[strip_of(peer), mine],
            plane_in.at[u, landed],
            r_send.at[u, 1, peer],
            r_recv.at[u, 1, landed],
            (2 * peer + core, z),
        )

    def to_line(u, peer, landed):
        return remote(
            line_out.at[u].at[piece_of(peer)],
            line_in.at[u, landed],
            r_send.at[u, 2, peer],
            r_recv.at[u, 2, landed],
            (g, peer),
        )

    def from_line(u, peer, landed):
        where = swap.at[u].at[strip_of(chip)].at[piece_of(landed)]
        return remote(where, where, r_send.at[u, 3, peer], r_recv.at[u, 3, landed], (g, peer))

    def from_chip(u, peer, landed):
        where = swap.at[u].at[strip_of(landed)]
        return remote(
            where, where, r_send.at[u, 4, peer], r_recv.at[u, 4, landed], (2 * peer + core, z)
        )

    def from_core(u, columns):
        return remote(
            swap.at[u],
            unit_of(u).at[:, columns],
            r_send.at[u, 5, 0],
            r_recv.at[u, 5, 0],
            (partner, z),
        )

    def others(size, me):
        return [lax.rem(me + k, size) for k in range(1, size)]

    def step(u, number):
        unit = unit_of(u)
        if number == 0:
            to_core(u).start()
        if number == 1:
            to_core(u).wait()

            @pl.loop(0, width_in // tall)
            def _(t):
                here = sub_rows(t, tall)
                value = unit[here, mine].astype(F32) + swap[u, here, :].astype(F32)
                unit[here, mine] = value.astype(BF16)

            for peer in others(chips, chip):
                to_chip(u, peer, chip).start()
        if number == 2:
            for peer in others(chips, chip):
                to_chip(u, peer, peer).wait_recv()
            value = unit[strip_of(chip), mine].astype(F32)
            for peer in others(chips, chip):
                value = value + plane_in[u, peer].astype(F32)
            line_out[u] = value.astype(BF16)
            for peer in others(planes, z):
                to_line(u, peer, z).start()
            for peer in others(chips, chip):
                to_chip(u, peer, chip).wait_send()
        if number == 3:
            for peer in others(planes, z):
                to_line(u, peer, peer).wait_recv()
            value = line_out.at[u][piece_of(z)].astype(F32)
            for peer in others(planes, z):
                value = value + line_in[u, peer].astype(F32)
            swap.at[u].at[strip_of(chip)][piece_of(z)] = value.astype(BF16)
            for peer in others(planes, z):
                from_line(u, peer, z).start()
            for peer in others(planes, z):
                to_line(u, peer, z).wait_send()
        if number == 4:
            for peer in others(planes, z):
                from_line(u, peer, peer).wait_recv()
            for peer in others(chips, chip):
                from_chip(u, peer, chip).start()
            for peer in others(planes, z):
                from_line(u, peer, z).wait_send()
        if number == 5:
            for peer in others(chips, chip):
                from_chip(u, peer, peer).wait_recv()
            from_core(u, mine).start()

            @pl.loop(0, width_in // tall)
            def _(t):
                here = sub_rows(t, tall)
                unit[here, mine] = swap[u, here, :]

            for peer in others(chips, chip):
                from_chip(u, peer, chip).wait_send()
        if number == 6:
            from_core(u, other).wait_recv()
            from_core(u, mine).wait_send()
            answer(u).start()

    def answer(u):
        target = skip_out if u < 2 else proj_out
        columns = slice(u % 2 * half_width, (u % 2 + 1) * half_width)
        return pltpu.make_async_copy(unit_of(u), target.at[:, columns], out_sem.at[u])

    def fetch(j, h):
        place = pl.ds(pl.multiple_of(j * rows, rows), rows)
        slot = h % 2
        return [
            pltpu.make_async_copy(p_all.at[h, :, place], p_back.at[slot], p_sem.at[2, slot]),
            pltpu.make_async_copy(q_all.at[h, :, place], q_back.at[slot], p_sem.at[3, slot]),
        ]

    def product(u, right):
        unit = unit_of(u)
        columns = slice(u % 2 * half_width, (u % 2 + 1) * half_width)

        @pl.when(at.works)
        def _():
            @pl.loop(0, width_in // head)
            def _(f):
                place = sub_rows(f, head)
                unit[place, :] = dot(feat_all[:, place], right[:, columns], (0, 0)).astype(BF16)

        @pl.when(jnp.logical_not(at.works))
        def _():
            unit[...] = jnp.zeros_like(unit)

    @pl.when(at.works)
    def _():
        for copy in fetch(lax.rem(z + 1, planes), 0):
            copy.start()

    for u in (0, 1):
        product(u, low)
        step(u, 0)

    def source_block(k, turn):
        j = lax.rem(z + 1 + k, planes)
        here = sub_rows(j, rows)
        per_turn = heads // 2
        for h in range(turn * per_turn, (turn + 1) * per_turn):
            part = slice(h * head, (h + 1) * head)
            slot = h % 2
            if h + 1 < (turn + 1) * per_turn:
                for copy in fetch(j, h + 1):
                    copy.start()
            else:

                @pl.when(k + 1 < planes)
                def _():
                    for copy in fetch(lax.rem(j + 1, planes), turn * per_turn):
                        copy.start()

                if turn == 0:

                    @pl.when(k + 1 == planes)
                    def _():
                        for copy in fetch(lax.rem(z + 1, planes), per_turn):
                            copy.start()

            for copy in fetch(j, h):
                copy.wait()
            grad = dot(p_back[slot], low[:, part], (0, 0))
            along = dot(q_back[slot], low[:, part], (0, 0))
            spread = dot(q_back[slot], parts[...], (0, 0))
            lane = lax.broadcasted_iota(jnp.int32, spread.shape, 1)
            chosen = (lane % heads == h) & (lane < 3 * heads)
            own = hid[here, part].astype(F32)
            by_src = jnp.sum(own * along, axis=1, keepdims=True) - jnp.sum(
                jnp.where(chosen, spread, 0.0), axis=1, keepdims=True
            )
            by_dst = dcol[here, h : h + 1]
            att_src, att_dst = (
                att_rows[i : i + 1, part].astype(F32) for i in (h, heads + h)
            )
            grad = grad + by_dst * att_dst + by_src * att_src
            back[here, part] = grad.astype(BF16)
            stat[1:2, part] += total_of(by_dst * own)
            stat[2:3, part] += total_of(by_src * own)
        if turn == 1:
            pl.when(j != z)(give(out, n_send, n_recv, j).wait_send)
            pl.when(j == z)(norm_own.wait)
            for f in range(width_in // head):
                part = slice(f * head, (f + 1) * head)
                stage[here, part] = (
                    dot(back[here, :], wp[part, :], (1, 1)) + dot(low[here, :], ws[part, :], (1, 1))
                ).astype(BF16)
            pl.when(j != z)(give(ig_out, i_send, i_recv, j).start)
            pl.when(j == z)(ig_own.start)

    for turn in range(2):

        @pl.loop(0, planes)
        def _(k):
            pl.when(at.works)(functools.partial(source_block, k, turn))
            for when, work in PLAN[turn]:

                @pl.when(k == when)
                def _():
                    for u, number in work:
                        step(u, number)

        product(2 + turn, back)
        step(2 + turn, 0)

    for u, number in PLAN[2]:
        step(u, number)
    everywhere(0, plain_sum)
    sums_out[2:5, :] = stat[0:3, :]
    sums_out[5:8, :] = jnp.zeros((3, width), F32)
    for u, number in PLAN[3]:
        step(u, number)

    for s in range(slots):
        for target, send, recv in ((out, n_send, n_recv), (ig_out, i_send, i_recv)):
            pl.when(jnp.logical_not(at.mine[s]))(
                remote(
                    stage.at[sub_rows(0, rows)],
                    target.at[s],
                    send.at[0],
                    recv.at[s],
                    (g, at.owner(s)),
                ).wait_recv
            )

    @pl.when(at.works)
    def _():
        ig_own.wait()
        for peer in others(planes, z):
            give(ig_out, i_send, i_recv, peer).wait_send()

    for u in range(4):
        answer(u).wait()
    sent(f_moves)
    sent(a_moves)
    sent(c_moves)


PLAN = (
    ((0, ((0, 1),)), (1, ((1, 1),)), (3, ((0, 2), (1, 2)))),
    ((0, ((2, 1),)), (1, ((0, 3), (1, 3))), (2, ((2, 2),)), (3, ((0, 4), (1, 4)))),
    ((3, 1), (2, 3), (0, 5), (1, 5), (3, 2), (2, 4), (3, 3), (0, 6), (1, 6)),
    ((2, 5), (3, 4), (2, 6), (3, 5), (3, 6)),
)


def shards(
    planes,
    group,
    features,
    adjacency,
    counts,
    proj_weight,
    skip_weight,
    attn_dst,
    attn_src,
    attn_bias,
    norm_gain,
    norm_shift,
    cotangent,
):
    slots, rows, width_in = features.shape
    nodes = adjacency.shape[2]
    heads, head = attn_dst.shape
    width = heads * head
    dims = (planes, group, slots, rows, nodes, heads, head, width_in)
    dma = pltpu.SemaphoreType.DMA
    chips = group // 2
    strip, quarter = width_in // chips, width // 4
    down = min(planes, strip // 16)
    piece = (strip // down, quarter // (planes // down))
    tallest = max(nodes, width_in)
    depth = 2 if nodes <= 1024 else 1

    own = jnp.repeat(jnp.eye(heads, dtype=BF16), head, axis=1)
    dst_row, src_row = own * attn_dst.reshape(1, width), own * attn_src.reshape(1, width)
    att_rows = jnp.concatenate([src_row, dst_row, jnp.zeros((16 - 2 * heads, width), BF16)])
    att_cols = jnp.pad(att_rows.T, ((0, 0), (0, 112)))

    shape = jax.ShapeDtypeStruct
    vmem = pltpu.VMEM
    square = shape((heads, nodes, nodes), BF16)
    output, input_grad, proj_grad, skip_grad, sums, _, _ = pl.pallas_call(
        functools.partial(layer_kernel, dims),
        out_shape=[
            shape((slots, rows, width), BF16),
            shape((slots, rows, width_in), BF16),
            shape((width_in, width), BF16),
            shape((width_in, width), BF16),
            shape((8, width), F32),
            square,
            square,
        ],
        in_specs=[ANY, ANY, ANY, SMEM, ANY, ANY, VMEM, VMEM, VMEM, VMEM, VMEM],
        out_specs=[ANY, ANY, ANY, ANY, VMEM, ANY, ANY],
        scratch_shapes=[
            vmem((nodes, width_in), BF16),
            vmem((nodes, width), BF16),
            vmem((nodes, max(nodes, 2 * width)), BF16),
            vmem((slots, rows, nodes), BF16),
            vmem((2, rows // 4, nodes), jnp.int32),
            vmem((width_in, width), BF16),
            vmem((width_in, width), BF16),
            vmem((nodes, width), F32),
            vmem((tallest, width), BF16),
            vmem((tallest, width), BF16),
            vmem((nodes, width), BF16),
            vmem((nodes, 128), F32),
            vmem((nodes, 128), BF16),
            vmem((16, nodes), F32),
            vmem((depth, rows, nodes), BF16),
            vmem((depth, rows, nodes), BF16),
            vmem((rows, nodes), BF16),
            vmem((2, nodes, rows), BF16),
            vmem((2, nodes, rows), BF16),
            vmem((8, width), F32),
            vmem((2, group, 8, width), F32),
            vmem((2, planes, 8, width), F32),
            vmem((4, width_in, quarter), BF16),
            vmem((4, chips, strip, quarter), BF16),
            vmem((4, planes) + piece, BF16),
            vmem((4, strip, quarter), BF16),
            dma((slots,)),
            dma((planes,)),
            dma((slots,)),
            dma((planes,)),
            dma((slots,)),
            dma((planes,)),
            dma((planes,)),
            dma((slots,)),
            dma((planes,)),
            dma((slots,)),
            dma((2, group)),
            dma((2, group)),
            dma((2, planes)),
            dma((2, planes)),
            dma((4, 6, max(chips, planes))),
            dma((4, 6, max(chips, planes))),
            dma((5,)),
            dma((2,)),
            dma((2,)),
            dma((4, 2)),
            dma((4,)),
        ],
        compiler_params=pltpu.CompilerParams(
            collective_id=0, has_side_effects=True, vmem_limit_bytes=63 * 2**20
        ),
    )(
        features,
        adjacency,
        cotangent,
        counts,
        proj_weight,
        skip_weight,
        att_rows,
        att_cols,
        attn_bias.reshape(1, width),
        norm_gain.reshape(1, width),
        norm_shift.reshape(1, width),
    )
    return (
        output,
        input_grad,
        proj_grad.astype(F32),
        skip_grad.astype(F32),
        sums[3].reshape(heads, head),
        sums[4].reshape(heads, head),
        sums[2],
        sums[0],
        sums[1],
    )


def solution(mesh):
    placed = (
        P("graph", "row", None),
        P("graph", "row", None),
        P("graph"),
        P(),
        P(),
        P(),
        P(),
        P(),
        P(),
        P(),
        P("graph", "row", None),
    )
    return jax.shard_map(
        functools.partial(shards, mesh.shape["row"], mesh.shape["graph"]),
        mesh=mesh,
        in_specs=placed,
        out_specs=(
            P("graph", "row", None),
            P("graph", "row", None),
            P(),
            P(),
            P(),
            P(),
            P(),
            P(),
            P(),
        ),
        check_vma=False,
    )
```

```python
import functools

import jax
import jax.numpy as jnp
from jax import lax
from jax.experimental import pallas as pl
from jax.experimental.pallas import tpu as pltpu
from jax.sharding import PartitionSpec as P

EPSILON = 1e-05
MESH = pl.DeviceIdType.MESH
LOG2E = 1.4426950408889634
LN2 = 0.6931471805599453
MASKED = -1e30
TILE = 64
WIDE_TILE = 256
ROUNDS = 8
F32 = jnp.float32
BF16 = jnp.bfloat16
ANY = pl.BlockSpec(memory_space=pl.ANY)
VMEM = pl.BlockSpec(memory_space=pltpu.VMEM)
SMEM = pl.BlockSpec(memory_space=pltpu.SMEM)


def dot(left, right, dims=(1, 0)):
    contract = (((dims[0],), (dims[1],)), ((), ()))
    return lax.dot_general(left, right, contract, preferred_element_type=F32)


class Place:
    def __init__(self, planes, slots, group):
        self.planes, self.slots, self.group = planes, slots, group
        self.g = lax.axis_index("graph")
        self.z = lax.axis_index("row")
        self.core = lax.rem(self.g, 2)
        turn = jnp.where(self.core == 1, self.z, planes - 1 - self.z)
        self.mine = [turn == self.turn(s) for s in range(slots)]
        self.slot = sum(jnp.where(own, s, 0) for s, own in enumerate(self.mine))
        self.works = functools.reduce(jnp.logical_or, self.mine)

    def turn(self, slot):
        return slot * self.planes // (self.slots + 1)

    def owner(self, slot):
        turn = self.turn(slot)
        return jnp.where(self.core == 1, turn, self.planes - 1 - turn)


def sub_rows(index, size):
    return pl.ds(pl.multiple_of(index * size, size), size)


def layer_kernel(
    dims,
    feat,
    adj,
    cot,
    counts,
    wp_in,
    ws_in,
    att_dst_in,
    att_src_in,
    bias,
    gain,
    shift,
    out,
    ig_out,
    proj_out,
    skip_out,
    sums_out,
    p_all,
    q_all,
    att_rows,
    feat_all,
    hid,
    wide,
    mask_own,
    adj_in,
    wp,
    ws,
    pre,
    mix,
    diff,
    low,
    dcol,
    parts,
    srow,
    p_slot,
    q_slot,
    centered,
    p_back,
    q_back,
    stat,
    stats_a,
    stats_b,
    swap,
    plane_in,
    line_in,
    line_out,
    f_send,
    f_recv,
    a_send,
    a_recv,
    c_send,
    c_recv,
    n_send,
    n_recv,
    i_send,
    i_recv,
    sa_send,
    sa_recv,
    sb_send,
    sb_recv,
    r_send,
    r_recv,
    own_sem,
    adj_sem,
    w_sem,
    p_sem,
    out_sem,
):
    planes, group, slots, rows, nodes, heads, head, width_in = dims
    width = heads * head
    tile = min(TILE, TILE * 1024 // nodes)
    tall = min(WIDE_TILE * 1024 // nodes * 1024 // nodes, rows)
    at = Place(planes, slots, group)
    g, z = at.g, at.z
    block = sub_rows(z, rows)
    mask_all = wide.at[:, 0:nodes]
    back = wide.at[:, 0:width]
    stage = wide.at[:, width : 2 * width]
    shared = wide.shape[1] < 3 * width
    ig = stage if shared else wide.at[:, 2 * width : 3 * width]

    barrier = pltpu.get_barrier_semaphore()
    for k in range(1, planes):
        pl.semaphore_signal(barrier, 1, device_id=(g, lax.rem(z + k, planes)), device_id_type=MESH)
    for k in range(1, group):
        pl.semaphore_signal(barrier, 1, device_id=(lax.rem(g + k, group), z), device_id_type=MESH)
    load_wp = pltpu.make_async_copy(wp_in, wp, w_sem.at[0])
    load_ws = pltpu.make_async_copy(ws_in, ws, w_sem.at[1])
    some = adj_in.shape[1]
    cuts = rows // some
    loads = [
        pltpu.make_async_copy(
            adj.at[i // cuts, pl.ds(i % cuts * some, some)], adj_in.at[i % 2], adj_sem.at[i % 2]
        )
        for i in range(cuts * slots)
    ]
    loads[0].start()
    loads[1].start()
    load_wp.start()
    load_ws.start()
    pl.semaphore_wait(barrier, planes - 1 + group - 1)

    def remote(source, target, send, recv, device):
        return pltpu.make_async_remote_copy(
            src_ref=source,
            dst_ref=target,
            send_sem=send,
            recv_sem=recv,
            device_id=device,
            device_id_type=MESH,
        )

    def moves(source, target, send, recv, own):
        found = []
        for s in range(slots):
            to = at.owner(s)
            away = remote(source.at[s], target.at[block], send.at[s], recv.at[z], (g, to))
            local = pltpu.make_async_copy(source.at[s], target.at[block], own)
            found.append((to, away, local))
        return found

    def start(copies):
        for far in range(1, planes):
            for to, away, _ in copies:
                pl.when(jnp.abs(to - z) == far)(away.start)
        for to, _, local in copies:
            pl.when(to == z)(local.start)

    def sent(copies):
        for to, away, _ in copies:
            pl.when(to != z)(away.wait_send)

    def arrived(k, source, target, send, recv, own):
        src = lax.rem(z + k, planes)
        there = target.at[sub_rows(src, rows)]
        pl.when(k == 0)(pltpu.make_async_copy(source.at[0], there, own).wait)
        pl.when(k != 0)(remote(source.at[0], there, send.at[0], recv.at[src], (g, src)).wait_recv)
        return src

    f_args = (feat, feat_all, f_send, f_recv, own_sem.at[0])
    a_args = (mask_own, mask_all, a_send, a_recv, own_sem.at[1])
    c_args = (cot, low, c_send, c_recv, own_sem.at[2])
    f_moves, a_moves, c_moves = moves(*f_args), moves(*a_args), moves(*c_args)
    start(f_moves)

    for i, load in enumerate(loads):
        load.wait()
        live_own = counts[i // cuts]

        @pl.loop(0, some // tile)
        def _(t):
            first = i % cuts * some + t * tile
            shape = (tile, nodes)
            row = lax.broadcasted_iota(jnp.int32, shape, 0) + (z * rows + first)
            col = lax.broadcasted_iota(jnp.int32, shape, 1)
            allowed = (adj_in[i % 2, sub_rows(t, tile), :] > 0) | (row == col)
            allowed = allowed & (row < live_own) & (col < live_own)
            mask_own[i // cuts, pl.ds(pl.multiple_of(first, tile), tile), :] = jnp.where(
                allowed, 0.0, MASKED
            ).astype(BF16)

        if i + 2 < len(loads):
            loads[i + 2].start()

    row = lax.broadcasted_iota(jnp.int32, (16, head), 0)
    for h in range(heads):
        src_row, dst_row = (
            kept[h : h + 1, :].astype(F32) for kept in (att_src_in, att_dst_in)
        )
        value = jnp.where(row == h, src_row, jnp.where(row == heads + h, dst_row, 0.0))
        att_rows[:, h * head : (h + 1) * head] = value.astype(BF16)

    load_wp.wait()
    load_ws.wait()
    start(a_moves)
    start(c_moves)
    live_count = counts[at.slot]

    def live_of(first, size):
        node = lax.broadcasted_iota(jnp.int32, (size, 1), 0) + first
        return (node < live_count).astype(F32)

    depth = p_slot.shape[0]

    def keep(h, here):
        slot = h % depth
        return [
            pltpu.make_async_copy(p_slot.at[slot], p_all.at[h, here], p_sem.at[0, slot]),
            pltpu.make_async_copy(q_slot.at[slot], q_all.at[h, here], p_sem.at[1, slot]),
        ]

    @pl.when(at.works)
    def _():
        @pl.loop(0, planes)
        def _(k):
            src = arrived(k, *f_args)
            here = sub_rows(src, rows)
            value = feat_all[here, :]
            for h in range(heads):
                part = slice(h * head, (h + 1) * head)
                hid[here, part] = dot(value, wp[:, part]).astype(BF16)
                pre[here, part] = dot(value, ws[:, part])
            made = hid[here, :]
            dcol[here, 0:16] = dot(made, att_rows[...], (1, 1)) * LOG2E
            srow[:, here] = dot(att_rows[...], made, (1, 1)) * LOG2E

        @pl.loop(0, planes)
        def _(k):
            src = arrived(k, *a_args)
            here = sub_rows(src, rows)
            for h in range(heads):
                part = slice(h * head, (h + 1) * head)
                slot = h % depth

                @pl.when((k > 0) | (h >= depth))
                def _():
                    for copy in keep(h, here):
                        copy.wait()

                @pl.loop(0, rows // tall)
                def _(t):
                    first = src * rows + t * tall
                    there = pl.ds(pl.multiple_of(first, tall), tall)
                    inside = sub_rows(t, tall)
                    masked = mask_all[there, :].astype(F32) + srow[h : h + 1, :]
                    dst = dcol[there, heads + h : heads + h + 1]

                    def leaky(raw):
                        small = jnp.exp2(-jnp.abs(raw))
                        soft = jnp.log(1.0 + small)
                        return soft + jnp.maximum(raw * (1.25 * LN2), raw * (0.25 * LN2)), soft

                    peak, _ = leaky(jnp.max(masked, axis=1, keepdims=True) + dst)
                    raw = masked + dst
                    logit, soft = leaky(raw)
                    weight = jnp.exp2((logit - peak) * (0.8 * LOG2E))
                    total = jnp.sum(weight, axis=1, keepdims=True)
                    share = weight * (live_of(first, tall) / total)
                    slope = jnp.exp2(jnp.minimum(raw, 0.0) - soft * LOG2E) * 0.8 + 0.2
                    sloped = share * slope
                    p_slot[slot, inside, :] = share.astype(BF16)
                    q_slot[slot, inside, :] = sloped.astype(BF16)
                    middle = jnp.sum(sloped, axis=1, keepdims=True)
                    centered[inside, :] = (sloped - middle * share).astype(BF16)

                for copy in keep(h, here):
                    copy.start()
                mixed = dot(p_slot[slot], hid[:, part])
                mix[here, part] = mixed.astype(BF16)
                pre[here, part] += mixed + bias[:, part]
                diff[here, part] = dot(centered[...], hid[:, part]).astype(BF16)

    zero = jnp.zeros((8, width), F32)
    tiles = nodes // tile

    def fold(value):
        return sum(value[8 * i : 8 * i + 8] for i in range(tile // 8))

    def total_of(value):
        return jnp.sum(value, axis=0, keepdims=True)

    @pl.when(at.works)
    def _():
        def add_act(t, total):
            here = sub_rows(t, tile)
            value = pre[here, :]
            act = jnp.where(value > 0, value, jnp.exp(jnp.minimum(value, 0.0)) - 1.0)
            pre[here, :] = act
            return total + fold(act * live_of(t * tile, tile))

        number = jnp.maximum(live_count, 1).astype(F32)
        mean = total_of(lax.fori_loop(0, tiles, add_act, zero)) / number

        def add_square(t, total):
            off = pre[sub_rows(t, tile), :] - mean
            return total + fold(off * off * live_of(t * tile, tile))

        square = total_of(lax.fori_loop(0, tiles, add_square, zero))
        for k in range(planes):
            arrived(jnp.int32(k), *c_args)

        def add_grad(t, totals):
            here = sub_rows(t, tile)
            grad = low[here, :].astype(F32) * live_of(t * tile, tile)
            return totals[0] + fold(grad), totals[1] + fold(grad * (pre[here, :] - mean))

        plain, along = lax.fori_loop(0, tiles, add_grad, (zero, zero))
        stat[0:1, :] = jnp.full((1, width), live_count.astype(F32))
        stat[1:2, :] = mean
        stat[2:3, :] = square
        stat[3:4, :] = total_of(plain)
        stat[4:5, :] = total_of(along)
        stat[5:8, :] = jnp.zeros((3, width), F32)

    @pl.when(jnp.logical_not(at.works))
    def _():
        stat[...] = zero

    def exchange(which, size, me, held, send, recv, device):
        copies = []
        for k in range(1, size):
            peer = lax.rem(me + k, size)
            copy = remote(
                stat, held.at[which, me], send.at[which, k], recv.at[which, me], device(peer)
            )
            copy.start()
            copies.append(copy)
        held[which, me] = stat[...]
        for k in range(1, size):
            peer = lax.rem(me + k, size)
            remote(
                stat, held.at[which, peer], send.at[which, k], recv.at[which, peer], device(peer)
            ).wait_recv()
        for copy in copies:
            copy.wait_send()

    def everywhere(which, combine):
        exchange(which, group, g, stats_a, sa_send, sa_recv, lambda peer: (peer, z))
        combine(stats_a.at[which], group)
        exchange(which, planes, z, stats_b, sb_send, sb_recv, lambda peer: (g, peer))
        combine(stats_b.at[which], planes)

    def spread_out(held, size):
        number = sum(held[i, 0:1, :] for i in range(size))
        mean = sum(held[i, 0:1, :] * held[i, 1:2, :] for i in range(size))
        mean = mean / jnp.maximum(number, 1.0)
        square, plain, along = zero[0:1], zero[0:1], zero[0:1]
        for i in range(size):
            off = held[i, 1:2, :] - mean
            square = square + held[i, 2:3, :] + held[i, 0:1, :] * off * off
            plain = plain + held[i, 3:4, :]
            along = along + held[i, 4:5, :] + held[i, 3:4, :] * off
        stat[0:1, :] = number
        stat[1:2, :] = mean
        stat[2:3, :] = square
        stat[3:4, :] = plain
        stat[4:5, :] = along

    def plain_sum(held, size):
        stat[...] = sum(held[i] for i in range(size))

    everywhere(0, spread_out)
    number, mean = stat[0:1, :], stat[1:2, :]
    inv_std = lax.rsqrt(stat[2:3, :] / number + EPSILON)

    def give(target, send, recv, to):
        return remote(
            stage.at[sub_rows(to, rows)],
            target.at[at.slot],
            send.at[to],
            recv.at[at.slot],
            (g, to),
        )

    norm_own = pltpu.make_async_copy(stage.at[block], out.at[at.slot], own_sem.at[3])
    ig_own = pltpu.make_async_copy(ig.at[block], ig_out.at[at.slot], own_sem.at[4])
    bit_rows = rows // ROUNDS

    def give_bit(r, to):
        first = to * rows + r * bit_rows
        return remote(
            ig.at[pl.ds(pl.multiple_of(first, bit_rows), bit_rows)],
            ig_out.at[at.slot, r * bit_rows : (r + 1) * bit_rows],
            i_send.at[to, r],
            i_recv.at[at.slot, r],
            (g, to),
        )

    shift_grad = stat[3:4, :]
    gain_grad = stat[4:5, :] * inv_std
    sums_out[0:1, :] = gain_grad
    sums_out[1:2, :] = shift_grad
    scale = gain[...] * inv_std
    shift_mean = shift_grad / number
    gain_mean = gain_grad / number
    stat[...] = zero

    @pl.when(at.works)
    def _():
        def finish(j, t, total):
            first = j * rows + t * tile
            here = pl.ds(pl.multiple_of(first, tile), tile)
            live = live_of(first, tile)
            act = pre[here, :]
            grown = jnp.minimum(act, 0.0) + 1.0
            normed = (act - mean) * inv_std
            stage[here, :] = ((gain[...] * normed + shift[...]) * live).astype(BF16)
            grad = low[here, :].astype(F32) * live
            grad = scale * (grad - shift_mean - normed * gain_mean) * live * grown
            grad_low = grad.astype(BF16)
            low[here, :] = grad_low
            grad_low = grad_low.astype(F32)
            lane = lax.broadcasted_iota(jnp.int32, (tile, 128), 1)
            along_mix = grad_low * mix[here, :].astype(F32)
            along_diff = grad_low * diff[here, :].astype(F32)
            spread = jnp.zeros((tile, 128), F32)
            for h in range(heads):
                part = slice(h * head, (h + 1) * head)
                one = jnp.sum(along_mix[:, part], axis=1, keepdims=True)
                spread = jnp.where(lane % heads == h, one, spread)
                dcol[here, h : h + 1] = jnp.sum(along_diff[:, part], axis=1, keepdims=True)
            top = spread.astype(BF16)
            rest = spread - top.astype(F32)
            middle = rest.astype(BF16)
            bottom = (rest - middle.astype(F32)).astype(BF16)
            third = lane // heads
            parts[here, :] = jnp.where(
                third == 0, top, jnp.where(third == 1, middle, jnp.where(third == 2, bottom, 0.0))
            ).astype(BF16)
            return total + fold(grad)

        def finish_block(k, total):
            j = lax.rem(z + 1 + k, planes)
            total = lax.fori_loop(0, rows // tile, functools.partial(finish, j), total)
            pl.when(j != z)(give(out, n_send, n_recv, j).start)
            pl.when(j == z)(norm_own.start)
            return total

        stat[0:1, :] = total_of(lax.fori_loop(0, planes, finish_block, zero))
        for h in range(depth):
            for copy in keep(h, block):
                copy.wait()

    chips = group // 2
    chip, core = g // 2, lax.rem(g, 2)
    partner = g + 1 - 2 * core
    half_width = width // 2
    quarter = half_width // 2
    strip = width_in // chips
    mine = pl.ds(pl.multiple_of(core * quarter, quarter), quarter)
    other = pl.ds(pl.multiple_of((1 - core) * quarter, quarter), quarter)
    lines = planes.bit_length() - 1
    regions = [(0, strip, 0, quarter)]
    sides = []
    for i in range(lines):
        top, high, left, across = regions[-1]
        bit = lax.rem(z // 2**i, 2)
        pair = []
        for b in (bit, 1 - bit):
            if high >= 32:
                pair.append((top + b * (high // 2), high // 2, left, across))
            else:
                pair.append((top, high, left + b * (across // 2), across // 2))
        regions.append(pair[0])
        sides.append((z + 2**i - 2 ** (i + 1) * bit, pair[0], pair[1]))

    def cut(region):
        top, high, left, across = region
        return (
            pl.ds(top if isinstance(top, int) else pl.multiple_of(top, high), high),
            pl.ds(left if isinstance(left, int) else pl.multiple_of(left, across), across),
        )

    def unit_of(u):
        kept = diff if u < 2 else mix
        return kept.at[0:width_in, u % 2 * half_width : (u % 2 + 1) * half_width]

    def strip_of(index):
        return pl.ds(pl.multiple_of(index * strip, strip), strip)

    def to_core(u):
        return remote(
            unit_of(u).at[:, other], swap.at[u], r_send.at[u, 0, 0], r_recv.at[u, 0, 0], (partner, z)
        )

    def to_chip(u, peer, landed):
        return remote(
            unit_of(u).at[strip_of(peer), mine],
            plane_in.at[u, landed],
            r_send.at[u, 1, peer],
            r_recv.at[u, 1, landed],
            (2 * peer + core, z),
        )

    def to_line(u, i):
        peer, kept, given = sides[i]
        landing = line_in.at[u, i, 0 : kept[1], 0 : kept[3]]
        return remote(
            line_out.at[u].at[cut(given)], landing, r_send.at[u, 2, i], r_recv.at[u, 2, i], (g, peer)
        )

    def from_line(u, i, landed=False):
        peer, kept, given = sides[i]
        where = swap.at[u].at[strip_of(chip)].at[cut(given if landed else kept)]
        return remote(where, where, r_send.at[u, 3, i], r_recv.at[u, 3, i], (g, peer))

    def from_chip(u, peer, landed):
        where = swap.at[u].at[strip_of(landed)]
        return remote(
            where, where, r_send.at[u, 4, peer], r_recv.at[u, 4, landed], (2 * peer + core, z)
        )

    def from_core(u, columns):
        return remote(
            swap.at[u],
            unit_of(u).at[:, columns],
            r_send.at[u, 5, 0],
            r_recv.at[u, 5, 0],
            (partner, z),
        )

    def others(size, me):
        return [lax.rem(me + k, size) for k in range(1, size)]

    last_step = 4 + 2 * lines

    def step(u, number):
        unit = unit_of(u)
        if number == 0:
            to_core(u).start()
        elif number == 1:
            to_core(u).wait()

            @pl.loop(0, width_in // tall)
            def _(t):
                here = sub_rows(t, tall)
                value = unit[here, mine].astype(F32) + swap[u, here, :].astype(F32)
                unit[here, mine] = value.astype(BF16)

            for peer in others(chips, chip):
                to_chip(u, peer, chip).start()
        elif number <= 2 + lines:
            i = number - 3
            if i < 0:
                for peer in others(chips, chip):
                    to_chip(u, peer, peer).wait_recv()
                value = unit[strip_of(chip), mine].astype(F32)
                for peer in others(chips, chip):
                    value = value + plane_in[u, peer].astype(F32)
                line_out[u] = value.astype(BF16)
            else:
                kept = sides[i][1]
                to_line(u, i).wait_recv()
                value = line_out.at[u][cut(kept)].astype(F32)
                value = value + line_in[u, i, 0 : kept[1], 0 : kept[3]].astype(F32)
                target = line_out.at[u] if i + 1 < lines else swap.at[u].at[strip_of(chip)]
                target[cut(kept)] = value.astype(BF16)
            if i + 1 < lines:
                to_line(u, i + 1).start()
            else:
                from_line(u, lines - 1).start()
            if i < 0:
                for peer in others(chips, chip):
                    to_chip(u, peer, chip).wait_send()
            else:
                to_line(u, i).wait_send()
        elif number <= 2 + 2 * lines:
            i = 2 + 2 * lines - number
            from_line(u, i, True).wait_recv()
            if i > 0:
                from_line(u, i - 1).start()
            else:
                for peer in others(chips, chip):
                    from_chip(u, peer, chip).start()
            from_line(u, i).wait_send()
        elif number < last_step:
            for peer in others(chips, chip):
                from_chip(u, peer, peer).wait_recv()
            from_core(u, mine).start()

            @pl.loop(0, width_in // tall)
            def _(t):
                here = sub_rows(t, tall)
                unit[here, mine] = swap[u, here, :]

            for peer in others(chips, chip):
                from_chip(u, peer, chip).wait_send()
        else:
            from_core(u, other).wait_recv()
            from_core(u, mine).wait_send()
            answer(u).start()

    def steps(*work):
        for u, number in work:
            step(u, number)

    def answer(u):
        target = skip_out if u < 2 else proj_out
        columns = slice(u % 2 * half_width, (u % 2 + 1) * half_width)
        return pltpu.make_async_copy(unit_of(u), target.at[:, columns], out_sem.at[u])

    def fetch(j, h):
        place = pl.ds(pl.multiple_of(j * rows, rows), rows)
        slot = h % 2
        return [
            pltpu.make_async_copy(p_all.at[h, :, place], p_back.at[slot], p_sem.at[2, slot]),
            pltpu.make_async_copy(q_all.at[h, :, place], q_back.at[slot], p_sem.at[3, slot]),
        ]

    def product(u, right):
        unit = unit_of(u)
        columns = slice(u % 2 * half_width, (u % 2 + 1) * half_width)

        @pl.when(at.works)
        def _():
            @pl.loop(0, width_in // head)
            def _(f):
                place = sub_rows(f, head)
                unit[place, :] = dot(feat_all[:, place], right[:, columns], (0, 0)).astype(BF16)

        @pl.when(jnp.logical_not(at.works))
        def _():
            unit[...] = jnp.zeros_like(unit)

    @pl.when(at.works)
    def _():
        for copy in fetch(lax.rem(z + 1, planes), 0):
            copy.start()

    for u in (0, 1):
        product(u, low)
        step(u, 0)

    def source_block(k, turn):
        j = lax.rem(z + 1 + k, planes)
        here = sub_rows(j, rows)
        per_turn = heads // 2
        for h in range(turn * per_turn, (turn + 1) * per_turn):
            part = slice(h * head, (h + 1) * head)
            slot = h % 2
            if h + 1 < (turn + 1) * per_turn:
                for copy in fetch(j, h + 1):
                    copy.start()
            else:

                @pl.when(k + 1 < planes)
                def _():
                    for copy in fetch(lax.rem(j + 1, planes), turn * per_turn):
                        copy.start()

                if turn == 0:

                    @pl.when(k + 1 == planes)
                    def _():
                        for copy in fetch(lax.rem(z + 1, planes), per_turn):
                            copy.start()

            for copy in fetch(j, h):
                copy.wait()
            grad = dot(p_back[slot], low[:, part], (0, 0))
            along = dot(q_back[slot], low[:, part], (0, 0))
            spread = dot(q_back[slot], parts[...], (0, 0))
            lane = lax.broadcasted_iota(jnp.int32, spread.shape, 1)
            chosen = (lane % heads == h) & (lane < 3 * heads)
            own = hid[here, part].astype(F32)
            by_src = jnp.sum(own * along, axis=1, keepdims=True) - jnp.sum(
                jnp.where(chosen, spread, 0.0), axis=1, keepdims=True
            )
            by_dst = dcol[here, h : h + 1]
            att_src, att_dst = (
                att_rows[i : i + 1, part].astype(F32) for i in (h, heads + h)
            )
            grad = grad + by_dst * att_dst + by_src * att_src
            back[here, part] = grad.astype(BF16)
            stat[1:2, part] += total_of(by_dst * own)
            stat[2:3, part] += total_of(by_src * own)

    def sent_norm(j):
        pl.when(j != z)(give(out, n_send, n_recv, j).wait_send)
        pl.when(j == z)(norm_own.wait)

    def input_block(k):
        j = lax.rem(z + 1 + k, planes)
        here = sub_rows(j, rows)
        if shared:
            sent_norm(j)
        for f in range(width_in // head):
            part = slice(f * head, (f + 1) * head)
            ig[here, part] = (
                dot(back[here, :], wp[part, :], (1, 1)) + dot(low[here, :], ws[part, :], (1, 1))
            ).astype(BF16)
        pl.when(j == z)(ig_own.start)

    def give_round(r):
        @pl.when(at.works)
        def _():
            for peer in others(planes, z):
                give_bit(r, peer).start()

    def walk(turn, *work):
        @pl.loop(0, planes)
        def _(k):
            pl.when(at.works)(functools.partial(source_block, k, turn))
            for when, todo in work:
                pl.when(k == when)(functools.partial(steps, *todo))

    walk(0, (0, ((0, 1), (1, 1))), (3, ((0, 2), (1, 2))))
    product(2, back)
    step(2, 0)
    walk(1, (0, ((2, 1),)), (3, ((2, 2),)))
    product(3, back)
    step(3, 0)

    @pl.when(at.works)
    def _():
        pl.loop(0, planes)(input_block)

    step(3, 1)
    give_round(0)
    exchange(1, group, g, stats_a, sa_send, sa_recv, lambda peer: (peer, z))
    plain_sum(stats_a.at[1], group)
    steps((0, 3), (1, 3))
    for number in range(2, last_step + 1):
        for u, ahead in ((3, 0), (2, 1), (0, 2), (1, 2)):
            if number + ahead <= last_step:
                step(u, number + ahead)
        if number - 1 < ROUNDS:
            give_round(number - 1)
    for r in range(last_step, ROUNDS):
        give_round(r)
    exchange(1, planes, z, stats_b, sb_send, sb_recv, lambda peer: (g, peer))
    plain_sum(stats_b.at[1], planes)
    sums_out[2:5, :] = stat[0:3, :]
    sums_out[5:8, :] = jnp.zeros((3, width), F32)

    for s in range(slots):

        @pl.when(jnp.logical_not(at.mine[s]))
        def _():
            landing = out.at[s]
            remote(landing, landing, n_send.at[0], n_recv.at[s], (g, at.owner(s))).wait_recv()
            for r in range(ROUNDS):
                landing = ig_out.at[s, r * bit_rows : (r + 1) * bit_rows]
                remote(landing, landing, i_send.at[0, r], i_recv.at[s, r], (g, at.owner(s))).wait_recv()

    @pl.when(at.works)
    def _():
        ig_own.wait()
        for peer in others(planes, z):
            for r in range(ROUNDS):
                give_bit(r, peer).wait_send()
        if not shared:
            for k in range(planes):
                sent_norm(lax.rem(z + k, planes))

    for u in range(4):
        answer(u).wait()
    sent(f_moves)
    sent(a_moves)
    sent(c_moves)


def shards(
    planes,
    group,
    features,
    adjacency,
    counts,
    proj_weight,
    skip_weight,
    attn_dst,
    attn_src,
    attn_bias,
    norm_gain,
    norm_shift,
    cotangent,
):
    slots, rows, width_in = features.shape
    nodes = adjacency.shape[2]
    heads, head = attn_dst.shape
    width = heads * head
    dims = (planes, group, slots, rows, nodes, heads, head, width_in)
    dma = pltpu.SemaphoreType.DMA
    chips = group // 2
    strip, quarter = width_in // chips, width // 4
    lines = planes.bit_length() - 1
    landing = (strip // 2, quarter) if strip >= 32 else (strip, quarter // 2)
    tallest = max(nodes, width_in)
    depth = 2 if nodes <= 1024 else 1

    shape = jax.ShapeDtypeStruct
    vmem = pltpu.VMEM
    square = shape((heads, nodes, nodes), BF16)
    output, input_grad, proj_grad, skip_grad, sums, _, _ = pl.pallas_call(
        functools.partial(layer_kernel, dims),
        out_shape=[
            shape((slots, rows, width), BF16),
            shape((slots, rows, width_in), BF16),
            shape((width_in, width), BF16),
            shape((width_in, width), BF16),
            shape((8, width), F32),
            square,
            square,
        ],
        in_specs=[ANY, ANY, ANY, SMEM, ANY, ANY, VMEM, VMEM, VMEM, VMEM, VMEM],
        out_specs=[ANY, ANY, ANY, ANY, VMEM, ANY, ANY],
        scratch_shapes=[
            vmem((16, width), BF16),
            vmem((nodes, width_in), BF16),
            vmem((nodes, width), BF16),
            vmem((nodes, max(nodes, (3 if nodes <= 1024 else 2) * width)), BF16),
            vmem((slots, rows, nodes), BF16),
            vmem((2, max(rows // 4, TILE), nodes), jnp.int32),
            vmem((width_in, width), BF16),
            vmem((width_in, width), BF16),
            vmem((nodes, width), F32),
            vmem((tallest, width), BF16),
            vmem((tallest, width), BF16),
            vmem((nodes, width), BF16),
            vmem((nodes, 128), F32),
            vmem((nodes, 128), BF16),
            vmem((16, nodes), F32),
            vmem((depth, rows, nodes), BF16),
            vmem((depth, rows, nodes), BF16),
            vmem((rows, nodes), BF16),
            vmem((2, nodes, rows), BF16),
            vmem((2, nodes, rows), BF16),
            vmem((8, width), F32),
            vmem((2, group, 8, width), F32),
            vmem((2, planes, 8, width), F32),
            vmem((4, width_in, quarter), BF16),
            vmem((4, chips, strip, quarter), BF16),
            vmem((4, lines) + landing, BF16),
            vmem((4, strip, quarter), BF16),
            dma((slots,)),
            dma((planes,)),
            dma((slots,)),
            dma((planes,)),
            dma((slots,)),
            dma((planes,)),
            dma((planes,)),
            dma((slots,)),
            dma((planes, ROUNDS)),
            dma((slots, ROUNDS)),
            dma((2, group)),
            dma((2, group)),
            dma((2, planes)),
            dma((2, planes)),
            dma((4, 6, max(chips, lines))),
            dma((4, 6, max(chips, lines))),
            dma((5,)),
            dma((2,)),
            dma((2,)),
            dma((4, 2)),
            dma((4,)),
        ],
        compiler_params=pltpu.CompilerParams(
            collective_id=0, has_side_effects=True, vmem_limit_bytes=63 * 2**20
        ),
    )(
        features,
        adjacency,
        cotangent,
        counts,
        proj_weight,
        skip_weight,
        attn_dst,
        attn_src,
        attn_bias.reshape(1, width),
        norm_gain.reshape(1, width),
        norm_shift.reshape(1, width),
    )
    return (
        output,
        input_grad,
        proj_grad.astype(F32),
        skip_grad.astype(F32),
        sums[3].reshape(heads, head),
        sums[4].reshape(heads, head),
        sums[2],
        sums[0],
        sums[1],
    )


def solution(mesh):
    placed = (
        P("graph", "row", None),
        P("graph", "row", None),
        P("graph"),
        P(),
        P(),
        P(),
        P(),
        P(),
        P(),
        P(),
        P("graph", "row", None),
    )
    return jax.shard_map(
        functools.partial(shards, mesh.shape["row"], mesh.shape["graph"]),
        mesh=mesh,
        in_specs=placed,
        out_specs=(
            P("graph", "row", None),
            P("graph", "row", None),
            P(),
            P(),
            P(),
            P(),
            P(),
            P(),
            P(),
        ),
        check_vma=False,
    )
```

```python
import functools

import jax
import jax.numpy as jnp
from jax import lax
from jax.experimental import pallas as pl
from jax.experimental.pallas import tpu as pltpu
from jax.sharding import PartitionSpec as P

EPSILON = 1e-05
MESH = pl.DeviceIdType.MESH
LOG2E = 1.4426950408889634
LN2 = 0.6931471805599453
MASKED = -1e30
TILE = 64
WIDE_TILE = 256
ROUNDS = 8
LOTS = 2
PACE = 3
BITS = 4
EARLY = (0, 2, 3, 4, 5)
F32 = jnp.float32
BF16 = jnp.bfloat16
ANY = pl.BlockSpec(memory_space=pl.ANY)
VMEM = pl.BlockSpec(memory_space=pltpu.VMEM)
SMEM = pl.BlockSpec(memory_space=pltpu.SMEM)


def dot(left, right, dims=(1, 0)):
    contract = (((dims[0],), (dims[1],)), ((), ()))
    return lax.dot_general(left, right, contract, preferred_element_type=F32)


class Place:
    def __init__(self, planes, slots, group):
        self.planes, self.slots, self.group = planes, slots, group
        self.g = lax.axis_index("graph")
        self.z = lax.axis_index("row")
        self.core = lax.rem(self.g, 2)
        turn = jnp.where(self.core == 1, self.z, planes - 1 - self.z)
        self.mine = [turn == self.turn(s) for s in range(slots)]
        self.slot = sum(jnp.where(own, s, 0) for s, own in enumerate(self.mine))
        self.works = functools.reduce(jnp.logical_or, self.mine)

    def turn(self, slot):
        return slot * self.planes // (self.slots + 1)

    def owner(self, slot):
        turn = self.turn(slot)
        return jnp.where(self.core == 1, turn, self.planes - 1 - turn)


def sub_rows(index, size):
    return pl.ds(pl.multiple_of(index * size, size), size)


def layer_kernel(
    dims,
    feat,
    adj,
    cot,
    counts,
    wp_in,
    ws_in,
    att_dst_in,
    att_src_in,
    bias,
    gain,
    shift,
    out,
    ig_out,
    proj_out,
    skip_out,
    sums_out,
    p_all,
    q_all,
    att_rows,
    feat_all,
    hid,
    wide,
    mask_own,
    adj_in,
    wp,
    ws,
    pre,
    mix,
    diff,
    low,
    dcol,
    parts,
    srow,
    p_slot,
    q_slot,
    centered,
    p_back,
    q_back,
    stat,
    stats_a,
    stats_b,
    swap_0,
    swap_1,
    swap_2,
    plane_0,
    plane_1,
    plane_2,
    line_in_0,
    line_in_1,
    line_in_2,
    line_out_0,
    line_out_1,
    line_out_2,
    f_send,
    f_recv,
    a_send,
    a_recv,
    c_send,
    c_recv,
    n_send,
    n_recv,
    i_send,
    i_recv,
    sa_send,
    sa_recv,
    sb_send,
    sb_recv,
    r_send,
    r_recv,
    lot_sem,
    own_sem,
    adj_sem,
    w_sem,
    p_sem,
    out_sem,
):
    planes, group, slots, rows, nodes, heads, head, width_in = dims
    width = heads * head
    tile = min(TILE, TILE * 1024 // nodes)
    tall = min(WIDE_TILE * 1024 // nodes * 1024 // nodes, rows)
    at = Place(planes, slots, group)
    g, z = at.g, at.z
    block = sub_rows(z, rows)
    resident = p_slot.shape[0] == heads
    mask_all = wide.at[:, 0:nodes]
    back = wide.at[:, 0:width]
    stage = wide.at[:, width : 2 * width]
    shared = wide.shape[1] < 3 * width
    ig = stage if shared else wide.at[:, 2 * width : 3 * width]

    barrier = pltpu.get_barrier_semaphore()
    for k in range(1, planes):
        pl.semaphore_signal(barrier, 1, device_id=(g, lax.rem(z + k, planes)), device_id_type=MESH)
    for k in range(1, group):
        pl.semaphore_signal(barrier, 1, device_id=(lax.rem(g + k, group), z), device_id_type=MESH)
    load_wp = pltpu.make_async_copy(wp_in, wp, w_sem.at[0])
    load_ws = pltpu.make_async_copy(ws_in, ws, w_sem.at[1])
    some = adj_in.shape[1]
    cuts = rows // some
    loads = [
        pltpu.make_async_copy(
            adj.at[i // cuts, pl.ds(i % cuts * some, some)], adj_in.at[i % 2], adj_sem.at[i % 2]
        )
        for i in range(cuts * slots)
    ]
    loads[0].start()
    loads[1].start()
    load_wp.start()
    load_ws.start()
    pl.semaphore_wait(barrier, planes - 1 + group - 1)

    def remote(source, target, send, recv, device):
        return pltpu.make_async_remote_copy(
            src_ref=source,
            dst_ref=target,
            send_sem=send,
            recv_sem=recv,
            device_id=device,
            device_id_type=MESH,
        )

    lot_rows = rows // LOTS

    def lot_of(source, target, s, src, lot):
        first = src * rows + lot * lot_rows
        return (
            source.at[s, lot * lot_rows : (lot + 1) * lot_rows],
            target.at[pl.ds(pl.multiple_of(first, lot_rows), lot_rows)],
        )

    def moves(source, target, send, recv, own):
        found = []
        for lot in range(LOTS):
            for s in range(slots):
                to = at.owner(s)
                here, there = lot_of(source, target, s, z, lot)
                away = remote(here, there, send.at[s, lot], recv.at[z, lot], (g, to))
                local = pltpu.make_async_copy(here, there, own.at[lot])
                found.append((to, away, local, lot))
        return found

    def start(copies):
        for lot in range(LOTS):
            for far in range(1, planes):
                for to, away, _, part in copies:
                    if part == lot:
                        pl.when(jnp.abs(to - z) == far)(away.start)
        for to, _, local, _ in copies:
            pl.when(to == z)(local.start)

    def sent(copies):
        for to, away, _, _ in copies:
            pl.when(to != z)(away.wait_send)

    def arrived(k, source, target, send, recv, own):
        src = lax.rem(z + k, planes)
        for lot in range(LOTS):
            here, there = lot_of(source, target, 0, src, lot)
            pl.when(k == 0)(pltpu.make_async_copy(here, there, own.at[lot]).wait)
            pl.when(k != 0)(
                remote(here, there, send.at[0, lot], recv.at[src, lot], (g, src)).wait_recv
            )
        return src

    f_args = (feat, feat_all, f_send, f_recv, lot_sem.at[0])
    a_args = (mask_own, mask_all, a_send, a_recv, lot_sem.at[1])
    c_args = (cot, low, c_send, c_recv, lot_sem.at[2])
    f_moves, a_moves, c_moves = moves(*f_args), moves(*a_args), moves(*c_args)
    start(f_moves)

    for i, load in enumerate(loads):
        load.wait()
        live_own = counts[i // cuts]

        @pl.loop(0, some // tile)
        def _(t):
            first = i % cuts * some + t * tile
            shape = (tile, nodes)
            row = lax.broadcasted_iota(jnp.int32, shape, 0) + (z * rows + first)
            col = lax.broadcasted_iota(jnp.int32, shape, 1)
            allowed = (adj_in[i % 2, sub_rows(t, tile), :] > 0) | (row == col)
            allowed = allowed & (row < live_own) & (col < live_own)
            mask_own[i // cuts, pl.ds(pl.multiple_of(first, tile), tile), :] = jnp.where(
                allowed, 0.0, MASKED
            ).astype(BF16)

        if i + 2 < len(loads):
            loads[i + 2].start()

    row = lax.broadcasted_iota(jnp.int32, (16, head), 0)
    for h in range(heads):
        src_row, dst_row = (
            kept[h : h + 1, :].astype(F32) for kept in (att_src_in, att_dst_in)
        )
        value = jnp.where(row == h, src_row, jnp.where(row == heads + h, dst_row, 0.0))
        att_rows[:, h * head : (h + 1) * head] = value.astype(BF16)

    load_wp.wait()
    load_ws.wait()
    start(a_moves)
    start(c_moves)
    live_count = counts[at.slot]

    def live_of(first, size):
        node = lax.broadcasted_iota(jnp.int32, (size, 1), 0) + first
        return (node < live_count).astype(F32)

    depth = p_slot.shape[0]

    def keep(h, here):
        if resident:
            return []
        slot = h % depth
        return [
            pltpu.make_async_copy(p_slot.at[slot], p_all.at[h, here], p_sem.at[0, slot]),
            pltpu.make_async_copy(q_slot.at[slot], q_all.at[h, here], p_sem.at[1, slot]),
        ]

    @pl.when(at.works)
    def _():
        @pl.loop(0, planes)
        def _(k):
            src = arrived(k, *f_args)
            here = sub_rows(src, rows)
            value = feat_all[here, :]
            for h in range(heads):
                part = slice(h * head, (h + 1) * head)
                hid[here, part] = dot(value, wp[:, part]).astype(BF16)
                pre[here, part] = dot(value, ws[:, part])
            made = hid[here, :]
            dcol[here, 0:16] = dot(made, att_rows[...], (1, 1)) * LOG2E
            srow[:, here] = dot(att_rows[...], made, (1, 1)) * LOG2E

        @pl.loop(0, planes)
        def _(k):
            src = arrived(k, *a_args)
            here = sub_rows(src, rows)
            for h in range(heads):
                part = slice(h * head, (h + 1) * head)
                slot = h if resident else h % depth
                base = src * rows if resident else 0

                if not resident:

                    @pl.when((k > 0) | (h >= depth))
                    def _():
                        for copy in keep(h, here):
                            copy.wait()

                @pl.loop(0, rows // tall)
                def _(t):
                    first = src * rows + t * tall
                    there = pl.ds(pl.multiple_of(first, tall), tall)
                    inside = pl.ds(pl.multiple_of(base + t * tall, tall), tall)
                    masked = mask_all[there, :].astype(F32) + srow[h : h + 1, :]
                    dst = dcol[there, heads + h : heads + h + 1]

                    def leaky(raw):
                        small = jnp.exp2(-jnp.abs(raw))
                        soft = jnp.log(1.0 + small)
                        return soft + jnp.maximum(raw * (1.25 * LN2), raw * (0.25 * LN2)), soft

                    peak, _ = leaky(jnp.max(masked, axis=1, keepdims=True) + dst)
                    raw = masked + dst
                    logit, soft = leaky(raw)
                    weight = jnp.exp2((logit - peak) * (0.8 * LOG2E))
                    total = jnp.sum(weight, axis=1, keepdims=True)
                    share = weight * (live_of(first, tall) / total)
                    slope = jnp.exp2(jnp.minimum(raw, 0.0) - soft * LOG2E) * 0.8 + 0.2
                    sloped = share * slope
                    p_slot[slot, inside, :] = share.astype(BF16)
                    q_slot[slot, inside, :] = sloped.astype(BF16)
                    middle = jnp.sum(sloped, axis=1, keepdims=True)
                    centered[sub_rows(t, tall), :] = (sloped - middle * share).astype(BF16)

                for copy in keep(h, here):
                    copy.start()
                mixed = dot(p_slot[slot, sub_rows(src, rows) if resident else slice(None), :], hid[:, part])
                mix[here, part] = mixed.astype(BF16)
                pre[here, part] += mixed + bias[:, part]
                diff[here, part] = dot(centered[...], hid[:, part]).astype(BF16)

    zero = jnp.zeros((8, width), F32)
    tiles = nodes // tile

    def fold(value):
        return sum(value[8 * i : 8 * i + 8] for i in range(tile // 8))

    def total_of(value):
        return jnp.sum(value, axis=0, keepdims=True)

    @pl.when(at.works)
    def _():
        def add_act(t, total):
            here = sub_rows(t, tile)
            value = pre[here, :]
            act = jnp.where(value > 0, value, jnp.exp(jnp.minimum(value, 0.0)) - 1.0)
            pre[here, :] = act
            return total + fold(act * live_of(t * tile, tile))

        number = jnp.maximum(live_count, 1).astype(F32)
        mean = total_of(lax.fori_loop(0, tiles, add_act, zero)) / number

        def add_square(t, total):
            off = pre[sub_rows(t, tile), :] - mean
            return total + fold(off * off * live_of(t * tile, tile))

        square = total_of(lax.fori_loop(0, tiles, add_square, zero))
        for k in range(planes):
            arrived(jnp.int32(k), *c_args)

        def add_grad(t, totals):
            here = sub_rows(t, tile)
            grad = low[here, :].astype(F32) * live_of(t * tile, tile)
            return totals[0] + fold(grad), totals[1] + fold(grad * (pre[here, :] - mean))

        plain, along = lax.fori_loop(0, tiles, add_grad, (zero, zero))
        stat[0:1, :] = jnp.full((1, width), live_count.astype(F32))
        stat[1:2, :] = mean
        stat[2:3, :] = square
        stat[3:4, :] = total_of(plain)
        stat[4:5, :] = total_of(along)
        stat[5:8, :] = jnp.zeros((3, width), F32)

    @pl.when(jnp.logical_not(at.works))
    def _():
        stat[...] = zero

    def exchange(which, size, me, held, send, recv, device):
        copies = []
        for k in range(1, size):
            peer = lax.rem(me + k, size)
            copy = remote(
                stat, held.at[which, me], send.at[which, k], recv.at[which, me], device(peer)
            )
            copy.start()
            copies.append(copy)
        held[which, me] = stat[...]
        for k in range(1, size):
            peer = lax.rem(me + k, size)
            remote(
                stat, held.at[which, peer], send.at[which, k], recv.at[which, peer], device(peer)
            ).wait_recv()
        for copy in copies:
            copy.wait_send()

    def everywhere(which, combine):
        exchange(which, group, g, stats_a, sa_send, sa_recv, lambda peer: (peer, z))
        combine(stats_a.at[which], group)
        exchange(which, planes, z, stats_b, sb_send, sb_recv, lambda peer: (g, peer))
        combine(stats_b.at[which], planes)

    def spread_out(held, size):
        number = sum(held[i, 0:1, :] for i in range(size))
        mean = sum(held[i, 0:1, :] * held[i, 1:2, :] for i in range(size))
        mean = mean / jnp.maximum(number, 1.0)
        square, plain, along = zero[0:1], zero[0:1], zero[0:1]
        for i in range(size):
            off = held[i, 1:2, :] - mean
            square = square + held[i, 2:3, :] + held[i, 0:1, :] * off * off
            plain = plain + held[i, 3:4, :]
            along = along + held[i, 4:5, :] + held[i, 3:4, :] * off
        stat[0:1, :] = number
        stat[1:2, :] = mean
        stat[2:3, :] = square
        stat[3:4, :] = plain
        stat[4:5, :] = along

    def plain_sum(held, size):
        stat[...] = sum(held[i] for i in range(size))

    everywhere(0, spread_out)
    number, mean = stat[0:1, :], stat[1:2, :]
    inv_std = lax.rsqrt(stat[2:3, :] / number + EPSILON)

    tile_rows = rows // BITS

    def give_norm(r, to):
        first = to * rows + r * tile_rows
        return remote(
            stage.at[pl.ds(pl.multiple_of(first, tile_rows), tile_rows)],
            out.at[at.slot, r * tile_rows : (r + 1) * tile_rows],
            n_send.at[to, r],
            n_recv.at[at.slot, r],
            (g, to),
        )

    def give_norms(first, last):
        @pl.when(at.works)
        def _():
            for p in range(first, min(last, BITS * (planes - 1))):
                r, k = p // (planes - 1), p % (planes - 1)
                give_norm(r, lax.rem(z + 1 + k, planes)).start()

    norm_own = pltpu.make_async_copy(stage.at[block], out.at[at.slot], own_sem.at[3])
    ig_own = pltpu.make_async_copy(ig.at[block], ig_out.at[at.slot], own_sem.at[4])
    bit_rows = rows // ROUNDS

    def give_bit(r, to):
        first = to * rows + r * bit_rows
        return remote(
            ig.at[pl.ds(pl.multiple_of(first, bit_rows), bit_rows)],
            ig_out.at[at.slot, r * bit_rows : (r + 1) * bit_rows],
            i_send.at[to, r],
            i_recv.at[at.slot, r],
            (g, to),
        )

    shift_grad = stat[3:4, :]
    gain_grad = stat[4:5, :] * inv_std
    sums_out[0:1, :] = gain_grad
    sums_out[1:2, :] = shift_grad
    scale = gain[...] * inv_std
    shift_mean = shift_grad / number
    gain_mean = gain_grad / number
    stat[...] = zero

    @pl.when(at.works)
    def _():
        def finish(r, t, total):
            cut_rows = tile_rows // tile
            j = lax.rem(z + 1 + t // cut_rows, planes)
            first = j * rows + r * tile_rows + lax.rem(t, cut_rows) * tile
            here = pl.ds(pl.multiple_of(first, tile), tile)
            live = live_of(first, tile)
            act = pre[here, :]
            grown = jnp.minimum(act, 0.0) + 1.0
            normed = (act - mean) * inv_std
            stage[here, :] = ((gain[...] * normed + shift[...]) * live).astype(BF16)
            grad = low[here, :].astype(F32) * live
            grad = scale * (grad - shift_mean - normed * gain_mean) * live * grown
            grad_low = grad.astype(BF16)
            low[here, :] = grad_low
            grad_low = grad_low.astype(F32)
            lane = lax.broadcasted_iota(jnp.int32, (tile, 128), 1)
            along_mix = grad_low * mix[here, :].astype(F32)
            along_diff = grad_low * diff[here, :].astype(F32)
            spread = jnp.zeros((tile, 128), F32)
            for h in range(heads):
                part = slice(h * head, (h + 1) * head)
                one = jnp.sum(along_mix[:, part], axis=1, keepdims=True)
                spread = jnp.where(lane % heads == h, one, spread)
                dcol[here, h : h + 1] = jnp.sum(along_diff[:, part], axis=1, keepdims=True)
            top = spread.astype(BF16)
            rest = spread - top.astype(F32)
            middle = rest.astype(BF16)
            bottom = (rest - middle.astype(F32)).astype(BF16)
            third = lane // heads
            parts[here, :] = jnp.where(
                third == 0, top, jnp.where(third == 1, middle, jnp.where(third == 2, bottom, 0.0))
            ).astype(BF16)
            return total + fold(grad)

        total = zero
        for r in range(BITS):
            total = lax.fori_loop(
                0, planes * tile_rows // tile, functools.partial(finish, r), total
            )
            for p in range(EARLY[r], EARLY[r + 1]):
                give_norm(p // (planes - 1), lax.rem(z + 1 + p % (planes - 1), planes)).start()
        norm_own.start()
        stat[0:1, :] = total_of(total)
        for h in range(depth):
            for copy in keep(h, block):
                copy.wait()

    chips = group // 2
    chip, core = g // 2, lax.rem(g, 2)
    partner = g + 1 - 2 * core
    swaps, plane_ins = (swap_0, swap_1, swap_2), (plane_0, plane_1, plane_2)
    line_ins, line_outs = (line_in_0, line_in_1, line_in_2), (line_out_0, line_out_1, line_out_2)
    spans = ((0, width), (0, width // 2), (width // 2, width))
    strip = width_in // chips

    def share(u, which):
        size = (spans[u][1] - spans[u][0]) // 2
        return pl.ds(pl.multiple_of(which * size, size), size)

    lines = planes.bit_length() - 1
    regions = [(0, strip, 0, 2)]
    sides = []
    for i in range(lines):
        top, high, left, across = regions[-1]
        bit = lax.rem(z // 2**i, 2)
        pair = []
        for b in (bit, 1 - bit):
            if high >= 32:
                pair.append((top + b * (high // 2), high // 2, left, across))
            else:
                pair.append((top, high, left + b * (across // 2), across // 2))
        regions.append(pair[0])
        sides.append((z + 2**i - 2 ** (i + 1) * bit, pair[0], pair[1]))

    def cut(u, region):
        top, high, left, across = region
        size = (spans[u][1] - spans[u][0]) // 4
        left, across = left * size, across * size
        return (
            pl.ds(top if isinstance(top, int) else pl.multiple_of(top, high), high),
            pl.ds(left if isinstance(left, int) else pl.multiple_of(left, across), across),
        )

    def unit_of(u):
        kept = mix if u else diff
        return kept.at[0:width_in, spans[u][0] : spans[u][1]]

    def strip_of(index):
        return pl.ds(pl.multiple_of(index * strip, strip), strip)

    def to_core(u):
        return remote(
            unit_of(u).at[:, share(u, 1 - core)], swaps[u], r_send.at[u, 0, 0], r_recv.at[u, 0, 0], (partner, z)
        )

    def to_chip(u, peer, landed):
        return remote(
            unit_of(u).at[strip_of(peer), share(u, core)],
            plane_ins[u].at[landed],
            r_send.at[u, 1, peer],
            r_recv.at[u, 1, landed],
            (2 * peer + core, z),
        )

    def landed_at(u, i):
        _, high, _, across = sides[i][1]
        return line_ins[u].at[i, 0:high, 0 : across * (spans[u][1] - spans[u][0]) // 4]

    def to_line(u, i):
        peer, kept, given = sides[i]
        return remote(
            line_outs[u].at[cut(u, given)], landed_at(u, i), r_send.at[u, 2, i], r_recv.at[u, 2, i], (g, peer)
        )

    def from_line(u, i, landed=False):
        peer, kept, given = sides[i]
        where = swaps[u].at[strip_of(chip)].at[cut(u, given if landed else kept)]
        return remote(where, where, r_send.at[u, 3, i], r_recv.at[u, 3, i], (g, peer))

    def from_chip(u, peer, landed):
        where = swaps[u].at[strip_of(landed)]
        return remote(
            where, where, r_send.at[u, 4, peer], r_recv.at[u, 4, landed], (2 * peer + core, z)
        )

    def from_core(u, which):
        return remote(
            swaps[u],
            unit_of(u).at[:, share(u, which)],
            r_send.at[u, 5, 0],
            r_recv.at[u, 5, 0],
            (partner, z),
        )

    def others(size, me):
        return [lax.rem(me + k, size) for k in range(1, size)]

    last_step = 4 + 2 * lines

    def step(u, number):
        unit, own = unit_of(u), share(u, core)
        if number == 0:
            to_core(u).start()
        elif number == 1:
            to_core(u).wait()

            @pl.loop(0, width_in // tall)
            def _(t):
                here = sub_rows(t, tall)
                value = unit[here, own].astype(F32) + swaps[u][here, :].astype(F32)
                unit[here, own] = value.astype(BF16)

            for peer in others(chips, chip):
                to_chip(u, peer, chip).start()
        elif number <= 2 + lines:
            i = number - 3
            if i < 0:
                for peer in others(chips, chip):
                    to_chip(u, peer, peer).wait_recv()
                value = unit[strip_of(chip), own].astype(F32)
                for peer in others(chips, chip):
                    value = value + plane_ins[u][peer].astype(F32)
                line_outs[u][...] = value.astype(BF16)
            else:
                kept = sides[i][1]
                to_line(u, i).wait_recv()
                value = line_outs[u][cut(u, kept)].astype(F32)
                value = value + landed_at(u, i)[...].astype(F32)
                target = line_outs[u] if i + 1 < lines else swaps[u].at[strip_of(chip)]
                target[cut(u, kept)] = value.astype(BF16)
            if i + 1 < lines:
                to_line(u, i + 1).start()
            else:
                from_line(u, lines - 1).start()
            if i < 0:
                for peer in others(chips, chip):
                    to_chip(u, peer, chip).wait_send()
            else:
                to_line(u, i).wait_send()
        elif number <= 2 + 2 * lines:
            i = 2 + 2 * lines - number
            from_line(u, i, True).wait_recv()
            if i > 0:
                from_line(u, i - 1).start()
            else:
                for peer in others(chips, chip):
                    from_chip(u, peer, chip).start()
            from_line(u, i).wait_send()
        elif number < last_step:
            for peer in others(chips, chip):
                from_chip(u, peer, peer).wait_recv()
            from_core(u, core).start()

            @pl.loop(0, width_in // tall)
            def _(t):
                here = sub_rows(t, tall)
                unit[here, own] = swaps[u][here, :]

            for peer in others(chips, chip):
                from_chip(u, peer, chip).wait_send()
        else:
            from_core(u, 1 - core).wait_recv()
            from_core(u, core).wait_send()
            answer(u).start()

    def steps(*work):
        for u, number in work:
            step(u, number)

    def answer(u):
        target = proj_out if u else skip_out
        return pltpu.make_async_copy(unit_of(u), target.at[:, slice(*spans[u])], out_sem.at[u])

    def fetch(j, h):
        if resident:
            return []
        place = pl.ds(pl.multiple_of(j * rows, rows), rows)
        slot = h % 2
        return [
            pltpu.make_async_copy(p_all.at[h, :, place], p_back.at[slot], p_sem.at[2, slot]),
            pltpu.make_async_copy(q_all.at[h, :, place], q_back.at[slot], p_sem.at[3, slot]),
        ]

    def product(u, right):
        unit = unit_of(u)
        columns = slice(*spans[u])

        @pl.when(at.works)
        def _():
            @pl.loop(0, width_in // head)
            def _(f):
                place = sub_rows(f, head)
                unit[place, :] = dot(feat_all[:, place], right[:, columns], (0, 0)).astype(BF16)

        @pl.when(jnp.logical_not(at.works))
        def _():
            unit[...] = jnp.zeros_like(unit)

    @pl.when(at.works)
    def _():
        for copy in fetch(lax.rem(z + 1, planes), 0):
            copy.start()

    product(0, low)
    step(0, 0)

    def source_block(k, turn):
        j = lax.rem(z + 1 + k, planes)
        here = sub_rows(j, rows)
        per_turn = heads // 2
        for h in range(turn * per_turn, (turn + 1) * per_turn):
            part = slice(h * head, (h + 1) * head)
            slot = h % 2
            if h + 1 < (turn + 1) * per_turn:
                for copy in fetch(j, h + 1):
                    copy.start()
            else:

                @pl.when(k + 1 < planes)
                def _():
                    for copy in fetch(lax.rem(j + 1, planes), turn * per_turn):
                        copy.start()

                if turn == 0:

                    @pl.when(k + 1 == planes)
                    def _():
                        for copy in fetch(lax.rem(z + 1, planes), per_turn):
                            copy.start()

            for copy in fetch(j, h):
                copy.wait()
            if resident:
                p_now, q_now = p_slot[h, :, sub_rows(j, rows)], q_slot[h, :, sub_rows(j, rows)]
            else:
                p_now, q_now = p_back[slot], q_back[slot]
            grad = dot(p_now, low[:, part], (0, 0))
            along = dot(q_now, low[:, part], (0, 0))
            spread = dot(q_now, parts[...], (0, 0))
            lane = lax.broadcasted_iota(jnp.int32, spread.shape, 1)
            chosen = (lane % heads == h) & (lane < 3 * heads)
            own = hid[here, part].astype(F32)
            by_src = jnp.sum(own * along, axis=1, keepdims=True) - jnp.sum(
                jnp.where(chosen, spread, 0.0), axis=1, keepdims=True
            )
            by_dst = dcol[here, h : h + 1]
            att_src, att_dst = (
                att_rows[i : i + 1, part].astype(F32) for i in (h, heads + h)
            )
            grad = grad + by_dst * att_dst + by_src * att_src
            back[here, part] = grad.astype(BF16)
            stat[1:2, part] += total_of(by_dst * own)
            stat[2:3, part] += total_of(by_src * own)

    def sent_norm(j):
        @pl.when(j != z)
        def _():
            for r in range(BITS):
                give_norm(r, j).wait_send()

        pl.when(j == z)(norm_own.wait)

    def input_block(k):
        j = lax.rem(z + 1 + k, planes)
        here = sub_rows(j, rows)
        if shared:
            sent_norm(j)
        for f in range(width_in // head):
            part = slice(f * head, (f + 1) * head)
            ig[here, part] = (
                dot(back[here, :], wp[part, :], (1, 1)) + dot(low[here, :], ws[part, :], (1, 1))
            ).astype(BF16)
        pl.when(j == z)(ig_own.start)

    def give_bits(first, last):
        @pl.when(at.works)
        def _():
            for p in range(first, min(last, ROUNDS * (planes - 1))):
                give_bit(p % ROUNDS, lax.rem(z + 1 + p // ROUNDS, planes)).start()

    def S(u, number):
        return lambda: step(u, number) if number <= last_step else None

    def N(first, last):
        return lambda: give_norms(first, last)

    def R(first, last):
        return lambda: give_bits(first, last)

    def do(*work):
        for one in work:
            one()

    def walk(turn, **work):
        @pl.loop(0, planes)
        def _(k):
            pl.when(at.works)(functools.partial(source_block, k, turn))
            for when, todo in work.items():
                pl.when(k == int(when[1:]))(functools.partial(do, *todo))

    def input_of(k):
        pl.when(at.works)(functools.partial(input_block, k))

    def I(k):
        return lambda: input_of(k)

    last = BITS * (planes - 1)
    do(N(5, 7))
    walk(0, k0=(S(0, 1),), k1=(N(7, 8),), k3=(N(8, 9),))
    product(1, back)
    do(S(1, 0), N(9, 10))
    walk(1, k0=(S(1, 1), N(10, 11)), k1=(I(0), N(11, last)), k3=(S(0, 2), R(0, 0)))
    product(2, back)
    do(S(2, 0), R(0, 0), I(1), S(2, 1), S(0, 3), I(2), S(1, 2), R(0, 6))
    for k in range(3, planes):
        input_of(k)
    exchange(1, group, g, stats_a, sa_send, sa_recv, lambda peer: (peer, z))
    plain_sum(stats_a.at[1], group)
    done, given = [3, 2, 1], 6
    for number in range(2, last_step + 1):
        for u, target in ((2, number), (1, number + 1), (0, number + 2)):
            while done[u] < min(target, last_step):
                done[u] += 1
                step(u, done[u])
        give_bits(given, given + PACE)
        given += PACE
    give_bits(given, ROUNDS * (planes - 1))
    exchange(1, planes, z, stats_b, sb_send, sb_recv, lambda peer: (g, peer))
    plain_sum(stats_b.at[1], planes)
    sums_out[2:5, :] = stat[0:3, :]
    sums_out[5:8, :] = jnp.zeros((3, width), F32)

    for s in range(slots):

        @pl.when(jnp.logical_not(at.mine[s]))
        def _():
            for r in range(BITS):
                landing = out.at[s, r * tile_rows : (r + 1) * tile_rows]
                remote(landing, landing, n_send.at[0, r], n_recv.at[s, r], (g, at.owner(s))).wait_recv()
            for r in range(ROUNDS):
                landing = ig_out.at[s, r * bit_rows : (r + 1) * bit_rows]
                remote(landing, landing, i_send.at[0, r], i_recv.at[s, r], (g, at.owner(s))).wait_recv()

    @pl.when(at.works)
    def _():
        ig_own.wait()
        for peer in others(planes, z):
            for r in range(ROUNDS):
                give_bit(r, peer).wait_send()
        if not shared:
            for k in range(planes):
                sent_norm(lax.rem(z + k, planes))

    for u in range(3):
        answer(u).wait()
    sent(f_moves)
    sent(a_moves)
    sent(c_moves)


def finish_kernel(
    out_in,
    ig_in,
    proj_in,
    skip_in,
    sums,
    out,
    ig,
    proj,
    skip,
    att_dst,
    att_src,
    bias,
    gain,
    shift,
    narrow,
    full,
    held,
    copy_sem,
    in_sem,
    wide_sem,
):
    heads, head = att_dst.shape
    passing = [
        (
            pltpu.make_async_copy(source.at[s], held.at[i, s], copy_sem.at[i, s]),
            pltpu.make_async_copy(held.at[i, s], target.at[s], copy_sem.at[i, s]),
        )
        for i, (source, target) in enumerate(((out_in, out), (ig_in, ig)))
        for s in range(out.shape[0])
    ]
    size = proj.shape[0] // 4
    lots = []
    for i, (source, target) in enumerate(((proj_in, proj), (skip_in, skip))):
        for k in range(4):
            rows = pl.ds(k * size, size)
            load = pltpu.make_async_copy(source.at[rows], narrow.at[i, rows], in_sem.at[i, k])
            store = pltpu.make_async_copy(full.at[i, rows], target.at[rows], wide_sem.at[i, k])
            lots.append((i, rows, load, store))
    for _, _, load, _ in lots:
        load.start()
    for load, _ in passing:
        load.start()
    for h in range(heads):
        part = slice(h * head, (h + 1) * head)
        att_dst[h : h + 1, :] = sums[3:4, part]
        att_src[h : h + 1, :] = sums[4:5, part]
    gain[...] = sums[0:1, :]
    shift[...] = sums[1:2, :]
    bias[...] = sums[2:3, :]
    for i, rows, load, store in lots:
        load.wait()
        full[i, rows, :] = narrow[i, rows, :].astype(F32)
        store.start()
    for load, store in passing:
        load.wait()
        store.start()
    for _, _, _, store in lots:
        store.wait()
    for _, store in passing:
        store.wait()


def shards(
    planes,
    group,
    features,
    adjacency,
    counts,
    proj_weight,
    skip_weight,
    attn_dst,
    attn_src,
    attn_bias,
    norm_gain,
    norm_shift,
    cotangent,
):
    slots, rows, width_in = features.shape
    nodes = adjacency.shape[2]
    heads, head = attn_dst.shape
    width = heads * head
    dims = (planes, group, slots, rows, nodes, heads, head, width_in)
    dma = pltpu.SemaphoreType.DMA
    chips = group // 2
    strip, shares = width_in // chips, (width // 2, width // 4, width // 4)
    lines = planes.bit_length() - 1
    tallest = max(nodes, width_in)
    resident = nodes <= 1024
    kept = (heads, nodes, nodes) if resident else (1, rows, nodes)

    shape = jax.ShapeDtypeStruct
    vmem = pltpu.VMEM
    square = shape((heads, 16, 128) if resident else (heads, nodes, nodes), BF16)
    output, input_grad, proj_grad, skip_grad, sums, _, _ = pl.pallas_call(
        functools.partial(layer_kernel, dims),
        out_shape=[
            shape((slots, rows, width), BF16),
            shape((slots, rows, width_in), BF16),
            shape((width_in, width), BF16),
            shape((width_in, width), BF16),
            shape((8, width), F32),
            square,
            square,
        ],
        in_specs=[ANY, ANY, ANY, SMEM, ANY, ANY, VMEM, VMEM, VMEM, VMEM, VMEM],
        out_specs=[ANY, ANY, ANY, ANY, VMEM, ANY, ANY],
        scratch_shapes=[
            vmem((16, width), BF16),
            vmem((nodes, width_in), BF16),
            vmem((nodes, width), BF16),
            vmem((nodes, max(nodes, (3 if nodes <= 1024 else 2) * width)), BF16),
            vmem((slots, rows, nodes), BF16),
            vmem((2, max(rows // 4, TILE), nodes), jnp.int32),
            vmem((width_in, width), BF16),
            vmem((width_in, width), BF16),
            vmem((nodes, width), F32),
            vmem((tallest, width), BF16),
            vmem((tallest, width), BF16),
            vmem((nodes, width), BF16),
            vmem((nodes, 128), F32),
            vmem((nodes, 128), BF16),
            vmem((16, nodes), F32),
            vmem(kept, BF16),
            vmem(kept, BF16),
            vmem((rows, nodes), BF16),
            vmem((1 if resident else 2, 16 if resident else nodes, rows), BF16),
            vmem((1 if resident else 2, 16 if resident else nodes, rows), BF16),
            vmem((8, width), F32),
            vmem((2, group, 8, width), F32),
            vmem((2, planes, 8, width), F32),
            *(vmem((width_in, one), BF16) for one in shares),
            *(vmem((chips, strip, one), BF16) for one in shares),
            *(vmem((lines, max(strip // 2, 16), one), BF16) for one in shares),
            *(vmem((strip, one), BF16) for one in shares),
            dma((slots, LOTS)),
            dma((planes, LOTS)),
            dma((slots, LOTS)),
            dma((planes, LOTS)),
            dma((slots, LOTS)),
            dma((planes, LOTS)),
            dma((planes, BITS)),
            dma((slots, BITS)),
            dma((planes, ROUNDS)),
            dma((slots, ROUNDS)),
            dma((2, group)),
            dma((2, group)),
            dma((2, planes)),
            dma((2, planes)),
            dma((3, 6, max(chips, lines))),
            dma((3, 6, max(chips, lines))),
            dma((3, LOTS)),
            dma((5,)),
            dma((2,)),
            dma((2,)),
            dma((4, 2)),
            dma((3,)),
        ],
        compiler_params=pltpu.CompilerParams(
            collective_id=0, has_side_effects=True, vmem_limit_bytes=63 * 2**20
        ),
    )(
        features,
        adjacency,
        cotangent,
        counts,
        proj_weight,
        skip_weight,
        attn_dst,
        attn_src,
        attn_bias.reshape(1, width),
        norm_gain.reshape(1, width),
        norm_shift.reshape(1, width),
    )
    line = shape((1, width), F32)
    weight, att = shape((width_in, width), F32), shape((heads, head), F32)
    output, input_grad, proj_grad, skip_grad, dst_grad, src_grad, bias, gain, shift = pl.pallas_call(
        finish_kernel,
        out_shape=[
            shape(output.shape, BF16),
            shape(input_grad.shape, BF16),
            weight,
            weight,
            att,
            att,
            line,
            line,
            line,
        ],
        in_specs=[ANY] * 4 + [VMEM],
        out_specs=[ANY] * 4 + [VMEM] * 5,
        scratch_shapes=[
            vmem((2, width_in, width), BF16),
            vmem((2, width_in, width), F32),
            vmem((2,) + output.shape, BF16),
            dma((2, slots)),
            dma((2, 4)),
            dma((2, 4)),
        ],
        compiler_params=pltpu.CompilerParams(vmem_limit_bytes=60 * 2**20),
    )(output, input_grad, proj_grad, skip_grad, sums)
    flat = (width,)
    return (
        output,
        input_grad,
        proj_grad,
        skip_grad,
        dst_grad,
        src_grad,
        bias.reshape(flat),
        gain.reshape(flat),
        shift.reshape(flat),
    )


def solution(mesh):
    placed = (
        P("graph", "row", None),
        P("graph", "row", None),
        P("graph"),
        P(),
        P(),
        P(),
        P(),
        P(),
        P(),
        P(),
        P("graph", "row", None),
    )
    return jax.shard_map(
        functools.partial(shards, mesh.shape["row"], mesh.shape["graph"]),
        mesh=mesh,
        in_specs=placed,
        out_specs=(
            P("graph", "row", None),
            P("graph", "row", None),
            P(),
            P(),
            P(),
            P(),
            P(),
            P(),
            P(),
        ),
        check_vma=False,
    )
```

```python
import functools

import jax
import jax.numpy as jnp
from jax import lax
from jax.experimental import pallas as pl
from jax.experimental.pallas import tpu as pltpu
from jax.sharding import PartitionSpec as P

EPSILON = 1e-05
MESH = pl.DeviceIdType.MESH
LOG2E = 1.4426950408889634
LN2 = 0.6931471805599453
MASKED = -1e30
TILE = 64
WIDE_TILE = 256
ROUNDS = 8
LOTS = 2
PACE = 3
BITS = 4
EARLY = (0, 2, 3, 4, 5)
F32 = jnp.float32
BF16 = jnp.bfloat16
ANY = pl.BlockSpec(memory_space=pl.ANY)
VMEM = pl.BlockSpec(memory_space=pltpu.VMEM)
SMEM = pl.BlockSpec(memory_space=pltpu.SMEM)


def dot(left, right, dims=(1, 0)):
    contract = (((dims[0],), (dims[1],)), ((), ()))
    return lax.dot_general(left, right, contract, preferred_element_type=F32)


class Place:
    def __init__(self, planes, slots, group):
        self.planes, self.slots, self.group = planes, slots, group
        self.g = lax.axis_index("graph")
        self.z = lax.axis_index("row")
        self.core = lax.rem(self.g, 2)
        turn = jnp.where(self.core == 1, self.z, planes - 1 - self.z)
        self.mine = [turn == self.turn(s) for s in range(slots)]
        self.slot = sum(jnp.where(own, s, 0) for s, own in enumerate(self.mine))
        self.works = functools.reduce(jnp.logical_or, self.mine)

    def turn(self, slot):
        return slot * self.planes // (self.slots + 1)

    def owner(self, slot):
        turn = self.turn(slot)
        return jnp.where(self.core == 1, turn, self.planes - 1 - turn)


def sub_rows(index, size):
    return pl.ds(pl.multiple_of(index * size, size), size)


def layer_kernel(
    dims,
    feat,
    adj,
    cot,
    counts,
    wp_in,
    ws_in,
    att_dst_in,
    att_src_in,
    bias,
    gain,
    shift,
    out,
    ig_out,
    proj_out,
    skip_out,
    sums_out,
    p_all,
    q_all,
    att_rows,
    feat_all,
    hid,
    wide,
    mask_own,
    adj_in,
    wp,
    ws,
    pre,
    mix,
    diff,
    low,
    dcol,
    parts,
    srow,
    p_slot,
    q_slot,
    centered,
    p_back,
    q_back,
    stat,
    stats_a,
    stats_b,
    swap_0,
    swap_1,
    swap_2,
    plane_0,
    plane_1,
    plane_2,
    line_in_0,
    line_in_1,
    line_in_2,
    line_out_0,
    line_out_1,
    line_out_2,
    f_send,
    f_recv,
    a_send,
    a_recv,
    c_send,
    c_recv,
    n_send,
    n_recv,
    i_send,
    i_recv,
    sa_send,
    sa_recv,
    sb_send,
    sb_recv,
    r_send,
    r_recv,
    lot_sem,
    own_sem,
    adj_sem,
    w_sem,
    p_sem,
    out_sem,
):
    planes, group, slots, rows, nodes, heads, head, width_in = dims
    width = heads * head
    tile = min(TILE, TILE * 1024 // nodes)
    tall = min(WIDE_TILE * 1024 // nodes * 1024 // nodes, rows)
    at = Place(planes, slots, group)
    g, z = at.g, at.z
    block = sub_rows(z, rows)
    resident = p_slot.shape[0] == heads
    mask_all = wide.at[:, 0:nodes]
    back = wide.at[:, 0:width]
    stage = wide.at[:, width : 2 * width]
    shared = wide.shape[1] < 3 * width
    ig = stage if shared else wide.at[:, 2 * width : 3 * width]

    barrier = pltpu.get_barrier_semaphore()
    for k in range(1, planes):
        pl.semaphore_signal(barrier, 1, device_id=(g, lax.rem(z + k, planes)), device_id_type=MESH)
    for k in range(1, group):
        pl.semaphore_signal(barrier, 1, device_id=(lax.rem(g + k, group), z), device_id_type=MESH)
    load_wp = pltpu.make_async_copy(wp_in, wp, w_sem.at[0])
    load_ws = pltpu.make_async_copy(ws_in, ws, w_sem.at[1])
    some = adj_in.shape[1]
    cuts = rows // some
    loads = [
        pltpu.make_async_copy(
            adj.at[i // cuts, pl.ds(i % cuts * some, some)], adj_in.at[i % 2], adj_sem.at[i % 2]
        )
        for i in range(cuts * slots)
    ]
    loads[0].start()
    loads[1].start()
    load_wp.start()
    load_ws.start()
    pl.semaphore_wait(barrier, planes - 1 + group - 1)

    def remote(source, target, send, recv, device):
        return pltpu.make_async_remote_copy(
            src_ref=source,
            dst_ref=target,
            send_sem=send,
            recv_sem=recv,
            device_id=device,
            device_id_type=MESH,
        )

    lot_rows = rows // LOTS

    def lot_of(source, target, s, src, lot):
        first = src * rows + lot * lot_rows
        return (
            source.at[s, lot * lot_rows : (lot + 1) * lot_rows],
            target.at[pl.ds(pl.multiple_of(first, lot_rows), lot_rows)],
        )

    def moves(source, target, send, recv, own):
        found = []
        for lot in range(LOTS):
            for s in range(slots):
                to = at.owner(s)
                here, there = lot_of(source, target, s, z, lot)
                away = remote(here, there, send.at[s, lot], recv.at[z, lot], (g, to))
                local = pltpu.make_async_copy(here, there, own.at[lot])
                found.append((to, away, local, lot))
        return found

    def start(copies):
        for lot in range(LOTS):
            for far in range(1, planes):
                for to, away, _, part in copies:
                    if part == lot:
                        pl.when(jnp.abs(to - z) == far)(away.start)
        for to, _, local, _ in copies:
            pl.when(to == z)(local.start)

    def sent(copies):
        for to, away, _, _ in copies:
            pl.when(to != z)(away.wait_send)

    def arrived(k, source, target, send, recv, own):
        src = lax.rem(z + k, planes)
        for lot in range(LOTS):
            here, there = lot_of(source, target, 0, src, lot)
            pl.when(k == 0)(pltpu.make_async_copy(here, there, own.at[lot]).wait)
            pl.when(k != 0)(
                remote(here, there, send.at[0, lot], recv.at[src, lot], (g, src)).wait_recv
            )
        return src

    f_args = (feat, feat_all, f_send, f_recv, lot_sem.at[0])
    a_args = (mask_own, mask_all, a_send, a_recv, lot_sem.at[1])
    c_args = (cot, low, c_send, c_recv, lot_sem.at[2])
    f_moves, a_moves, c_moves = moves(*f_args), moves(*a_args), moves(*c_args)
    start(f_moves)

    for i, load in enumerate(loads):
        load.wait()
        live_own = counts[i // cuts]

        @pl.loop(0, some // tile)
        def _(t):
            first = i % cuts * some + t * tile
            shape = (tile, nodes)
            row = lax.broadcasted_iota(jnp.int32, shape, 0) + (z * rows + first)
            col = lax.broadcasted_iota(jnp.int32, shape, 1)
            allowed = (adj_in[i % 2, sub_rows(t, tile), :] > 0) | (row == col)
            allowed = allowed & (row < live_own) & (col < live_own)
            mask_own[i // cuts, pl.ds(pl.multiple_of(first, tile), tile), :] = jnp.where(
                allowed, 0.0, MASKED
            ).astype(BF16)

        if i + 2 < len(loads):
            loads[i + 2].start()

    row = lax.broadcasted_iota(jnp.int32, (16, head), 0)
    for h in range(heads):
        src_row, dst_row = (
            kept[h : h + 1, :].astype(F32) for kept in (att_src_in, att_dst_in)
        )
        value = jnp.where(row == h, src_row, jnp.where(row == heads + h, dst_row, 0.0))
        att_rows[:, h * head : (h + 1) * head] = value.astype(BF16)

    load_wp.wait()
    load_ws.wait()
    start(a_moves)
    start(c_moves)
    live_count = counts[at.slot]

    def live_of(first, size):
        node = lax.broadcasted_iota(jnp.int32, (size, 1), 0) + first
        return (node < live_count).astype(F32)

    depth = p_slot.shape[0]

    def keep(h, here):
        if resident:
            return []
        slot = h % depth
        return [
            pltpu.make_async_copy(p_slot.at[slot], p_all.at[h, here], p_sem.at[0, slot]),
            pltpu.make_async_copy(q_slot.at[slot], q_all.at[h, here], p_sem.at[1, slot]),
        ]

    @pl.when(at.works)
    def _():
        @pl.loop(0, planes)
        def _(k):
            src = arrived(k, *f_args)
            here = sub_rows(src, rows)
            value = feat_all[here, :]
            for h in range(heads):
                part = slice(h * head, (h + 1) * head)
                hid[here, part] = dot(value, wp[:, part]).astype(BF16)
                pre[here, part] = dot(value, ws[:, part])
            made = hid[here, :]
            dcol[here, 0:16] = dot(made, att_rows[...], (1, 1)) * LOG2E
            srow[:, here] = dot(att_rows[...], made, (1, 1)) * LOG2E

        @pl.loop(0, planes)
        def _(k):
            src = arrived(k, *a_args)
            here = sub_rows(src, rows)
            for h in range(heads):
                part = slice(h * head, (h + 1) * head)
                slot = h if resident else h % depth
                base = src * rows if resident else 0

                if not resident:

                    @pl.when((k > 0) | (h >= depth))
                    def _():
                        for copy in keep(h, here):
                            copy.wait()

                @pl.loop(0, rows // tall)
                def _(t):
                    first = src * rows + t * tall
                    there = pl.ds(pl.multiple_of(first, tall), tall)
                    inside = pl.ds(pl.multiple_of(base + t * tall, tall), tall)
                    masked = mask_all[there, :].astype(F32) + srow[h : h + 1, :]
                    dst = dcol[there, heads + h : heads + h + 1]

                    def leaky(raw):
                        small = jnp.exp2(-jnp.abs(raw))
                        soft = jnp.log(1.0 + small)
                        return soft + jnp.maximum(raw * (1.25 * LN2), raw * (0.25 * LN2)), soft

                    peak, _ = leaky(jnp.max(masked, axis=1, keepdims=True) + dst)
                    raw = masked + dst
                    logit, soft = leaky(raw)
                    weight = jnp.exp2((logit - peak) * (0.8 * LOG2E))
                    total = jnp.sum(weight, axis=1, keepdims=True)
                    share = weight * (live_of(first, tall) / total)
                    slope = jnp.exp2(jnp.minimum(raw, 0.0) - soft * LOG2E) * 0.8 + 0.2
                    sloped = share * slope
                    p_slot[slot, inside, :] = share.astype(BF16)
                    q_slot[slot, inside, :] = sloped.astype(BF16)
                    middle = jnp.sum(sloped, axis=1, keepdims=True)
                    centered[sub_rows(t, tall), :] = (sloped - middle * share).astype(BF16)

                for copy in keep(h, here):
                    copy.start()
                mixed = dot(p_slot[slot, sub_rows(src, rows) if resident else slice(None), :], hid[:, part])
                mix[here, part] = mixed.astype(BF16)
                pre[here, part] += mixed + bias[:, part]
                diff[here, part] = dot(centered[...], hid[:, part]).astype(BF16)

    zero = jnp.zeros((8, width), F32)
    tiles = nodes // tile

    def fold(value):
        return sum(value[8 * i : 8 * i + 8] for i in range(tile // 8))

    def total_of(value):
        return jnp.sum(value, axis=0, keepdims=True)

    @pl.when(at.works)
    def _():
        def add_act(t, total):
            here = sub_rows(t, tile)
            value = pre[here, :]
            act = jnp.where(value > 0, value, jnp.exp(jnp.minimum(value, 0.0)) - 1.0)
            pre[here, :] = act
            return total + fold(act * live_of(t * tile, tile))

        number = jnp.maximum(live_count, 1).astype(F32)
        mean = total_of(lax.fori_loop(0, tiles, add_act, zero)) / number

        def add_square(t, total):
            off = pre[sub_rows(t, tile), :] - mean
            return total + fold(off * off * live_of(t * tile, tile))

        square = total_of(lax.fori_loop(0, tiles, add_square, zero))
        for k in range(planes):
            arrived(jnp.int32(k), *c_args)

        def add_grad(t, totals):
            here = sub_rows(t, tile)
            grad = low[here, :].astype(F32) * live_of(t * tile, tile)
            return totals[0] + fold(grad), totals[1] + fold(grad * (pre[here, :] - mean))

        plain, along = lax.fori_loop(0, tiles, add_grad, (zero, zero))
        stat[0:1, :] = jnp.full((1, width), live_count.astype(F32))
        stat[1:2, :] = mean
        stat[2:3, :] = square
        stat[3:4, :] = total_of(plain)
        stat[4:5, :] = total_of(along)
        stat[5:8, :] = jnp.zeros((3, width), F32)

    @pl.when(jnp.logical_not(at.works))
    def _():
        stat[...] = zero

    def exchange(which, size, me, held, send, recv, device):
        copies = []
        for k in range(1, size):
            peer = lax.rem(me + k, size)
            copy = remote(
                stat, held.at[which, me], send.at[which, k], recv.at[which, me], device(peer)
            )
            copy.start()
            copies.append(copy)
        held[which, me] = stat[...]
        for k in range(1, size):
            peer = lax.rem(me + k, size)
            remote(
                stat, held.at[which, peer], send.at[which, k], recv.at[which, peer], device(peer)
            ).wait_recv()
        for copy in copies:
            copy.wait_send()

    def everywhere(which, combine):
        exchange(which, group, g, stats_a, sa_send, sa_recv, lambda peer: (peer, z))
        combine(stats_a.at[which], group)
        exchange(which, planes, z, stats_b, sb_send, sb_recv, lambda peer: (g, peer))
        combine(stats_b.at[which], planes)

    def spread_out(held, size):
        number = sum(held[i, 0:1, :] for i in range(size))
        mean = sum(held[i, 0:1, :] * held[i, 1:2, :] for i in range(size))
        mean = mean / jnp.maximum(number, 1.0)
        square, plain, along = zero[0:1], zero[0:1], zero[0:1]
        for i in range(size):
            off = held[i, 1:2, :] - mean
            square = square + held[i, 2:3, :] + held[i, 0:1, :] * off * off
            plain = plain + held[i, 3:4, :]
            along = along + held[i, 4:5, :] + held[i, 3:4, :] * off
        stat[0:1, :] = number
        stat[1:2, :] = mean
        stat[2:3, :] = square
        stat[3:4, :] = plain
        stat[4:5, :] = along

    def plain_sum(held, size):
        stat[...] = sum(held[i] for i in range(size))

    everywhere(0, spread_out)
    number, mean = stat[0:1, :], stat[1:2, :]
    inv_std = lax.rsqrt(stat[2:3, :] / number + EPSILON)

    tile_rows = rows // BITS

    def give_norm(r, to):
        first = to * rows + r * tile_rows
        return remote(
            stage.at[pl.ds(pl.multiple_of(first, tile_rows), tile_rows)],
            out.at[at.slot, r * tile_rows : (r + 1) * tile_rows],
            n_send.at[to, r],
            n_recv.at[at.slot, r],
            (g, to),
        )

    def give_norms(first, last):
        @pl.when(at.works)
        def _():
            for p in range(first, min(last, BITS * (planes - 1))):
                r, k = p // (planes - 1), p % (planes - 1)
                give_norm(r, lax.rem(z + 1 + k, planes)).start()

    norm_own = pltpu.make_async_copy(stage.at[block], out.at[at.slot], own_sem.at[3])
    ig_own = pltpu.make_async_copy(ig.at[block], ig_out.at[at.slot], own_sem.at[4])
    bit_rows = rows // ROUNDS

    def give_bit(r, to):
        first = to * rows + r * bit_rows
        return remote(
            ig.at[pl.ds(pl.multiple_of(first, bit_rows), bit_rows)],
            ig_out.at[at.slot, r * bit_rows : (r + 1) * bit_rows],
            i_send.at[to, r],
            i_recv.at[at.slot, r],
            (g, to),
        )

    shift_grad = stat[3:4, :]
    gain_grad = stat[4:5, :] * inv_std
    sums_out[0:1, :] = gain_grad
    sums_out[1:2, :] = shift_grad
    scale = gain[...] * inv_std
    shift_mean = shift_grad / number
    gain_mean = gain_grad / number
    stat[...] = zero

    @pl.when(at.works)
    def _():
        def finish(r, t, total):
            cut_rows = tile_rows // tile
            j = lax.rem(z + 1 + t // cut_rows, planes)
            first = j * rows + r * tile_rows + lax.rem(t, cut_rows) * tile
            here = pl.ds(pl.multiple_of(first, tile), tile)
            live = live_of(first, tile)
            act = pre[here, :]
            grown = jnp.minimum(act, 0.0) + 1.0
            normed = (act - mean) * inv_std
            stage[here, :] = ((gain[...] * normed + shift[...]) * live).astype(BF16)
            grad = low[here, :].astype(F32) * live
            grad = scale * (grad - shift_mean - normed * gain_mean) * live * grown
            grad_low = grad.astype(BF16)
            low[here, :] = grad_low
            grad_low = grad_low.astype(F32)
            lane = lax.broadcasted_iota(jnp.int32, (tile, 128), 1)
            along_mix = grad_low * mix[here, :].astype(F32)
            along_diff = grad_low * diff[here, :].astype(F32)
            spread = jnp.zeros((tile, 128), F32)
            for h in range(heads):
                part = slice(h * head, (h + 1) * head)
                one = jnp.sum(along_mix[:, part], axis=1, keepdims=True)
                spread = jnp.where(lane % heads == h, one, spread)
                dcol[here, h : h + 1] = jnp.sum(along_diff[:, part], axis=1, keepdims=True)
            top = spread.astype(BF16)
            rest = spread - top.astype(F32)
            middle = rest.astype(BF16)
            bottom = (rest - middle.astype(F32)).astype(BF16)
            third = lane // heads
            parts[here, :] = jnp.where(
                third == 0, top, jnp.where(third == 1, middle, jnp.where(third == 2, bottom, 0.0))
            ).astype(BF16)
            return total + fold(grad)

        total = zero
        for r in range(BITS):
            total = lax.fori_loop(
                0, planes * tile_rows // tile, functools.partial(finish, r), total
            )
            for p in range(EARLY[r], EARLY[r + 1]):
                give_norm(p // (planes - 1), lax.rem(z + 1 + p % (planes - 1), planes)).start()
        norm_own.start()
        stat[0:1, :] = total_of(total)
        for h in range(depth):
            for copy in keep(h, block):
                copy.wait()

    chips = group // 2
    chip, core = g // 2, lax.rem(g, 2)
    partner = g + 1 - 2 * core
    swaps, plane_ins = (swap_0, swap_1, swap_2), (plane_0, plane_1, plane_2)
    line_ins, line_outs = (line_in_0, line_in_1, line_in_2), (line_out_0, line_out_1, line_out_2)
    spans = ((0, width), (0, width // 2), (width // 2, width))
    strip = width_in // chips

    def share(u, which):
        size = (spans[u][1] - spans[u][0]) // 2
        return pl.ds(pl.multiple_of(which * size, size), size)

    lines = planes.bit_length() - 1
    regions = [(0, strip, 0, 2)]
    sides = []
    for i in range(lines):
        top, high, left, across = regions[-1]
        bit = lax.rem(z // 2**i, 2)
        pair = []
        for b in (bit, 1 - bit):
            if high >= 32:
                pair.append((top + b * (high // 2), high // 2, left, across))
            else:
                pair.append((top, high, left + b * (across // 2), across // 2))
        regions.append(pair[0])
        sides.append((z + 2**i - 2 ** (i + 1) * bit, pair[0], pair[1]))

    def cut(u, region):
        top, high, left, across = region
        size = (spans[u][1] - spans[u][0]) // 4
        left, across = left * size, across * size
        return (
            pl.ds(top if isinstance(top, int) else pl.multiple_of(top, high), high),
            pl.ds(left if isinstance(left, int) else pl.multiple_of(left, across), across),
        )

    def unit_of(u):
        kept = mix if u else diff
        return kept.at[0:width_in, spans[u][0] : spans[u][1]]

    def strip_of(index):
        return pl.ds(pl.multiple_of(index * strip, strip), strip)

    def to_core(u):
        return remote(
            unit_of(u).at[:, share(u, 1 - core)], swaps[u], r_send.at[u, 0, 0], r_recv.at[u, 0, 0], (partner, z)
        )

    def to_chip(u, peer, landed):
        return remote(
            unit_of(u).at[strip_of(peer), share(u, core)],
            plane_ins[u].at[landed],
            r_send.at[u, 1, peer],
            r_recv.at[u, 1, landed],
            (2 * peer + core, z),
        )

    def landed_at(u, i):
        _, high, _, across = sides[i][1]
        return line_ins[u].at[i, 0:high, 0 : across * (spans[u][1] - spans[u][0]) // 4]

    def to_line(u, i):
        peer, kept, given = sides[i]
        return remote(
            line_outs[u].at[cut(u, given)], landed_at(u, i), r_send.at[u, 2, i], r_recv.at[u, 2, i], (g, peer)
        )

    def from_line(u, i, landed=False):
        peer, kept, given = sides[i]
        where = swaps[u].at[strip_of(chip)].at[cut(u, given if landed else kept)]
        return remote(where, where, r_send.at[u, 3, i], r_recv.at[u, 3, i], (g, peer))

    def from_chip(u, peer, landed):
        where = swaps[u].at[strip_of(landed)]
        return remote(
            where, where, r_send.at[u, 4, peer], r_recv.at[u, 4, landed], (2 * peer + core, z)
        )

    def from_core(u, which):
        return remote(
            swaps[u],
            unit_of(u).at[:, share(u, which)],
            r_send.at[u, 5, 0],
            r_recv.at[u, 5, 0],
            (partner, z),
        )

    def others(size, me):
        return [lax.rem(me + k, size) for k in range(1, size)]

    last_step = 4 + 2 * lines

    def step(u, number):
        unit, own = unit_of(u), share(u, core)
        if number == 0:
            to_core(u).start()
        elif number == 1:
            to_core(u).wait()

            @pl.loop(0, width_in // tall)
            def _(t):
                here = sub_rows(t, tall)
                value = unit[here, own].astype(F32) + swaps[u][here, :].astype(F32)
                unit[here, own] = value.astype(BF16)

            for peer in others(chips, chip):
                to_chip(u, peer, chip).start()
        elif number <= 2 + lines:
            i = number - 3
            if i < 0:
                for peer in others(chips, chip):
                    to_chip(u, peer, peer).wait_recv()
                value = unit[strip_of(chip), own].astype(F32)
                for peer in others(chips, chip):
                    value = value + plane_ins[u][peer].astype(F32)
                line_outs[u][...] = value.astype(BF16)
            else:
                kept = sides[i][1]
                to_line(u, i).wait_recv()
                value = line_outs[u][cut(u, kept)].astype(F32)
                value = value + landed_at(u, i)[...].astype(F32)
                target = line_outs[u] if i + 1 < lines else swaps[u].at[strip_of(chip)]
                target[cut(u, kept)] = value.astype(BF16)
            if i + 1 < lines:
                to_line(u, i + 1).start()
            else:
                from_line(u, lines - 1).start()
            if i < 0:
                for peer in others(chips, chip):
                    to_chip(u, peer, chip).wait_send()
            else:
                to_line(u, i).wait_send()
        elif number <= 2 + 2 * lines:
            i = 2 + 2 * lines - number
            from_line(u, i, True).wait_recv()
            if i > 0:
                from_line(u, i - 1).start()
            else:
                for peer in others(chips, chip):
                    from_chip(u, peer, chip).start()
            from_line(u, i).wait_send()
        elif number < last_step:
            for peer in others(chips, chip):
                from_chip(u, peer, peer).wait_recv()
            from_core(u, core).start()

            @pl.loop(0, width_in // tall)
            def _(t):
                here = sub_rows(t, tall)
                unit[here, own] = swaps[u][here, :]

            for peer in others(chips, chip):
                from_chip(u, peer, chip).wait_send()
        else:
            from_core(u, 1 - core).wait_recv()
            from_core(u, core).wait_send()
            answer(u).start()

    def steps(*work):
        for u, number in work:
            step(u, number)

    def answer(u):
        target = proj_out if u else skip_out
        return pltpu.make_async_copy(unit_of(u), target.at[:, slice(*spans[u])], out_sem.at[u])

    def fetch(j, h):
        if resident:
            return []
        place = pl.ds(pl.multiple_of(j * rows, rows), rows)
        slot = h % 2
        return [
            pltpu.make_async_copy(p_all.at[h, :, place], p_back.at[slot], p_sem.at[2, slot]),
            pltpu.make_async_copy(q_all.at[h, :, place], q_back.at[slot], p_sem.at[3, slot]),
        ]

    def product(u, right):
        unit = unit_of(u)
        columns = slice(*spans[u])

        @pl.when(at.works)
        def _():
            @pl.loop(0, width_in // head)
            def _(f):
                place = sub_rows(f, head)
                unit[place, :] = dot(feat_all[:, place], right[:, columns], (0, 0)).astype(BF16)

        @pl.when(jnp.logical_not(at.works))
        def _():
            unit[...] = jnp.zeros_like(unit)

    @pl.when(at.works)
    def _():
        for copy in fetch(lax.rem(z + 1, planes), 0):
            copy.start()

    product(0, low)
    step(0, 0)

    def source_block(k, turn):
        j = lax.rem(z + 1 + k, planes)
        here = sub_rows(j, rows)
        per_turn = heads // 2
        for h in range(turn * per_turn, (turn + 1) * per_turn):
            part = slice(h * head, (h + 1) * head)
            slot = h % 2
            if h + 1 < (turn + 1) * per_turn:
                for copy in fetch(j, h + 1):
                    copy.start()
            else:

                @pl.when(k + 1 < planes)
                def _():
                    for copy in fetch(lax.rem(j + 1, planes), turn * per_turn):
                        copy.start()

                if turn == 0:

                    @pl.when(k + 1 == planes)
                    def _():
                        for copy in fetch(lax.rem(z + 1, planes), per_turn):
                            copy.start()

            for copy in fetch(j, h):
                copy.wait()
            if resident:
                p_now, q_now = p_slot[h, :, sub_rows(j, rows)], q_slot[h, :, sub_rows(j, rows)]
            else:
                p_now, q_now = p_back[slot], q_back[slot]
            grad = dot(p_now, low[:, part], (0, 0))
            along = dot(q_now, low[:, part], (0, 0))
            spread = dot(q_now, parts[...], (0, 0))
            lane = lax.broadcasted_iota(jnp.int32, spread.shape, 1)
            chosen = (lane % heads == h) & (lane < 3 * heads)
            own = hid[here, part].astype(F32)
            by_src = jnp.sum(own * along, axis=1, keepdims=True) - jnp.sum(
                jnp.where(chosen, spread, 0.0), axis=1, keepdims=True
            )
            by_dst = dcol[here, h : h + 1]
            att_src, att_dst = (
                att_rows[i : i + 1, part].astype(F32) for i in (h, heads + h)
            )
            grad = grad + by_dst * att_dst + by_src * att_src
            back[here, part] = grad.astype(BF16)
            stat[1:2, part] += total_of(by_dst * own)
            stat[2:3, part] += total_of(by_src * own)

    def sent_norm(j):
        @pl.when(j != z)
        def _():
            for r in range(BITS):
                give_norm(r, j).wait_send()

        pl.when(j == z)(norm_own.wait)

    def input_block(k):
        j = lax.rem(z + 1 + k, planes)
        here = sub_rows(j, rows)
        if shared:
            sent_norm(j)
        for f in range(width_in // head):
            part = slice(f * head, (f + 1) * head)
            ig[here, part] = (
                dot(back[here, :], wp[part, :], (1, 1)) + dot(low[here, :], ws[part, :], (1, 1))
            ).astype(BF16)
        pl.when(j == z)(ig_own.start)

    def give_bits(first, last):
        @pl.when(at.works)
        def _():
            for p in range(first, min(last, ROUNDS * (planes - 1))):
                give_bit(p % ROUNDS, lax.rem(z + 1 + p // ROUNDS, planes)).start()

    def S(u, number):
        return lambda: step(u, number) if number <= last_step else None

    def N(first, last):
        return lambda: give_norms(first, last)

    def R(first, last):
        return lambda: give_bits(first, last)

    def do(*work):
        for one in work:
            one()

    def walk(turn, **work):
        @pl.loop(0, planes)
        def _(k):
            pl.when(at.works)(functools.partial(source_block, k, turn))
            for when, todo in work.items():
                pl.when(k == int(when[1:]))(functools.partial(do, *todo))

    def input_of(k):
        pl.when(at.works)(functools.partial(input_block, k))

    def I(k):
        return lambda: input_of(k)

    last = BITS * (planes - 1)
    do(N(5, 7))
    walk(0, k0=(S(0, 1),), k1=(N(7, 8),), k3=(N(8, 9),))
    product(1, back)
    do(S(1, 0), N(9, 10))
    walk(1, k0=(S(1, 1), N(10, 11)), k1=(I(0), N(11, last)), k3=(S(0, 2), R(0, 0)))
    product(2, back)
    do(S(2, 0), R(0, 0), I(1), S(2, 1), S(0, 3), I(2), S(1, 2), R(0, 6))
    for k in range(3, planes):
        input_of(k)
    exchange(1, group, g, stats_a, sa_send, sa_recv, lambda peer: (peer, z))
    plain_sum(stats_a.at[1], group)
    done, given = [3, 2, 1], 6
    for number in range(2, last_step + 1):
        for u, target in ((2, number), (1, number + 1), (0, number + 2)):
            while done[u] < min(target, last_step):
                done[u] += 1
                step(u, done[u])
        give_bits(given, given + PACE)
        given += PACE
    give_bits(given, ROUNDS * (planes - 1))
    exchange(1, planes, z, stats_b, sb_send, sb_recv, lambda peer: (g, peer))
    plain_sum(stats_b.at[1], planes)
    sums_out[2:5, :] = stat[0:3, :]
    sums_out[5:8, :] = jnp.zeros((3, width), F32)

    for s in range(slots):

        @pl.when(jnp.logical_not(at.mine[s]))
        def _():
            for r in range(BITS):
                landing = out.at[s, r * tile_rows : (r + 1) * tile_rows]
                remote(landing, landing, n_send.at[0, r], n_recv.at[s, r], (g, at.owner(s))).wait_recv()
            for r in range(ROUNDS):
                landing = ig_out.at[s, r * bit_rows : (r + 1) * bit_rows]
                remote(landing, landing, i_send.at[0, r], i_recv.at[s, r], (g, at.owner(s))).wait_recv()

    @pl.when(at.works)
    def _():
        ig_own.wait()
        for peer in others(planes, z):
            for r in range(ROUNDS):
                give_bit(r, peer).wait_send()
        if not shared:
            for k in range(planes):
                sent_norm(lax.rem(z + k, planes))

    for u in range(3):
        answer(u).wait()
    sent(f_moves)
    sent(a_moves)
    sent(c_moves)


def finish_kernel(
    near,
    out_in,
    ig_in,
    proj_in,
    skip_in,
    sums,
    out,
    ig,
    proj,
    skip,
    att_dst,
    att_src,
    bias,
    gain,
    shift,
    narrow,
    full,
    held,
    copy_sem,
    in_sem,
    wide_sem,
):
    heads, head = att_dst.shape
    passing = []
    for i, (source, target) in enumerate(((out_in, out), (ig_in, ig))):
        for s in range(out.shape[0]):
            load = None if near else pltpu.make_async_copy(source.at[s], held.at[i, s], copy_sem.at[i, s])
            kept = source.at[s] if near else held.at[i, s]
            store = pltpu.make_async_copy(kept, target.at[s], copy_sem.at[i, s])
            passing.append((load, store))
    size = proj.shape[0] // 4
    lots = []
    for i, (source, target) in enumerate(((proj_in, proj), (skip_in, skip))):
        for k in range(4):
            rows = pl.ds(k * size, size)
            load = None if near else pltpu.make_async_copy(source.at[rows], narrow.at[i, rows], in_sem.at[i, k])
            store = pltpu.make_async_copy(full.at[i, rows], target.at[rows], wide_sem.at[i, k])
            lots.append((source if near else narrow.at[i], i, rows, load, store))
    if near:
        for _, store in passing:
            store.start()
    else:
        for _, _, _, load, _ in lots:
            load.start()
        for load, _ in passing:
            load.start()
    for h in range(heads):
        part = slice(h * head, (h + 1) * head)
        att_dst[h : h + 1, :] = sums[3:4, part]
        att_src[h : h + 1, :] = sums[4:5, part]
    gain[...] = sums[0:1, :]
    shift[...] = sums[1:2, :]
    bias[...] = sums[2:3, :]
    for source, i, rows, load, store in lots:
        if not near:
            load.wait()
        full[i, rows, :] = source[rows, :].astype(F32)
        store.start()
    if not near:
        for load, store in passing:
            load.wait()
            store.start()
    for _, _, _, _, store in lots:
        store.wait()
    for _, store in passing:
        store.wait()


def shards(
    planes,
    group,
    features,
    adjacency,
    counts,
    proj_weight,
    skip_weight,
    attn_dst,
    attn_src,
    attn_bias,
    norm_gain,
    norm_shift,
    cotangent,
):
    slots, rows, width_in = features.shape
    nodes = adjacency.shape[2]
    heads, head = attn_dst.shape
    width = heads * head
    dims = (planes, group, slots, rows, nodes, heads, head, width_in)
    dma = pltpu.SemaphoreType.DMA
    chips = group // 2
    strip, shares = width_in // chips, (width // 2, width // 4, width // 4)
    lines = planes.bit_length() - 1
    tallest = max(nodes, width_in)
    resident = nodes <= 1024
    kept = (heads, nodes, nodes) if resident else (1, rows, nodes)

    shape = jax.ShapeDtypeStruct
    vmem = pltpu.VMEM
    near = pltpu.VMEM if resident else shape
    square = shape((heads, 16, 128) if resident else (heads, nodes, nodes), BF16)
    output, input_grad, proj_grad, skip_grad, sums, _, _ = pl.pallas_call(
        functools.partial(layer_kernel, dims),
        out_shape=[
            near((slots, rows, width), BF16),
            near((slots, rows, width_in), BF16),
            near((width_in, width), BF16),
            near((width_in, width), BF16),
            shape((8, width), F32),
            square,
            square,
        ],
        in_specs=[ANY, ANY, ANY, SMEM, ANY, ANY, VMEM, VMEM, VMEM, VMEM, VMEM],
        out_specs=[ANY, ANY, ANY, ANY, VMEM, ANY, ANY],
        scratch_shapes=[
            vmem((16, width), BF16),
            vmem((nodes, width_in), BF16),
            vmem((nodes, width), BF16),
            vmem((nodes, max(nodes, (3 if nodes <= 1024 else 2) * width)), BF16),
            vmem((slots, rows, nodes), BF16),
            vmem((2, max(rows // 4, TILE), nodes), jnp.int32),
            vmem((width_in, width), BF16),
            vmem((width_in, width), BF16),
            vmem((nodes, width), F32),
            vmem((tallest, width), BF16),
            vmem((tallest, width), BF16),
            vmem((nodes, width), BF16),
            vmem((nodes, 128), F32),
            vmem((nodes, 128), BF16),
            vmem((16, nodes), F32),
            vmem(kept, BF16),
            vmem(kept, BF16),
            vmem((rows, nodes), BF16),
            vmem((1 if resident else 2, 16 if resident else nodes, rows), BF16),
            vmem((1 if resident else 2, 16 if resident else nodes, rows), BF16),
            vmem((8, width), F32),
            vmem((2, group, 8, width), F32),
            vmem((2, planes, 8, width), F32),
            *(vmem((width_in, one), BF16) for one in shares),
            *(vmem((chips, strip, one), BF16) for one in shares),
            *(vmem((lines, max(strip // 2, 16), one), BF16) for one in shares),
            *(vmem((strip, one), BF16) for one in shares),
            dma((slots, LOTS)),
            dma((planes, LOTS)),
            dma((slots, LOTS)),
            dma((planes, LOTS)),
            dma((slots, LOTS)),
            dma((planes, LOTS)),
            dma((planes, BITS)),
            dma((slots, BITS)),
            dma((planes, ROUNDS)),
            dma((slots, ROUNDS)),
            dma((2, group)),
            dma((2, group)),
            dma((2, planes)),
            dma((2, planes)),
            dma((3, 6, max(chips, lines))),
            dma((3, 6, max(chips, lines))),
            dma((3, LOTS)),
            dma((5,)),
            dma((2,)),
            dma((2,)),
            dma((4, 2)),
            dma((3,)),
        ],
        compiler_params=pltpu.CompilerParams(
            collective_id=0,
            has_side_effects=True,
            vmem_limit_bytes=(54 if resident else 63) * 2**20,
        ),
    )(
        features,
        adjacency,
        cotangent,
        counts,
        proj_weight,
        skip_weight,
        attn_dst,
        attn_src,
        attn_bias.reshape(1, width),
        norm_gain.reshape(1, width),
        norm_shift.reshape(1, width),
    )
    line = shape((1, width), F32)
    weight, att = shape((width_in, width), F32), shape((heads, head), F32)
    output, input_grad, proj_grad, skip_grad, dst_grad, src_grad, bias, gain, shift = pl.pallas_call(
        functools.partial(finish_kernel, resident),
        out_shape=[
            shape(output.shape, BF16),
            shape(input_grad.shape, BF16),
            weight,
            weight,
            att,
            att,
            line,
            line,
            line,
        ],
        in_specs=[VMEM if resident else ANY] * 4 + [VMEM],
        out_specs=[ANY] * 4 + [VMEM] * 5,
        scratch_shapes=[
            vmem((1, 16, 128) if resident else (2, width_in, width), BF16),
            vmem((2, width_in, width), F32),
            vmem((2, slots, 16, 128) if resident else (2,) + output.shape, BF16),
            dma((2, slots)),
            dma((2, 4)),
            dma((2, 4)),
        ],
        compiler_params=pltpu.CompilerParams(vmem_limit_bytes=(40 if resident else 60) * 2**20),
    )(output, input_grad, proj_grad, skip_grad, sums)
    flat = (width,)
    return (
        output,
        input_grad,
        proj_grad,
        skip_grad,
        dst_grad,
        src_grad,
        bias.reshape(flat),
        gain.reshape(flat),
        shift.reshape(flat),
    )


def solution(mesh):
    placed = (
        P("graph", "row", None),
        P("graph", "row", None),
        P("graph"),
        P(),
        P(),
        P(),
        P(),
        P(),
        P(),
        P(),
        P("graph", "row", None),
    )
    return jax.shard_map(
        functools.partial(shards, mesh.shape["row"], mesh.shape["graph"]),
        mesh=mesh,
        in_specs=placed,
        out_specs=(
            P("graph", "row", None),
            P("graph", "row", None),
            P(),
            P(),
            P(),
            P(),
            P(),
            P(),
            P(),
        ),
        check_vma=False,
    )
```

```python
import functools

import jax
import jax.numpy as jnp
from jax import lax
from jax.experimental import pallas as pl
from jax.experimental.pallas import tpu as pltpu
from jax.sharding import PartitionSpec as P

EPSILON = 1e-05
MESH = pl.DeviceIdType.MESH
LOG2E = 1.4426950408889634
LN2 = 0.6931471805599453
MASKED = -1e30
TILE = 64
WIDE_TILE = 256
ROUNDS = 8
LOTS = 2
PACE = 3
BITS = 4
EARLY = (0, 3, 5, 6, 7)
F32 = jnp.float32
BF16 = jnp.bfloat16
ANY = pl.BlockSpec(memory_space=pl.ANY)
VMEM = pl.BlockSpec(memory_space=pltpu.VMEM)
SMEM = pl.BlockSpec(memory_space=pltpu.SMEM)


def dot(left, right, dims=(1, 0)):
    contract = (((dims[0],), (dims[1],)), ((), ()))
    return lax.dot_general(left, right, contract, preferred_element_type=F32)


class Place:
    def __init__(self, planes, slots, group):
        self.planes, self.slots, self.group = planes, slots, group
        self.g = lax.axis_index("graph")
        self.z = lax.axis_index("row")
        self.core = lax.rem(self.g, 2)
        turn = jnp.where(self.core == 1, self.z, planes - 1 - self.z)
        self.mine = [turn == self.turn(s) for s in range(slots)]
        self.slot = sum(jnp.where(own, s, 0) for s, own in enumerate(self.mine))
        self.works = functools.reduce(jnp.logical_or, self.mine)

    def turn(self, slot):
        return slot * self.planes // (self.slots + 1)

    def owner(self, slot):
        turn = self.turn(slot)
        return jnp.where(self.core == 1, turn, self.planes - 1 - turn)


def sub_rows(index, size):
    return pl.ds(pl.multiple_of(index * size, size), size)


def layer_kernel(
    dims,
    feat,
    adj,
    cot,
    counts,
    wp_in,
    ws_in,
    att_dst_in,
    att_src_in,
    bias,
    gain,
    shift,
    out,
    ig_out,
    proj_out,
    skip_out,
    sums_out,
    p_all,
    q_all,
    att_rows,
    feat_all,
    hid,
    wide,
    mask_own,
    adj_in,
    wp,
    ws,
    pre,
    mix,
    diff,
    low,
    dcol,
    parts,
    srow,
    p_slot,
    q_slot,
    centered,
    p_back,
    q_back,
    stat,
    stats_a,
    stats_b,
    swap_0,
    swap_1,
    swap_2,
    plane_0,
    plane_1,
    plane_2,
    line_in_0,
    line_in_1,
    line_in_2,
    line_out_0,
    line_out_1,
    line_out_2,
    f_send,
    f_recv,
    a_send,
    a_recv,
    c_send,
    c_recv,
    n_send,
    n_recv,
    i_send,
    i_recv,
    sa_send,
    sa_recv,
    sb_send,
    sb_recv,
    r_send,
    r_recv,
    lot_sem,
    own_sem,
    adj_sem,
    w_sem,
    p_sem,
    out_sem,
):
    planes, group, slots, rows, nodes, heads, head, width_in = dims
    width = heads * head
    tile = min(TILE, TILE * 1024 // nodes)
    tall = min(WIDE_TILE * 1024 // nodes * 1024 // nodes, rows)
    at = Place(planes, slots, group)
    g, z = at.g, at.z
    block = sub_rows(z, rows)
    resident = p_slot.shape[0] == heads
    mask_all = wide.at[:, 0:nodes]
    back = wide.at[:, 0:width]
    stage = wide.at[:, width : 2 * width]
    shared = wide.shape[1] < 3 * width
    ig = stage if shared else wide.at[:, 2 * width : 3 * width]

    barrier = pltpu.get_barrier_semaphore()
    for k in range(1, planes):
        pl.semaphore_signal(barrier, 1, device_id=(g, lax.rem(z + k, planes)), device_id_type=MESH)
    for k in range(1, group):
        pl.semaphore_signal(barrier, 1, device_id=(lax.rem(g + k, group), z), device_id_type=MESH)
    load_wp = pltpu.make_async_copy(wp_in, wp, w_sem.at[0])
    load_ws = pltpu.make_async_copy(ws_in, ws, w_sem.at[1])
    some = adj_in.shape[1]
    cuts = rows // some
    loads = [
        pltpu.make_async_copy(
            adj.at[i // cuts, pl.ds(i % cuts * some, some)], adj_in.at[i % 2], adj_sem.at[i % 2]
        )
        for i in range(cuts * slots)
    ]
    loads[0].start()
    loads[1].start()
    load_wp.start()
    load_ws.start()
    pl.semaphore_wait(barrier, planes - 1 + group - 1)

    def remote(source, target, send, recv, device):
        return pltpu.make_async_remote_copy(
            src_ref=source,
            dst_ref=target,
            send_sem=send,
            recv_sem=recv,
            device_id=device,
            device_id_type=MESH,
        )

    lot_rows = rows // LOTS

    def lot_of(source, target, s, src, lot):
        first = src * rows + lot * lot_rows
        return (
            source.at[s, lot * lot_rows : (lot + 1) * lot_rows],
            target.at[pl.ds(pl.multiple_of(first, lot_rows), lot_rows)],
        )

    def moves(source, target, send, recv, own):
        found = []
        for lot in range(LOTS):
            for s in range(slots):
                to = at.owner(s)
                here, there = lot_of(source, target, s, z, lot)
                away = remote(here, there, send.at[s, lot], recv.at[z, lot], (g, to))
                local = pltpu.make_async_copy(here, there, own.at[lot])
                found.append((to, away, local, lot))
        return found

    def start(copies):
        for lot in range(LOTS):
            for far in range(1, planes):
                for to, away, _, part in copies:
                    if part == lot:
                        pl.when(jnp.abs(to - z) == far)(away.start)
        for to, _, local, _ in copies:
            pl.when(to == z)(local.start)

    def sent(copies):
        for to, away, _, _ in copies:
            pl.when(to != z)(away.wait_send)

    def arrived(k, source, target, send, recv, own):
        src = lax.rem(z + k, planes)
        for lot in range(LOTS):
            here, there = lot_of(source, target, 0, src, lot)
            pl.when(k == 0)(pltpu.make_async_copy(here, there, own.at[lot]).wait)
            pl.when(k != 0)(
                remote(here, there, send.at[0, lot], recv.at[src, lot], (g, src)).wait_recv
            )
        return src

    f_args = (feat, feat_all, f_send, f_recv, lot_sem.at[0])
    a_args = (mask_own, mask_all, a_send, a_recv, lot_sem.at[1])
    c_args = (cot, low, c_send, c_recv, lot_sem.at[2])
    f_moves, a_moves, c_moves = moves(*f_args), moves(*a_args), moves(*c_args)
    start(f_moves)

    for i, load in enumerate(loads):
        load.wait()
        live_own = counts[i // cuts]

        @pl.loop(0, some // tile)
        def _(t):
            first = i % cuts * some + t * tile
            shape = (tile, nodes)
            row = lax.broadcasted_iota(jnp.int32, shape, 0) + (z * rows + first)
            col = lax.broadcasted_iota(jnp.int32, shape, 1)
            allowed = (adj_in[i % 2, sub_rows(t, tile), :] > 0) | (row == col)
            allowed = allowed & (row < live_own) & (col < live_own)
            mask_own[i // cuts, pl.ds(pl.multiple_of(first, tile), tile), :] = jnp.where(
                allowed, 0.0, MASKED
            ).astype(BF16)

        if i + 2 < len(loads):
            loads[i + 2].start()

    row = lax.broadcasted_iota(jnp.int32, (16, head), 0)
    for h in range(heads):
        src_row, dst_row = (
            kept[h : h + 1, :].astype(F32) for kept in (att_src_in, att_dst_in)
        )
        value = jnp.where(row == h, src_row, jnp.where(row == heads + h, dst_row, 0.0))
        att_rows[:, h * head : (h + 1) * head] = value.astype(BF16)

    load_wp.wait()
    load_ws.wait()
    start(a_moves)
    start(c_moves)
    live_count = counts[at.slot]

    def live_of(first, size):
        node = lax.broadcasted_iota(jnp.int32, (size, 1), 0) + first
        return (node < live_count).astype(F32)

    depth = p_slot.shape[0]

    def keep(h, here):
        if resident:
            return []
        slot = h % depth
        return [
            pltpu.make_async_copy(p_slot.at[slot], p_all.at[h, here], p_sem.at[0, slot]),
            pltpu.make_async_copy(q_slot.at[slot], q_all.at[h, here], p_sem.at[1, slot]),
        ]

    @pl.when(at.works)
    def _():
        @pl.loop(0, planes)
        def _(k):
            src = arrived(k, *f_args)
            here = sub_rows(src, rows)
            value = feat_all[here, :]
            for h in range(heads):
                part = slice(h * head, (h + 1) * head)
                hid[here, part] = dot(value, wp[:, part]).astype(BF16)
                pre[here, part] = dot(value, ws[:, part])
            made = hid[here, :]
            dcol[here, 0:16] = dot(made, att_rows[...], (1, 1)) * LOG2E
            srow[:, here] = dot(att_rows[...], made, (1, 1)) * LOG2E

        @pl.loop(0, planes)
        def _(k):
            src = arrived(k, *a_args)
            here = sub_rows(src, rows)
            for h in range(heads):
                part = slice(h * head, (h + 1) * head)
                slot = h if resident else h % depth
                base = src * rows if resident else 0

                if not resident:

                    @pl.when((k > 0) | (h >= depth))
                    def _():
                        for copy in keep(h, here):
                            copy.wait()

                @pl.loop(0, rows // tall)
                def _(t):
                    first = src * rows + t * tall
                    there = pl.ds(pl.multiple_of(first, tall), tall)
                    inside = pl.ds(pl.multiple_of(base + t * tall, tall), tall)
                    masked = mask_all[there, :].astype(F32) + srow[h : h + 1, :]
                    dst = dcol[there, heads + h : heads + h + 1]

                    def leaky(raw):
                        small = jnp.exp2(-jnp.abs(raw))
                        soft = jnp.log(1.0 + small)
                        return soft + jnp.maximum(raw * (1.25 * LN2), raw * (0.25 * LN2)), soft

                    peak, _ = leaky(jnp.max(masked, axis=1, keepdims=True) + dst)
                    raw = masked + dst
                    logit, soft = leaky(raw)
                    weight = jnp.exp2((logit - peak) * (0.8 * LOG2E))
                    total = jnp.sum(weight, axis=1, keepdims=True)
                    share = weight * (live_of(first, tall) / total)
                    slope = jnp.exp2(jnp.minimum(raw, 0.0) - soft * LOG2E) * 0.8 + 0.2
                    sloped = share * slope
                    p_slot[slot, inside, :] = share.astype(BF16)
                    q_slot[slot, inside, :] = sloped.astype(BF16)
                    middle = jnp.sum(sloped, axis=1, keepdims=True)
                    centered[sub_rows(t, tall), :] = (sloped - middle * share).astype(BF16)

                for copy in keep(h, here):
                    copy.start()
                mixed = dot(p_slot[slot, sub_rows(src, rows) if resident else slice(None), :], hid[:, part])
                mix[here, part] = mixed.astype(BF16)
                pre[here, part] += mixed + bias[:, part]
                diff[here, part] = dot(centered[...], hid[:, part]).astype(BF16)

    zero = jnp.zeros((8, width), F32)
    tiles = nodes // tile

    def fold(value):
        return sum(value[8 * i : 8 * i + 8] for i in range(tile // 8))

    def total_of(value):
        return jnp.sum(value, axis=0, keepdims=True)

    @pl.when(at.works)
    def _():
        def add_act(t, total):
            here = sub_rows(t, tile)
            value = pre[here, :]
            act = jnp.where(value > 0, value, jnp.exp(jnp.minimum(value, 0.0)) - 1.0)
            pre[here, :] = act
            return total + fold(act * live_of(t * tile, tile))

        number = jnp.maximum(live_count, 1).astype(F32)
        mean = total_of(lax.fori_loop(0, tiles, add_act, zero)) / number

        def add_square(t, total):
            off = pre[sub_rows(t, tile), :] - mean
            return total + fold(off * off * live_of(t * tile, tile))

        square = total_of(lax.fori_loop(0, tiles, add_square, zero))
        for k in range(planes):
            arrived(jnp.int32(k), *c_args)

        def add_grad(t, totals):
            here = sub_rows(t, tile)
            grad = low[here, :].astype(F32) * live_of(t * tile, tile)
            return totals[0] + fold(grad), totals[1] + fold(grad * (pre[here, :] - mean))

        plain, along = lax.fori_loop(0, tiles, add_grad, (zero, zero))
        stat[0:1, :] = jnp.full((1, width), live_count.astype(F32))
        stat[1:2, :] = mean
        stat[2:3, :] = square
        stat[3:4, :] = total_of(plain)
        stat[4:5, :] = total_of(along)
        stat[5:8, :] = jnp.zeros((3, width), F32)

    @pl.when(jnp.logical_not(at.works))
    def _():
        stat[...] = zero

    def exchange(which, size, me, held, send, recv, device):
        copies = []
        for k in range(1, size):
            peer = lax.rem(me + k, size)
            copy = remote(
                stat, held.at[which, me], send.at[which, k], recv.at[which, me], device(peer)
            )
            copy.start()
            copies.append(copy)
        held[which, me] = stat[...]
        for k in range(1, size):
            peer = lax.rem(me + k, size)
            remote(
                stat, held.at[which, peer], send.at[which, k], recv.at[which, peer], device(peer)
            ).wait_recv()
        for copy in copies:
            copy.wait_send()

    def everywhere(which, combine):
        exchange(which, group, g, stats_a, sa_send, sa_recv, lambda peer: (peer, z))
        combine(stats_a.at[which], group)
        exchange(which, planes, z, stats_b, sb_send, sb_recv, lambda peer: (g, peer))
        combine(stats_b.at[which], planes)

    def spread_out(held, size):
        number = sum(held[i, 0:1, :] for i in range(size))
        mean = sum(held[i, 0:1, :] * held[i, 1:2, :] for i in range(size))
        mean = mean / jnp.maximum(number, 1.0)
        square, plain, along = zero[0:1], zero[0:1], zero[0:1]
        for i in range(size):
            off = held[i, 1:2, :] - mean
            square = square + held[i, 2:3, :] + held[i, 0:1, :] * off * off
            plain = plain + held[i, 3:4, :]
            along = along + held[i, 4:5, :] + held[i, 3:4, :] * off
        stat[0:1, :] = number
        stat[1:2, :] = mean
        stat[2:3, :] = square
        stat[3:4, :] = plain
        stat[4:5, :] = along

    def plain_sum(held, size):
        stat[...] = sum(held[i] for i in range(size))

    everywhere(0, spread_out)
    number, mean = stat[0:1, :], stat[1:2, :]
    inv_std = lax.rsqrt(stat[2:3, :] / number + EPSILON)

    tile_rows = rows // BITS

    def give_norm(r, to):
        first = to * rows + r * tile_rows
        return remote(
            stage.at[pl.ds(pl.multiple_of(first, tile_rows), tile_rows)],
            out.at[at.slot, r * tile_rows : (r + 1) * tile_rows],
            n_send.at[to, r],
            n_recv.at[at.slot, r],
            (g, to),
        )

    def give_norms(first, last):
        @pl.when(at.works)
        def _():
            for p in range(first, min(last, BITS * (planes - 1))):
                r, k = p // (planes - 1), p % (planes - 1)
                give_norm(r, lax.rem(z + 1 + k, planes)).start()

    norm_own = pltpu.make_async_copy(stage.at[block], out.at[at.slot], own_sem.at[3])
    ig_own = pltpu.make_async_copy(ig.at[block], ig_out.at[at.slot], own_sem.at[4])
    bit_rows = rows // ROUNDS

    def give_bit(r, to):
        first = to * rows + r * bit_rows
        return remote(
            ig.at[pl.ds(pl.multiple_of(first, bit_rows), bit_rows)],
            ig_out.at[at.slot, r * bit_rows : (r + 1) * bit_rows],
            i_send.at[to, r],
            i_recv.at[at.slot, r],
            (g, to),
        )

    shift_grad = stat[3:4, :]
    gain_grad = stat[4:5, :] * inv_std
    sums_out[0:1, :] = gain_grad
    sums_out[1:2, :] = shift_grad
    scale = gain[...] * inv_std
    shift_mean = shift_grad / number
    gain_mean = gain_grad / number
    stat[...] = zero

    @pl.when(at.works)
    def _():
        def finish(r, t, total):
            cut_rows = tile_rows // tile
            j = lax.rem(z + 1 + t // cut_rows, planes)
            first = j * rows + r * tile_rows + lax.rem(t, cut_rows) * tile
            here = pl.ds(pl.multiple_of(first, tile), tile)
            live = live_of(first, tile)
            act = pre[here, :]
            grown = jnp.minimum(act, 0.0) + 1.0
            normed = (act - mean) * inv_std
            stage[here, :] = ((gain[...] * normed + shift[...]) * live).astype(BF16)
            grad = low[here, :].astype(F32) * live
            grad = scale * (grad - shift_mean - normed * gain_mean) * live * grown
            grad_low = grad.astype(BF16)
            low[here, :] = grad_low
            grad_low = grad_low.astype(F32)
            lane = lax.broadcasted_iota(jnp.int32, (tile, 128), 1)
            along_mix = grad_low * mix[here, :].astype(F32)
            along_diff = grad_low * diff[here, :].astype(F32)
            spread = jnp.zeros((tile, 128), F32)
            for h in range(heads):
                part = slice(h * head, (h + 1) * head)
                one = jnp.sum(along_mix[:, part], axis=1, keepdims=True)
                spread = jnp.where(lane % heads == h, one, spread)
                dcol[here, h : h + 1] = jnp.sum(along_diff[:, part], axis=1, keepdims=True)
            top = spread.astype(BF16)
            rest = spread - top.astype(F32)
            middle = rest.astype(BF16)
            bottom = (rest - middle.astype(F32)).astype(BF16)
            third = lane // heads
            parts[here, :] = jnp.where(
                third == 0, top, jnp.where(third == 1, middle, jnp.where(third == 2, bottom, 0.0))
            ).astype(BF16)
            return total + fold(grad)

        total = zero
        for r in range(BITS):
            total = lax.fori_loop(
                0, planes * tile_rows // tile, functools.partial(finish, r), total
            )
            for p in range(EARLY[r], EARLY[r + 1]):
                give_norm(p // (planes - 1), lax.rem(z + 1 + p % (planes - 1), planes)).start()
        norm_own.start()
        stat[0:1, :] = total_of(total)
        for h in range(depth):
            for copy in keep(h, block):
                copy.wait()

    chips = group // 2
    chip, core = g // 2, lax.rem(g, 2)
    partner = g + 1 - 2 * core
    swaps, plane_ins = (swap_0, swap_1, swap_2), (plane_0, plane_1, plane_2)
    line_ins, line_outs = (line_in_0, line_in_1, line_in_2), (line_out_0, line_out_1, line_out_2)
    spans = ((0, width), (0, width // 2), (width // 2, width))
    strip = width_in // chips

    def share(u, which):
        size = (spans[u][1] - spans[u][0]) // 2
        return pl.ds(pl.multiple_of(which * size, size), size)

    lines = planes.bit_length() - 1
    regions = [(0, strip, 0, 2)]
    sides = []
    for i in range(lines):
        top, high, left, across = regions[-1]
        bit = lax.rem(z // 2**i, 2)
        pair = []
        for b in (bit, 1 - bit):
            if high >= 32:
                pair.append((top + b * (high // 2), high // 2, left, across))
            else:
                pair.append((top, high, left + b * (across // 2), across // 2))
        regions.append(pair[0])
        sides.append((z + 2**i - 2 ** (i + 1) * bit, pair[0], pair[1]))

    def cut(u, region):
        top, high, left, across = region
        size = (spans[u][1] - spans[u][0]) // 4
        left, across = left * size, across * size
        return (
            pl.ds(top if isinstance(top, int) else pl.multiple_of(top, high), high),
            pl.ds(left if isinstance(left, int) else pl.multiple_of(left, across), across),
        )

    def unit_of(u):
        kept = mix if u else diff
        return kept.at[0:width_in, spans[u][0] : spans[u][1]]

    def strip_of(index):
        return pl.ds(pl.multiple_of(index * strip, strip), strip)

    def to_core(u):
        return remote(
            unit_of(u).at[:, share(u, 1 - core)], swaps[u], r_send.at[u, 0, 0], r_recv.at[u, 0, 0], (partner, z)
        )

    def to_chip(u, peer, landed):
        return remote(
            unit_of(u).at[strip_of(peer), share(u, core)],
            plane_ins[u].at[landed],
            r_send.at[u, 1, peer],
            r_recv.at[u, 1, landed],
            (2 * peer + core, z),
        )

    def landed_at(u, i):
        _, high, _, across = sides[i][1]
        return line_ins[u].at[i, 0:high, 0 : across * (spans[u][1] - spans[u][0]) // 4]

    def to_line(u, i):
        peer, kept, given = sides[i]
        return remote(
            line_outs[u].at[cut(u, given)], landed_at(u, i), r_send.at[u, 2, i], r_recv.at[u, 2, i], (g, peer)
        )

    def from_line(u, i, landed=False):
        peer, kept, given = sides[i]
        where = swaps[u].at[strip_of(chip)].at[cut(u, given if landed else kept)]
        return remote(where, where, r_send.at[u, 3, i], r_recv.at[u, 3, i], (g, peer))

    def from_chip(u, peer, landed):
        where = swaps[u].at[strip_of(landed)]
        return remote(
            where, where, r_send.at[u, 4, peer], r_recv.at[u, 4, landed], (2 * peer + core, z)
        )

    def from_core(u, which):
        return remote(
            swaps[u],
            unit_of(u).at[:, share(u, which)],
            r_send.at[u, 5, 0],
            r_recv.at[u, 5, 0],
            (partner, z),
        )

    def others(size, me):
        return [lax.rem(me + k, size) for k in range(1, size)]

    last_step = 4 + 2 * lines

    def step(u, number):
        unit, own = unit_of(u), share(u, core)
        if number == 0:
            to_core(u).start()
        elif number == 1:
            to_core(u).wait()

            @pl.loop(0, width_in // tall)
            def _(t):
                here = sub_rows(t, tall)
                value = unit[here, own].astype(F32) + swaps[u][here, :].astype(F32)
                unit[here, own] = value.astype(BF16)

            for peer in others(chips, chip):
                to_chip(u, peer, chip).start()
        elif number <= 2 + lines:
            i = number - 3
            if i < 0:
                for peer in others(chips, chip):
                    to_chip(u, peer, peer).wait_recv()
                value = unit[strip_of(chip), own].astype(F32)
                for peer in others(chips, chip):
                    value = value + plane_ins[u][peer].astype(F32)
                line_outs[u][...] = value.astype(BF16)
            else:
                kept = sides[i][1]
                to_line(u, i).wait_recv()
                value = line_outs[u][cut(u, kept)].astype(F32)
                value = value + landed_at(u, i)[...].astype(F32)
                target = line_outs[u] if i + 1 < lines else swaps[u].at[strip_of(chip)]
                target[cut(u, kept)] = value.astype(BF16)
            if i + 1 < lines:
                to_line(u, i + 1).start()
            else:
                from_line(u, lines - 1).start()
            if i < 0:
                for peer in others(chips, chip):
                    to_chip(u, peer, chip).wait_send()
            else:
                to_line(u, i).wait_send()
        elif number <= 2 + 2 * lines:
            i = 2 + 2 * lines - number
            from_line(u, i, True).wait_recv()
            if i > 0:
                from_line(u, i - 1).start()
            else:
                for peer in others(chips, chip):
                    from_chip(u, peer, chip).start()
            from_line(u, i).wait_send()
        elif number < last_step:
            for peer in others(chips, chip):
                from_chip(u, peer, peer).wait_recv()
            from_core(u, core).start()

            @pl.loop(0, width_in // tall)
            def _(t):
                here = sub_rows(t, tall)
                unit[here, own] = swaps[u][here, :]

            for peer in others(chips, chip):
                from_chip(u, peer, chip).wait_send()
        else:
            from_core(u, 1 - core).wait_recv()
            from_core(u, core).wait_send()
            answer(u).start()

    def steps(*work):
        for u, number in work:
            step(u, number)

    def answer(u):
        target = proj_out if u else skip_out
        return pltpu.make_async_copy(unit_of(u), target.at[:, slice(*spans[u])], out_sem.at[u])

    def fetch(j, h):
        if resident:
            return []
        place = pl.ds(pl.multiple_of(j * rows, rows), rows)
        slot = h % 2
        return [
            pltpu.make_async_copy(p_all.at[h, :, place], p_back.at[slot], p_sem.at[2, slot]),
            pltpu.make_async_copy(q_all.at[h, :, place], q_back.at[slot], p_sem.at[3, slot]),
        ]

    def product(u, right):
        unit = unit_of(u)
        columns = slice(*spans[u])

        @pl.when(at.works)
        def _():
            @pl.loop(0, width_in // head)
            def _(f):
                place = sub_rows(f, head)
                unit[place, :] = dot(feat_all[:, place], right[:, columns], (0, 0)).astype(BF16)

        @pl.when(jnp.logical_not(at.works))
        def _():
            unit[...] = jnp.zeros_like(unit)

    @pl.when(at.works)
    def _():
        for copy in fetch(lax.rem(z + 1, planes), 0):
            copy.start()

    product(0, low)
    step(0, 0)

    def source_block(k, turn):
        j = lax.rem(z + 1 + k, planes)
        here = sub_rows(j, rows)
        per_turn = heads // 2
        for h in range(turn * per_turn, (turn + 1) * per_turn):
            part = slice(h * head, (h + 1) * head)
            slot = h % 2
            if h + 1 < (turn + 1) * per_turn:
                for copy in fetch(j, h + 1):
                    copy.start()
            else:

                @pl.when(k + 1 < planes)
                def _():
                    for copy in fetch(lax.rem(j + 1, planes), turn * per_turn):
                        copy.start()

                if turn == 0:

                    @pl.when(k + 1 == planes)
                    def _():
                        for copy in fetch(lax.rem(z + 1, planes), per_turn):
                            copy.start()

            for copy in fetch(j, h):
                copy.wait()
            if resident:
                p_now, q_now = p_slot[h, :, sub_rows(j, rows)], q_slot[h, :, sub_rows(j, rows)]
            else:
                p_now, q_now = p_back[slot], q_back[slot]
            grad = dot(p_now, low[:, part], (0, 0))
            along = dot(q_now, low[:, part], (0, 0))
            spread = dot(q_now, parts[...], (0, 0))
            lane = lax.broadcasted_iota(jnp.int32, spread.shape, 1)
            chosen = (lane % heads == h) & (lane < 3 * heads)
            own = hid[here, part].astype(F32)
            by_src = jnp.sum(own * along, axis=1, keepdims=True) - jnp.sum(
                jnp.where(chosen, spread, 0.0), axis=1, keepdims=True
            )
            by_dst = dcol[here, h : h + 1]
            att_src, att_dst = (
                att_rows[i : i + 1, part].astype(F32) for i in (h, heads + h)
            )
            grad = grad + by_dst * att_dst + by_src * att_src
            back[here, part] = grad.astype(BF16)
            stat[1:2, part] += total_of(by_dst * own)
            stat[2:3, part] += total_of(by_src * own)

    def sent_norm(j):
        @pl.when(j != z)
        def _():
            for r in range(BITS):
                give_norm(r, j).wait_send()

        pl.when(j == z)(norm_own.wait)

    def input_block(k):
        j = lax.rem(z + 1 + k, planes)
        here = sub_rows(j, rows)
        if shared:
            sent_norm(j)
        for f in range(width_in // head):
            part = slice(f * head, (f + 1) * head)
            ig[here, part] = (
                dot(back[here, :], wp[part, :], (1, 1)) + dot(low[here, :], ws[part, :], (1, 1))
            ).astype(BF16)
        pl.when(j == z)(ig_own.start)

    def give_bits(first, last):
        @pl.when(at.works)
        def _():
            for p in range(first, min(last, ROUNDS * (planes - 1))):
                give_bit(p % ROUNDS, lax.rem(z + 1 + p // ROUNDS, planes)).start()

    def S(u, number):
        return lambda: step(u, number) if number <= last_step else None

    def N(first, last):
        return lambda: give_norms(first, last)

    def R(first, last):
        return lambda: give_bits(first, last)

    def do(*work):
        for one in work:
            one()

    def walk(turn, **work):
        @pl.loop(0, planes)
        def _(k):
            pl.when(at.works)(functools.partial(source_block, k, turn))
            for when, todo in work.items():
                pl.when(k == int(when[1:]))(functools.partial(do, *todo))

    def input_of(k):
        pl.when(at.works)(functools.partial(input_block, k))

    def I(k):
        return lambda: input_of(k)

    last = BITS * (planes - 1)
    do(N(7, 8))
    walk(0, k0=(S(0, 1),), k1=(N(8, 9),), k3=(N(9, 10),))
    product(1, back)
    do(S(1, 0), N(10, 11))
    walk(1, k0=(S(1, 1), N(11, last)), k1=(I(0),), k3=(S(0, 2), R(0, 0)))
    product(2, back)
    do(S(2, 0), R(0, 0), I(1), S(2, 1), S(0, 3), R(0, 3), I(2), S(1, 2), R(3, 6))
    for k in range(3, planes):
        input_of(k)
    exchange(1, group, g, stats_a, sa_send, sa_recv, lambda peer: (peer, z))
    plain_sum(stats_a.at[1], group)
    done, given = [3, 2, 1], 6
    for number in range(2, last_step + 1):
        for u, target in ((2, number), (1, number + 1), (0, number + 2)):
            while done[u] < min(target, last_step):
                done[u] += 1
                step(u, done[u])
        give_bits(given, given + PACE)
        given += PACE
    give_bits(given, ROUNDS * (planes - 1))
    exchange(1, planes, z, stats_b, sb_send, sb_recv, lambda peer: (g, peer))
    plain_sum(stats_b.at[1], planes)
    sums_out[2:5, :] = stat[0:3, :]
    sums_out[5:8, :] = jnp.zeros((3, width), F32)

    for s in range(slots):

        @pl.when(jnp.logical_not(at.mine[s]))
        def _():
            for r in range(BITS):
                landing = out.at[s, r * tile_rows : (r + 1) * tile_rows]
                remote(landing, landing, n_send.at[0, r], n_recv.at[s, r], (g, at.owner(s))).wait_recv()
            for r in range(ROUNDS):
                landing = ig_out.at[s, r * bit_rows : (r + 1) * bit_rows]
                remote(landing, landing, i_send.at[0, r], i_recv.at[s, r], (g, at.owner(s))).wait_recv()

    @pl.when(at.works)
    def _():
        ig_own.wait()
        for peer in others(planes, z):
            for r in range(ROUNDS):
                give_bit(r, peer).wait_send()
        if not shared:
            for k in range(planes):
                sent_norm(lax.rem(z + k, planes))

    for u in range(3):
        answer(u).wait()
    sent(f_moves)
    sent(a_moves)
    sent(c_moves)


def finish_kernel(
    near,
    out_in,
    ig_in,
    proj_in,
    skip_in,
    sums,
    out,
    ig,
    proj,
    skip,
    att_dst,
    att_src,
    bias,
    gain,
    shift,
    narrow,
    full,
    held,
    copy_sem,
    in_sem,
    wide_sem,
):
    heads, head = att_dst.shape
    passing = []
    for i, (source, target) in enumerate(((out_in, out), (ig_in, ig))):
        for s in range(out.shape[0]):
            load = None if near else pltpu.make_async_copy(source.at[s], held.at[i, s], copy_sem.at[i, s])
            kept = source.at[s] if near else held.at[i, s]
            store = pltpu.make_async_copy(kept, target.at[s], copy_sem.at[i, s])
            passing.append((load, store))
    size = proj.shape[0] // 4
    lots = []
    for i, (source, target) in enumerate(((proj_in, proj), (skip_in, skip))):
        for k in range(4):
            rows = pl.ds(k * size, size)
            load = None if near else pltpu.make_async_copy(source.at[rows], narrow.at[i, rows], in_sem.at[i, k])
            store = pltpu.make_async_copy(full.at[i, rows], target.at[rows], wide_sem.at[i, k])
            lots.append((source if near else narrow.at[i], i, rows, load, store))
    if near:
        for _, store in passing:
            store.start()
    else:
        for _, _, _, load, _ in lots:
            load.start()
        for load, _ in passing:
            load.start()
    for h in range(heads):
        part = slice(h * head, (h + 1) * head)
        att_dst[h : h + 1, :] = sums[3:4, part]
        att_src[h : h + 1, :] = sums[4:5, part]
    gain[...] = sums[0:1, :]
    shift[...] = sums[1:2, :]
    bias[...] = sums[2:3, :]
    for source, i, rows, load, store in lots:
        if not near:
            load.wait()
        full[i, rows, :] = source[rows, :].astype(F32)
        store.start()
    if not near:
        for load, store in passing:
            load.wait()
            store.start()
    for _, _, _, _, store in lots:
        store.wait()
    for _, store in passing:
        store.wait()


def shards(
    planes,
    group,
    features,
    adjacency,
    counts,
    proj_weight,
    skip_weight,
    attn_dst,
    attn_src,
    attn_bias,
    norm_gain,
    norm_shift,
    cotangent,
):
    slots, rows, width_in = features.shape
    nodes = adjacency.shape[2]
    heads, head = attn_dst.shape
    width = heads * head
    dims = (planes, group, slots, rows, nodes, heads, head, width_in)
    dma = pltpu.SemaphoreType.DMA
    chips = group // 2
    strip, shares = width_in // chips, (width // 2, width // 4, width // 4)
    lines = planes.bit_length() - 1
    tallest = max(nodes, width_in)
    resident = nodes <= 1024
    kept = (heads, nodes, nodes) if resident else (1, rows, nodes)

    shape = jax.ShapeDtypeStruct
    vmem = pltpu.VMEM
    near = pltpu.VMEM if resident else shape
    square = shape((heads, 16, 128) if resident else (heads, nodes, nodes), BF16)
    output, input_grad, proj_grad, skip_grad, sums, _, _ = pl.pallas_call(
        functools.partial(layer_kernel, dims),
        out_shape=[
            near((slots, rows, width), BF16),
            near((slots, rows, width_in), BF16),
            near((width_in, width), BF16),
            near((width_in, width), BF16),
            shape((8, width), F32),
            square,
            square,
        ],
        in_specs=[ANY, ANY, ANY, SMEM, ANY, ANY, VMEM, VMEM, VMEM, VMEM, VMEM],
        out_specs=[ANY, ANY, ANY, ANY, VMEM, ANY, ANY],
        scratch_shapes=[
            vmem((16, width), BF16),
            vmem((nodes, width_in), BF16),
            vmem((nodes, width), BF16),
            vmem((nodes, max(nodes, (3 if nodes <= 1024 else 2) * width)), BF16),
            vmem((slots, rows, nodes), BF16),
            vmem((2, max(rows // 4, TILE), nodes), jnp.int32),
            vmem((width_in, width), BF16),
            vmem((width_in, width), BF16),
            vmem((nodes, width), F32),
            vmem((tallest, width), BF16),
            vmem((tallest, width), BF16),
            vmem((nodes, width), BF16),
            vmem((nodes, 128), F32),
            vmem((nodes, 128), BF16),
            vmem((16, nodes), F32),
            vmem(kept, BF16),
            vmem(kept, BF16),
            vmem((rows, nodes), BF16),
            vmem((1 if resident else 2, 16 if resident else nodes, rows), BF16),
            vmem((1 if resident else 2, 16 if resident else nodes, rows), BF16),
            vmem((8, width), F32),
            vmem((2, group, 8, width), F32),
            vmem((2, planes, 8, width), F32),
            *(vmem((width_in, one), BF16) for one in shares),
            *(vmem((chips, strip, one), BF16) for one in shares),
            *(vmem((lines, max(strip // 2, 16), one), BF16) for one in shares),
            *(vmem((strip, one), BF16) for one in shares),
            dma((slots, LOTS)),
            dma((planes, LOTS)),
            dma((slots, LOTS)),
            dma((planes, LOTS)),
            dma((slots, LOTS)),
            dma((planes, LOTS)),
            dma((planes, BITS)),
            dma((slots, BITS)),
            dma((planes, ROUNDS)),
            dma((slots, ROUNDS)),
            dma((2, group)),
            dma((2, group)),
            dma((2, planes)),
            dma((2, planes)),
            dma((3, 6, max(chips, lines))),
            dma((3, 6, max(chips, lines))),
            dma((3, LOTS)),
            dma((5,)),
            dma((2,)),
            dma((2,)),
            dma((4, 2)),
            dma((3,)),
        ],
        compiler_params=pltpu.CompilerParams(
            collective_id=0,
            has_side_effects=True,
            vmem_limit_bytes=(54 if resident else 63) * 2**20,
        ),
    )(
        features,
        adjacency,
        cotangent,
        counts,
        proj_weight,
        skip_weight,
        attn_dst,
        attn_src,
        attn_bias.reshape(1, width),
        norm_gain.reshape(1, width),
        norm_shift.reshape(1, width),
    )
    line = shape((1, width), F32)
    weight, att = shape((width_in, width), F32), shape((heads, head), F32)
    output, input_grad, proj_grad, skip_grad, dst_grad, src_grad, bias, gain, shift = pl.pallas_call(
        functools.partial(finish_kernel, resident),
        out_shape=[
            shape(output.shape, BF16),
            shape(input_grad.shape, BF16),
            weight,
            weight,
            att,
            att,
            line,
            line,
            line,
        ],
        in_specs=[VMEM if resident else ANY] * 4 + [VMEM],
        out_specs=[ANY] * 4 + [VMEM] * 5,
        scratch_shapes=[
            vmem((1, 16, 128) if resident else (2, width_in, width), BF16),
            vmem((2, width_in, width), F32),
            vmem((2, slots, 16, 128) if resident else (2,) + output.shape, BF16),
            dma((2, slots)),
            dma((2, 4)),
            dma((2, 4)),
        ],
        compiler_params=pltpu.CompilerParams(vmem_limit_bytes=(40 if resident else 60) * 2**20),
    )(output, input_grad, proj_grad, skip_grad, sums)
    flat = (width,)
    return (
        output,
        input_grad,
        proj_grad,
        skip_grad,
        dst_grad,
        src_grad,
        bias.reshape(flat),
        gain.reshape(flat),
        shift.reshape(flat),
    )


def solution(mesh):
    placed = (
        P("graph", "row", None),
        P("graph", "row", None),
        P("graph"),
        P(),
        P(),
        P(),
        P(),
        P(),
        P(),
        P(),
        P("graph", "row", None),
    )
    return jax.shard_map(
        functools.partial(shards, mesh.shape["row"], mesh.shape["graph"]),
        mesh=mesh,
        in_specs=placed,
        out_specs=(
            P("graph", "row", None),
            P("graph", "row", None),
            P(),
            P(),
            P(),
            P(),
            P(),
            P(),
            P(),
        ),
        check_vma=False,
    )
```
